32 devices in a mesh: seq: 4 (over x, core), tensor: 4 (over z), dp: 2 (over y).
Axes of the slice: x: 2, y: 2, z: 4, core: 2. Of those that a mesh axis runs over, the one named last changes fastest.
Arguments:
- states: bfloat16 [8, 2048, 2048], P('dp', 'seq'), may hold values from -6 to 6
- ln1_gain: bfloat16 [2048], P('dp'), may hold values from 0.099609375 to 1.8984375
- ln1_bias: bfloat16 [2048], P('dp'), may hold values from -4 to 4
- ln2_gain: bfloat16 [2048], P('dp'), may hold values from 0.099609375 to 1.8984375
- ln2_bias: bfloat16 [2048], P('dp'), may hold values from -4 to 4
- qkv_weight: bfloat16 [2048, 6144], P('dp', 'tensor'), may hold values from -0.125 to 0.125
- qkv_bias: bfloat16 [6144], P(('tensor', 'dp')), may hold values from -4 to 4
- dense_weight: bfloat16 [2048, 2048], P('tensor', 'dp'), may hold values from -1 to 1
- dense_bias: bfloat16 [2048], P('dp'), may hold values from -4 to 4
- up_weight: bfloat16 [2048, 8192], P('dp', 'tensor'), may hold values from -0.125 to 0.125
- up_bias: bfloat16 [8192], P(('tensor', 'dp')), may hold values from -4 to 4
- down_weight: bfloat16 [8192, 2048], P('tensor', 'dp'), may hold values from -0.09375 to 0.09375
- out_bias: bfloat16 [2048], P('dp'), may hold values from -4 to 4
- out_grad: bfloat16 [8, 2048, 2048], P('dp', 'seq'), may hold values from -6 to 6
Outputs:
- output: bfloat16 [8, 2048, 2048], P('dp', 'seq', 'tensor')
- input_grad: float32 [8, 2048, 2048], P('dp', 'seq', 'tensor')
- ln1_gain_grad: float32 [2048], P(('tensor', 'dp'))
- ln1_bias_grad: float32 [2048], P(('tensor', 'dp'))
- ln2_gain_grad: float32 [2048], P(('tensor', 'dp'))
- ln2_bias_grad: float32 [2048], P(('tensor', 'dp'))
- qkv_weight_grad: float32 [2048, 6144], P('dp', 'tensor')
- qkv_bias_grad: float32 [6144], P(('tensor', 'dp'))
- dense_weight_grad: float32 [2048, 2048], P('tensor', 'dp')
- dense_bias_grad: float32 [2048], P('dp')
- up_weight_grad: float32 [2048, 8192], P('dp', 'tensor')
- up_bias_grad: float32 [8192], P(('tensor', 'dp'))
- down_weight_grad: float32 [8192, 2048], P('tensor', 'dp')
- out_bias_grad: float32 [2048], P('dp')
The draws below stay inside these ranges and needn't reach their ends.
All inputs are finite; a program needn't handle non-finite values.
Results may differ from the reference program's by a relative error of at most 0.019.
Values may be sent and summed in bfloat16 or wider, within the bound.
A program may use at most 320 MiB of HBM per device.

```python
import jax
import jax.numpy as jnp
from jax import lax

D = 2048
HEADS = 16
HD = 128
ROT = 32
FF = 8192
SEQS = 8
LEN = 2048


def block_scale(key, shape, cuts, least, largest):
    gain = 1.0
    for dim, parts in cuts:
        draws = jax.random.uniform(jax.random.fold_in(jax.random.fold_in(key, 6), dim), (parts,), jnp.float32, least / len(cuts), largest / len(cuts))
        gain = gain * jnp.repeat(jnp.exp(draws), shape[dim] // parts).reshape((-1,) + (1,) * (len(shape) - 1 - dim))
    return gain


def normal_values(key, shape, spread, reach, split=(), held_as=jnp.bfloat16):
    values = jax.random.normal(key, shape, jnp.float32) * spread
    if len(split) > 0:
        values = block_scale(key, shape, split, -0.22, 0.18) * values
    return jnp.clip(values, min=-reach, max=reach).astype(held_as)


def setup_inputs(seed: int = 0) -> dict:
    keys = jax.random.split(jax.random.key(seed), 15)
    states = normal_values(keys[0], (SEQS, LEN, D), 1.0, 6.0, ((0, 2), (1, 4)))
    ln1_gain = jnp.clip(1.0 + 0.18 * jax.random.normal(keys[1], (D,), jnp.float32), 0.099609375, 1.8984375).astype(jnp.bfloat16)
    ln1_bias = normal_values(keys[2], (D,), 0.3, 4.0, ((0, 2),))
    ln2_gain = jnp.clip(1.0 + 0.18 * jax.random.normal(keys[3], (D,), jnp.float32), 0.099609375, 1.8984375).astype(jnp.bfloat16)
    ln2_bias = normal_values(keys[4], (D,), 0.3, 4.0, ((0, 2),))
    qkv_weight = normal_values(keys[5], (D, 3 * D), D ** -0.5, 0.125, ((0, 2), (1, 4)))
    qkv_bias = normal_values(keys[6], (3 * D,), 0.3, 4.0, ((0, 8),))
    dense_weight = normal_values(keys[7], (D, D), (D // 64) ** -0.5, 1.0, ((0, 4), (1, 2)))
    dense_bias = normal_values(keys[8], (D,), 0.5, 4.0, ((0, 2),))
    up_weight = normal_values(keys[9], (D, FF), D ** -0.5, 0.125, ((0, 2), (1, 4)))
    up_bias = normal_values(keys[10], (FF,), 0.3, 4.0, ((0, 8),))
    down_weight = normal_values(keys[11], (FF, D), (FF // 2) ** -0.5, 0.09375, ((0, 4), (1, 2)))
    out_bias = normal_values(keys[12], (D,), 0.5, 4.0, ((0, 2),))
    out_grad = normal_values(keys[13], (SEQS, LEN, D), 1.0, 6.0, ((0, 2), (1, 4)))
    return dict(states=states, ln1_gain=ln1_gain, ln1_bias=ln1_bias, ln2_gain=ln2_gain, ln2_bias=ln2_bias, qkv_weight=qkv_weight, qkv_bias=qkv_bias, dense_weight=dense_weight, dense_bias=dense_bias, up_weight=up_weight, up_bias=up_bias, down_weight=down_weight, out_bias=out_bias, out_grad=out_grad)


@jax.custom_vjp
def low(v):
    return lax.optimization_barrier(v.astype(jnp.bfloat16)).astype(jnp.float32)

@jax.custom_vjp
def low_back(v):
    return v

def low_keep(v):
    return (low(v), None)

def low_pass(kept, grad):
    return (grad,)

def back_keep(v):
    return (v, None)

def back_low(kept, grad):
    return (low(grad),)
low.defvjp(low_keep, low_pass)
low_back.defvjp(back_keep, back_low)

def norm_apply(values, scale_in, shift_in):
    center = values - lax.optimization_barrier(jnp.mean(values, -1, keepdims=True))
    return center * lax.rsqrt(lax.optimization_barrier(jnp.mean(center * center, -1, keepdims=True)) + 1e-05) * scale_in + shift_in

def matmul(left_side, right_side):
    return jnp.dot(left_side, right_side, precision=lax.Precision.HIGHEST)

def turn_tables(length):
    half_rot = ROT // 2
    frequency = 10000.0 ** (-jnp.arange(half_rot, dtype=jnp.float32) * 2.0 / ROT)
    places = jnp.arange(length).astype(jnp.float32)
    angles = places[:, None] * frequency[None, :]
    angles = jnp.concatenate([angles, angles], -1)
    return (jnp.cos(angles), jnp.sin(angles))

def rotate(values, cosine, sine_table):
    half_rot = ROT // 2
    rotated_part = values[..., :ROT]
    turned = jnp.concatenate([-rotated_part[..., half_rot:], rotated_part[..., :half_rot]], -1)
    return jnp.concatenate([rotated_part * cosine + turned * sine_table, values[..., ROT:]], -1)

def sequence_forward(inputs, params):
    gain_one, shift_one, gain_two, shift_two, qkv_full, qkv_shift, dense_full, dense_shift, up_full, up_shift, down_full, out_shift = params
    length = inputs.shape[0]
    cosine, sine_table = turn_tables(length)
    causal = jnp.arange(length)[:, None] >= jnp.arange(length)[None, :]
    normed_one = low(norm_apply(inputs, gain_one, shift_one))
    projected = low_back(matmul(normed_one, qkv_full) + qkv_shift)
    per_head = projected.reshape(length, HEADS, 3, HD).transpose(1, 2, 0, 3)

    def head_attend(head_block):
        queries = low(rotate(head_block[0], cosine, sine_table))
        keys_all = low(rotate(head_block[1], cosine, sine_table))
        values_all = low(head_block[2])
        scores = matmul(queries, keys_all.T) * HD ** (-0.5)
        scores = low_back(jnp.where(causal, scores, -1e+30))
        weights = jax.nn.softmax(scores, -1)
        return matmul(low(weights), values_all)
    attended = lax.map(jax.checkpoint(head_attend), per_head)
    attended = low(low_back(attended.transpose(1, 0, 2).reshape(length, HEADS * HD)))
    normed_two = low(norm_apply(inputs, gain_two, shift_two))
    pre_act = low_back(matmul(normed_two, up_full) + up_shift)
    activated = low(jax.nn.gelu(pre_act, approximate=False))
    return inputs + (matmul(attended, dense_full) + dense_shift) + (matmul(activated, down_full) + out_shift)

def reference(states, ln1_gain, ln1_bias, ln2_gain, ln2_bias, qkv_weight, qkv_bias, dense_weight, dense_bias, up_weight, up_bias, down_weight, out_bias, out_grad):
    params = tuple((member.astype(jnp.float32) for member in (ln1_gain, ln1_bias, ln2_gain, ln2_bias, qkv_weight, qkv_bias, dense_weight, dense_bias, up_weight, up_bias, down_weight, out_bias)))

    def one_sequence(totals, couple):
        inputs, cotangent = couple
        result, pullback = jax.vjp(sequence_forward, inputs.astype(jnp.float32), params)
        input_grad, param_grads = pullback(cotangent.astype(jnp.float32))
        totals = jax.tree.map(jnp.add, totals, param_grads)
        return (totals, (result.astype(jnp.bfloat16), input_grad))
    initial = tuple((jnp.zeros_like(member) for member in params))
    totals, (output, input_grad) = lax.scan(one_sequence, initial, (states, out_grad))
    return (output, input_grad, totals[0], totals[1], totals[2], totals[3], totals[4], totals[5], totals[6], totals[7], totals[8], totals[9], totals[10], totals[11])
```

```python
import functools
import math

import jax
import jax.numpy as jnp
from jax import lax
from jax.experimental import pallas as pl
from jax.experimental.pallas import tpu as pltpu
from jax.sharding import PartitionSpec as P

HD = 128
ROT = 32
EPS = 1e-05
F32 = jnp.float32
BF16 = jnp.bfloat16
NT = (((1,), (1,)), ((), ()))
NN = (((1,), (0,)), ((), ()))
TN = (((0,), (0,)), ((), ()))


def mm(a, b, dims=NN):
    return lax.dot_general(a, b, dims, preferred_element_type=F32)


def swap(block, axis, distance):
    return lax.ppermute(block, axis, [(i, i ^ distance) for i in range(lax.axis_size(axis))])


def ordered(mine, other, second):
    return jnp.where(
        second, jnp.concatenate([other, mine], 0), jnp.concatenate([mine, other], 0)
    )


def halves(array, index, axis):
    size = array.shape[axis] // 2
    return tuple(
        lax.dynamic_slice_in_dim(array, place * size, size, axis) for place in (index, 1 - index)
    )


def gather_other(shard, core):
    size = shard.shape[0] // 2
    got = swap(lax.dynamic_slice_in_dim(shard, core * size, size, 0), "dp", 1)
    return ordered(got, swap(got, "seq", 1), core == 1)


def reduce_grad(lhs_own, rhs_own, lhs_oth, rhs_oth, core):
    own_keep, own_send = halves(lhs_own, core, 1)
    oth_keep, oth_send = halves(lhs_oth, core, 1)
    sent = swap(
        (mm(own_send, rhs_own, TN).astype(BF16), mm(oth_send, rhs_oth, TN).astype(BF16)), "seq", 1
    )
    oth = (mm(oth_keep, rhs_oth, TN) + sent[1].astype(F32)).astype(BF16)
    got = swap(oth, "dp", 1)
    own = (mm(own_keep, rhs_own, TN) + sent[0].astype(F32) + got.astype(F32)).astype(BF16)
    step = 2
    while step < lax.axis_size("seq"):
        own = (own.astype(F32) + swap(own, "seq", step).astype(F32)).astype(BF16)
        step *= 2
    return ordered(own, swap(own, "seq", 1), core == 1).astype(F32)


def turn_tables(first_place, length):
    half_rot = ROT // 2
    frequency = 10000.0 ** (-jnp.arange(half_rot, dtype=F32) * 2.0 / ROT)
    places = (first_place + jnp.arange(length)).astype(F32)
    angles = places[:, None] * frequency[None, :]
    return jnp.cos(angles), jnp.sin(angles)


def rotate(values, cosine, sine):
    half_rot = ROT // 2
    low = values[..., :half_rot]
    high = values[..., half_rot:ROT]
    return jnp.concatenate(
        [low * cosine - high * sine, high * cosine + low * sine, values[..., ROT:]], -1
    )


def attention_kernel(
    parts, rows, block, scale, cos_ref, sin_ref, *refs
):
    ins = refs[:parts]
    outs = refs[parts : 2 * parts]
    q_s, k_s, v_s, g_s, kt_s, vt_s, prob_s, dk_s, dv_s, o_s, dq_s = refs[2 * parts :]
    index = lax.axis_index("seq")
    length = parts * rows
    for k in range(parts):
        at = pl.ds(pl.multiple_of((index ^ k) * rows, rows), rows)
        q_s[at, :] = ins[k][0, :, 0:HD]
        k_s[at, :] = ins[k][0, :, HD : 2 * HD]
        v_s[at, :] = ins[k][0, :, 2 * HD : 3 * HD]
        g_s[at, :] = ins[k][0, :, 3 * HD : 4 * HD]
    for j in range(length // block):
        at = slice(j * block, (j + 1) * block)
        kt_s[:, at] = k_s[at, :].T
        vt_s[:, at] = v_s[at, :].T
    dk_s[...] = jnp.zeros_like(dk_s)
    dv_s[...] = jnp.zeros_like(dv_s)
    factor = scale * math.log2(math.e)
    for i in range(length // block):
        qat = slice(i * block, (i + 1) * block)
        q = q_s[qat, :]
        g = g_s[qat, :]
        gt = g.T.astype(F32)

        def keys(j):
            return pl.ds(pl.multiple_of(j * block, block), block)

        def score(j, top, masked):
            s = mm(k_s[keys(j), :], q, NT)
            if masked:
                key = lax.broadcasted_iota(jnp.int32, s.shape, 0)
                query = lax.broadcasted_iota(jnp.int32, s.shape, 1)
                s = jnp.where(key <= query, s, -1e30)
            prob_s[keys(j), :] = s
            return jnp.maximum(top, jnp.max(s.reshape(block // 8, 8, block), 0))

        top = jnp.full((8, block), -1e30, F32)
        top = lax.fori_loop(0, i, lambda j, t: score(j, t, False), top)
        top = jnp.max(score(i, top, True), 0, keepdims=True)

        def weigh(j, carry):
            total, acc = carry
            e = jnp.exp2((prob_s[keys(j), :] - top) * factor)
            prob_s[keys(j), :] = e
            total = total + jnp.sum(e.reshape(block // 8, 8, block), 0)
            return total, acc + mm(vt_s[:, keys(j)], e.astype(BF16))

        total, acc = lax.fori_loop(
            0, i + 1, weigh, (jnp.zeros((8, block), F32), jnp.zeros((HD, block), F32))
        )
        inverse = 1.0 / jnp.sum(total, 0, keepdims=True)
        acc = acc * inverse
        delta = jnp.sum(acc * gt, 0, keepdims=True)
        o_s[qat, :] = acc.T.astype(BF16)

        def back(j, dqt):
            p = prob_s[keys(j), :] * inverse
            ds = (p * (mm(v_s[keys(j), :], g, NT) - delta)).astype(BF16)
            dv_s[keys(j), :] += mm(p.astype(BF16), g)
            dk_s[keys(j), :] += mm(ds, q)
            return dqt + mm(kt_s[:, keys(j)], ds)

        dqt = lax.fori_loop(0, i + 1, back, jnp.zeros((HD, block), F32))
        dq_s[qat, :] = dqt.T
    half_rot = ROT // 2
    lane = lax.broadcasted_iota(jnp.int32, (rows, HD), 1)
    for k in range(parts):
        at = pl.ds(pl.multiple_of((index ^ k) * rows, rows), rows)
        cosine = cos_ref[at, :]
        sine = sin_ref[at, :]

        def turn_back(w):
            turned = jnp.where(
                lane < half_rot, pltpu.roll(w, HD - half_rot, 1), pltpu.roll(w, half_rot, 1)
            )
            return (w * cosine + turned * sine) * scale

        outs[k][0, :, 0:HD] = o_s[at, :]
        outs[k][0, :, HD : 2 * HD] = turn_back(dq_s[at, :]).astype(BF16)
        outs[k][0, :, 2 * HD : 3 * HD] = turn_back(dk_s[at, :]).astype(BF16)
        outs[k][0, :, 3 * HD : 4 * HD] = dv_s[at, :].astype(BF16)


def attention(blocks):
    parts = len(blocks)
    _, rows, width = blocks[0].shape
    length = parts * rows
    block = min(256, rows)
    cosine, sine = turn_tables(0, length)
    rest = HD - ROT
    cos_full = jnp.concatenate([cosine, cosine, jnp.ones((length, rest), F32)], 1)
    sin_full = jnp.concatenate([sine, -sine, jnp.zeros((length, rest), F32)], 1)
    scale = HD ** (-0.5)
    pair = length * length * HD
    whole = pl.BlockSpec((1, rows, width), lambda: (0, 0, 0))
    table = pl.BlockSpec((length, HD), lambda: (0, 0))
    return pl.pallas_call(
        functools.partial(attention_kernel, parts, rows, block, scale),
        out_shape=[jax.ShapeDtypeStruct((1, rows, width), BF16)] * parts,
        in_specs=[table, table] + [whole] * parts,
        out_specs=[whole] * parts,
        scratch_shapes=[pltpu.VMEM((length, HD), BF16)] * 4
        + [pltpu.VMEM((HD, length), BF16)] * 2
        + [pltpu.VMEM((length, block), F32)]
        + [pltpu.VMEM((length, HD), F32)] * 2
        + [pltpu.VMEM((length, HD), BF16)]
        + [pltpu.VMEM((length, HD), F32)],
        compiler_params=pltpu.CompilerParams(vmem_limit_bytes=40 * 1024 * 1024),
        cost_estimate=pl.CostEstimate(
            flops=6 * pair, bytes_accessed=8 * length * width, transcendentals=length * length // 2
        ),
    )(cos_full, sin_full, *blocks)


def on_device(
    states,
    ln1_gain,
    ln1_bias,
    ln2_gain,
    ln2_bias,
    qkv_weight,
    qkv_bias,
    dense_weight,
    dense_bias,
    up_weight,
    up_bias,
    down_weight,
    out_bias,
    out_grad,
):
    micros, rows, features = states.shape
    heads = qkv_weight.shape[1] // (3 * HD)
    tokens = micros * rows
    n = lax.axis_size("seq")
    pairs = heads * micros // n
    s = lax.axis_index("seq")
    core = s % 2
    d = lax.axis_index("dp")
    t = lax.axis_index("tensor")
    columns = features // lax.axis_size("tensor")

    def own_first(array, axis):
        return halves(array, d, axis)

    def absolute(own, other, axis=0):
        return jnp.where(
            d == 1, jnp.concatenate([other, own], axis), jnp.concatenate([own, other], axis)
        )

    small = (ln1_gain, ln1_bias, ln2_gain, ln2_bias, dense_bias, out_bias, qkv_bias, up_bias)
    small_got = swap(jnp.concatenate(small, 0), "dp", 1)
    other = []
    place = 0
    for vector in small:
        other.append(small_got[place : place + vector.shape[0]].astype(F32))
        place += vector.shape[0]
    qkv_other = gather_other(qkv_weight, core)
    up_other = gather_other(up_weight, core)
    dense_other = gather_other(dense_weight, core)
    down_other = gather_other(down_weight, core)

    x = states.reshape(tokens, features)
    xf = x.astype(F32)
    mean = jnp.mean(xf, -1, keepdims=True)
    center = xf - mean
    inverse = lax.rsqrt(jnp.mean(center * center, -1, keepdims=True) + EPS)
    x_own, x_oth = own_first(x, 1)
    unit_own = (x_own.astype(F32) - mean) * inverse
    unit_oth = (x_oth.astype(F32) - mean) * inverse
    g1 = (ln1_gain.astype(F32), other[0])
    g2 = (ln2_gain.astype(F32), other[2])
    one_own = (unit_own * g1[0] + ln1_bias.astype(F32)).astype(BF16)
    one_oth = (unit_oth * g1[1] + other[1]).astype(BF16)
    two_own = (unit_own * g2[0] + ln2_bias.astype(F32)).astype(BF16)
    two_oth = (unit_oth * g2[1] + other[3]).astype(BF16)
    cot = out_grad.reshape(tokens, features)
    cot_own, cot_oth = own_first(cot, 1)

    projected = (
        mm(one_own, qkv_weight) + mm(one_oth, qkv_other) + absolute(qkv_bias.astype(F32), other[6])
    )
    projected = projected.reshape(micros, rows, heads, 3, HD)
    cosine, sine = turn_tables(s * rows, rows)
    cosine = cosine[:, None, :]
    sine = sine[:, None, :]
    queries = rotate(projected[:, :, :, 0], cosine, sine)
    keys = rotate(projected[:, :, :, 1], cosine, sine)
    attended_grad = mm(cot_own, dense_weight, NT) + mm(cot_oth, dense_other, NT)
    payload = jnp.concatenate(
        [queries, keys, projected[:, :, :, 2], attended_grad.reshape(micros, rows, heads, HD)], -1
    ).astype(BF16)
    payload = payload.transpose(2, 0, 1, 3).reshape(n, pairs, 1, rows, 4 * HD)

    returned = []
    for pair in range(pairs):
        sent = [
            lax.dynamic_index_in_dim(payload[:, pair], s ^ k, 0, False) for k in range(n)
        ]
        blocks = [sent[0]] + [swap(sent[k], "seq", k) for k in range(1, n)]
        results = attention(blocks)
        back = jnp.stack([results[0]] + [swap(results[k], "seq", k) for k in range(1, n)])
        returned.append(
            jnp.concatenate(
                [lax.dynamic_slice_in_dim(back, s ^ j, 1, 0) for j in range(n)], 0
            )
        )
    returned = jnp.stack(returned, 1).reshape(heads, micros, rows, 4, HD)
    attended = returned[:, :, :, 0].transpose(1, 2, 0, 3).reshape(tokens, heads * HD)
    qkv_grad = (
        returned[:, :, :, 1:].transpose(1, 2, 0, 3, 4).reshape(tokens, heads * 3 * HD)
    )

    pre_act = mm(two_own, up_weight) + mm(two_oth, up_other) + absolute(
        up_bias.astype(F32), other[7]
    )
    tail = 0.5 * (1.0 + lax.erf(pre_act * math.sqrt(0.5)))
    activated = (pre_act * tail).astype(BF16)
    slope = (
        tail + pre_act * jnp.exp(-0.5 * pre_act * pre_act) * (1.0 / math.sqrt(2.0 * math.pi))
    ).astype(BF16)
    act_grad = mm(cot_own, down_weight, NT) + mm(cot_oth, down_other, NT)
    pre_grad = (act_grad * slope.astype(F32)).astype(BF16)

    down_grad = reduce_grad(activated, cot_own, activated, cot_oth, core)
    up_grad = reduce_grad(two_own, pre_grad, two_oth, pre_grad, core)
    dense_grad = reduce_grad(attended, cot_own, attended, cot_oth, core)
    qkv_w_grad = reduce_grad(one_own, qkv_grad, one_oth, qkv_grad, core)

    down_grad = down_grad
    partial = absolute(
        (mm(attended, dense_weight) + mm(activated, down_weight)).astype(BF16),
        (mm(attended, dense_other) + mm(activated, down_other)).astype(BF16),
        1,
    )
    branch = lax.psum_scatter(partial, "tensor", scatter_dimension=1, tiled=True).astype(F32)
    bias = absolute(
        dense_bias.astype(F32) + out_bias.astype(F32), other[4] + other[5]
    )
    first = t * columns
    output = (
        lax.dynamic_slice_in_dim(x, first, columns, 1).astype(F32)
        + branch
        + lax.dynamic_slice_in_dim(bias, first, columns, 0)
    ).astype(BF16)

    two_grad = (mm(pre_grad, up_weight, NT), mm(pre_grad, up_other, NT))
    one_grad = (mm(qkv_grad, qkv_weight, NT), mm(qkv_grad, qkv_other, NT))
    unit = (unit_own, unit_oth)

    def norm_back(grads, gains):
        scaled = [g * gain for g, gain in zip(grads, gains)]
        center = sum(jnp.sum(e, -1, keepdims=True) for e in scaled) / features
        along = sum(jnp.sum(e * u, -1, keepdims=True) for e, u in zip(scaled, unit)) / features
        return [inverse * (e - center - u * along) for e, u in zip(scaled, unit)]

    part_one = norm_back(one_grad, g1)
    part_two = norm_back(two_grad, g2)
    input_part = absolute(
        (part_one[0] + part_two[0]).astype(BF16), (part_one[1] + part_two[1]).astype(BF16), 1
    )
    input_cols = lax.psum_scatter(input_part, "tensor", scatter_dimension=1, tiled=True)
    input_grad = lax.dynamic_slice_in_dim(cot, first, columns, 1).astype(F32) + input_cols.astype(
        F32
    )

    norm_terms = absolute(
        *[
            jnp.stack(
                [
                    jnp.sum(one_grad[i] * unit[i], 0),
                    jnp.sum(one_grad[i], 0),
                    jnp.sum(two_grad[i] * unit[i], 0),
                    jnp.sum(two_grad[i], 0),
                ],
                1,
            )
            for i in range(2)
        ]
    )
    norm_terms = lax.psum(norm_terms, ("seq", "dp", "tensor"))
    vectors = lax.psum(
        jnp.concatenate(
            [
                jnp.sum(qkv_grad.astype(F32), 0),
                jnp.sum(pre_grad.astype(F32), 0),
                jnp.sum(cot.astype(F32), 0),
            ]
        ),
        ("seq", "dp"),
    )
    norm_count = columns // 2
    norm_mine = lax.dynamic_slice_in_dim(norm_terms, first + d * norm_count, norm_count, 0)
    vector_grads = []
    place = 0
    for size in (qkv_grad.shape[1], pre_grad.shape[1], features):
        vector_grads.append(
            lax.dynamic_slice_in_dim(vectors, place + d * (size // 2), size // 2, 0)
        )
        place += size

    def side_by_side(grad):
        return grad

    shape = (micros, rows, columns)
    return (
        output.reshape(shape),
        input_grad.reshape(shape),
        norm_mine[:, 0],
        norm_mine[:, 1],
        norm_mine[:, 2],
        norm_mine[:, 3],
        qkv_w_grad,
        vector_grads[0],
        side_by_side(dense_grad),
        vector_grads[2],
        up_grad,
        vector_grads[1],
        side_by_side(down_grad),
        vector_grads[2],
    )


def solution(mesh):
    placed = (
        P("dp", "seq", None),
        P("dp"),
        P("dp"),
        P("dp"),
        P("dp"),
        P("dp", "tensor"),
        P(("tensor", "dp")),
        P("tensor", "dp"),
        P("dp"),
        P("dp", "tensor"),
        P(("tensor", "dp")),
        P("tensor", "dp"),
        P("dp"),
        P("dp", "seq", None),
    )
    return jax.shard_map(
        on_device,
        mesh=mesh,
        in_specs=placed,
        out_specs=(
            P("dp", "seq", "tensor"),
            P("dp", "seq", "tensor"),
            P(("tensor", "dp")),
            P(("tensor", "dp")),
            P(("tensor", "dp")),
            P(("tensor", "dp")),
            P("dp", "tensor"),
            P(("tensor", "dp")),
            P("tensor", "dp"),
            P("dp"),
            P("dp", "tensor"),
            P(("tensor", "dp")),
            P("tensor", "dp"),
            P("dp"),
        ),
        check_vma=False,
    )
```

```python
import functools
import math

import jax
import jax.numpy as jnp
import numpy as np
from jax import lax
from jax.experimental import pallas as pl
from jax.experimental.pallas import tpu as pltpu
from jax.sharding import PartitionSpec as P

HD = 128
ROT = 32
HALF_ROT = ROT // 2
EPS = 1e-05
F32 = jnp.float32
BF16 = jnp.bfloat16
NN = (((1,), (0,)), ((), ()))
NT = (((1,), (1,)), ((), ()))
TN = (((0,), (0,)), ((), ()))
WEIGHT = 0.1
GROUPS = (1, 3)
PIECES = {"down": 4, "up": 4, "qkv": 2, "dense": 1}
VMEM_LIMIT = 60 * 1024 * 1024
KEEP, SEND, KEEP_AT, SEND_AT, SEQ, TENSOR, ORDER = 4, 6, 8, 10, 12, 13, 14


def bit(value, b):
    return lax.rem(lax.div(value, jnp.int32(1 << b)), jnp.int32(2))


def xor(value, other):
    value, other = jnp.int32(value), jnp.int32(other)
    return sum((1 << b) * lax.rem(bit(value, b) + bit(other, b), jnp.int32(2)) for b in range(4))


class Places:
    def __init__(self, straight):
        self.straight = straight

    def __getitem__(self, key):
        s = lax.axis_index("seq")
        if key == SEQ:
            return s
        if key == TENSOR:
            return lax.axis_index("tensor")
        if key >= ORDER:
            return self.head(key - ORDER)
        core = lax.rem(s, jnp.int32(2))
        d = lax.axis_index("dp")
        places = (2 * d, 2 * d + 1, 2 * (1 - d) + core, 2 * (1 - d) + 1 - core)
        if key < KEEP:
            return places[key]
        if key < KEEP_AT:
            return (core, 2, 1 - core, 3)[key - KEEP]
        return (2 * d + core, places[2], 2 * d + 1 - core, places[3])[key - KEEP_AT]

    def head(self, slot):
        return xor(lax.axis_index("seq"), slot) if self.straight else slot

    def either(self, key, i):
        return (1 - i) * self[key] + i * self[key + 1]


class Ride:
    def __init__(self, source, axis, distance, first=0, rows=None, lead=None):
        self.source, self.axis, self.distance = source, axis, distance
        self.first, self.lead = first, lead
        self.rows = source.shape[-2] - first if rows is None else rows
        self.result = None

    @property
    def shape(self):
        return (self.rows, self.source.shape[-1])

    def target(self):
        return {self.axis: xor(lax.axis_index(self.axis), self.distance)}

    def copy(self, source, target, sent, got):
        at = pl.ds(self.first, self.rows)
        return pltpu.make_async_remote_copy(
            src_ref=source.at[at] if self.lead is None else source.at[self.lead, at],
            dst_ref=target,
            send_sem=sent,
            recv_sem=got,
            device_id=self.target(),
            device_id_type=pl.DeviceIdType.MESH,
        )


class Line:
    def __init__(self, first):
        self.last = [first]
        self.rides = []
        self.count = 0

    def ride(self, *args, **kwargs):
        self.rides.append(Ride(*args, **kwargs))
        return self.rides[-1]


def mm(a, b, dims=NN):
    return lax.dot_general(a, b, dims, preferred_element_type=F32)


def swap(block, axis, distance):
    return lax.ppermute(block, axis, [(i, i ^ distance) for i in range(lax.axis_size(axis))])


def spec(block, index):
    if block is None:
        return pl.BlockSpec(memory_space=pl.ANY)
    return pl.BlockSpec(block, index)


def call(line, kernel, w, grid, inputs, outputs, scratch=(), flops=0, nbytes=0, name=None, alias=None):
    before = list(line.last)
    rides, line.rides = line.rides, []
    skip = len(before) + len(rides)
    ends = len(inputs) + len(outputs)

    def at(index):
        return None if index is None else lambda *steps: index(*steps, w)

    def on_step(last, work):
        chosen = True
        for axis, size in enumerate(grid):
            if size > 1:
                step = pl.program_id(axis)
                chosen = jnp.logical_and(chosen, step == (size - 1 if last else 0))
        if chosen is True:
            work()
        else:
            pl.when(chosen)(work)

    def body(*refs):
        sources = refs[len(before) : skip]
        own = refs[skip : skip + ends]
        targets = refs[skip + ends : skip + ends + len(rides)]
        rest = refs[skip + ends + len(rides) :]
        if not rides:
            kernel(w, *own, *rest)
            return
        *rest, sent, got = rest
        copies = lambda: [
            ride.copy(source, target, sent.at[i], got.at[i])
            for i, (ride, source, target) in enumerate(zip(rides, sources, targets))
        ]

        def start():
            barrier = pltpu.get_barrier_semaphore()
            partners = {(ride.axis, ride.distance): ride for ride in rides}
            for ride in partners.values():
                pl.semaphore_signal(
                    barrier, inc=1, device_id=ride.target(), device_id_type=pl.DeviceIdType.MESH
                )
            pl.semaphore_wait(barrier, len(partners))
            for copy in copies():
                copy.start()

        def wait():
            for copy in copies():
                copy.wait()

        on_step(False, start)
        kernel(w, *own, *rest)
        on_step(True, wait)

    params = dict(
        vmem_limit_bytes=VMEM_LIMIT, dimension_semantics=("arbitrary",) * len(grid)
    )
    sems = []
    if rides:
        params.update(collective_id=line.count, has_side_effects=True)
        line.count += 1
        sems = [pltpu.SemaphoreType.DMA((len(rides),))] * 2
    anywhere = pl.BlockSpec(memory_space=pl.ANY)
    results = pl.pallas_call(
        body,
        grid=grid,
        in_specs=[anywhere] * skip + [spec(block, at(index)) for _, block, index in inputs],
        out_specs=[spec(block, at(index)) for _, _, block, index in outputs]
        + [anywhere] * len(rides),
        scratch_shapes=list(scratch) + sems,
        out_shape=[jax.ShapeDtypeStruct(shape, dtype) for shape, dtype, _, _ in outputs]
        + [jax.ShapeDtypeStruct(ride.shape, ride.source.dtype) for ride in rides],
        compiler_params=pltpu.CompilerParams(**params),
        cost_estimate=pl.CostEstimate(
            flops=int(flops * WEIGHT), bytes_accessed=int(nbytes * WEIGHT), transcendentals=0
        ),
        input_output_aliases={} if alias is None else {skip + alias: 0},
        name=name,
    )(*before, *[ride.source for ride in rides], *[array for array, _, _ in inputs])
    for ride, result in zip(rides, results[len(outputs) :]):
        ride.result = result
    results = results[: len(outputs)]
    line.last = [results[-1]]
    return results


def fixed(*index):
    return lambda *_: index


def groups(values):
    return jnp.sum(values.reshape(values.shape[0] // 8, 8, values.shape[1]), 0)


def columns_at(w, b, size):
    return pl.ds(pl.multiple_of(w[b] * size, size), size)


def norm_kernel(w, x, cot, vectors, one, two, total):
    quarter = x.shape[1] // 4

    @pl.when(pl.program_id(0) == 0)
    def _():
        total[...] = jnp.zeros_like(total)

    values = x[...].astype(F32)
    mean = jnp.mean(values, -1, keepdims=True)
    center = values - mean
    inverse = lax.rsqrt(jnp.mean(center * center, -1, keepdims=True) + EPS)
    for b in range(4):
        at = slice(b * quarter, (b + 1) * quarter)
        unit = (x[:, columns_at(w, b, quarter)].astype(F32) - mean) * inverse
        one[:, at] = (unit * vectors[0:1, at] + vectors[1:2, at]).astype(BF16)
        two[:, at] = (unit * vectors[2:3, at] + vectors[3:4, at]).astype(BF16)
    total[...] += groups(cot[...].astype(F32))


def norms(line, w, x, cot, vectors):
    tokens, features = x.shape
    size = min(256, tokens)
    row = (size, features)
    along = lambda i, w: (i, 0)
    return call(
        line,
        norm_kernel,
        w,
        (tokens // size,),
        [(x, row, along), (cot, row, along), (vectors, vectors.shape, fixed(0, 0))],
        [
            ((tokens, features), BF16, row, along),
            ((tokens, features), BF16, row, along),
            ((8, features), F32, (8, features), fixed(0, 0)),
        ],
        flops=30 * tokens * features,
        nbytes=8 * tokens * features,
        name="norms",
    )


def turned(values):
    lane = lax.broadcasted_iota(jnp.int32, values.shape, 1)
    return jnp.where(
        lane < HALF_ROT, pltpu.roll(values, HD - HALF_ROT, 1), pltpu.roll(values, HALF_ROT, 1)
    )


def turn_tables(length):
    frequency = 10000.0 ** (-np.arange(HALF_ROT) * 2.0 / ROT)
    angles = np.arange(length)[:, None] * frequency[None, :]
    cosine = np.ones((length, HD), np.float32)
    sine = np.zeros((length, HD), np.float32)
    cosine[:, :ROT] = np.tile(np.cos(angles), (1, 2))
    sine[:, :HALF_ROT] = np.sin(angles)
    sine[:, HALF_ROT:ROT] = -np.sin(angles)
    return jnp.asarray(cosine), jnp.asarray(sine)


def project_kernel(
    slots, w, one, q0, q1, q2, bias, cosine, sine, c0, c1, c2, c3, d0, d1, d2, *outs
):
    step = pl.program_id(0)
    quarter = c0.shape[1]
    u = (
        mm(one[:, : 2 * quarter], q0[...])
        + mm(one[:, 2 * quarter : 3 * quarter], q1[...])
        + mm(one[:, 3 * quarter :], q2[...])
        + bias[...]
    )
    g = (
        mm(c0[...], d0[:, :quarter], NT)
        + mm(c1[...], d0[:, quarter:], NT)
        + mm(c2[...], d1[...], NT)
        + mm(c3[...], d2[...], NT)
    )
    cos, sin = cosine[...], sine[...]
    rows = u.shape[0]
    at_rows = pl.ds(pl.multiple_of(pl.program_id(1) * rows, rows), rows)
    flip = lax.rem(w.head(2 * step), jnp.int32(2))
    blocks = []
    for head in range(2):
        at = head * 3 * HD
        query, key = u[:, at : at + HD], u[:, at + HD : at + 2 * HD]
        blocks.append(
            jnp.concatenate(
                [
                    (query * cos - turned(query) * sin).astype(BF16),
                    (key * cos - turned(key) * sin).astype(BF16),
                    u[:, at + 2 * HD : at + 3 * HD].astype(BF16),
                    g[:, head * HD : (head + 1) * HD].astype(BF16),
                ],
                1,
            )
        )
    for pair in range(slots // 2):
        for turn in range(2):

            @pl.when((step == pair) & (flip == turn))
            def _():
                outs[2 * pair + turn][at_rows, :] = blocks[0]
                outs[2 * pair + 1 - turn][at_rows, :] = blocks[1]


def projections(line, w, first, count, rows, one, qkv, bias, tables, cot, dense):
    features = one.shape[1]
    quarter = features // 4
    heads = dense[0][1] // HD
    wide = 6 * HD
    pair = lambda i, m, w: (0, lax.div(w.head(2 * i), jnp.int32(2)))
    own = lambda i, m, w: (w[SEQ], 0)
    inputs = [(one, (rows, features), lambda i, m, w: (m + first, 0))]
    inputs += [(array, (height, wide), pair) for array, height, _, _ in qkv]
    inputs += [(bias, (1, wide), pair)]
    inputs += [(table, (rows, HD), own) for table in tables]
    for b in range(4):
        inputs.append((cot, (rows, quarter), lambda i, m, w, b=b: (m + first, w[b])))
    for array, _, width, place in dense:
        inputs.append(
            (array, (2 * HD, width), lambda i, m, w, b=place: (lax.div(w.head(2 * i), jnp.int32(2)), b))
        )
    return call(
        line,
        functools.partial(project_kernel, heads),
        w,
        (heads // 2, count),
        inputs,
        [((count * rows, 4 * HD), BF16, (count * rows, 4 * HD), fixed(0, 0))] * heads,
        flops=2 * count * rows * features * heads * 4 * HD,
        nbytes=2 * features * (heads * 4 * HD + 2 * count * rows) + 8 * count * rows * heads * HD,
        name="projections",
    )


def attention_kernel(parts, scale, qsize, ksize, w, *refs):
    ins = refs[:parts]
    cos_ref, sin_ref = refs[parts : parts + 2]
    outs = refs[parts + 2 : 2 * parts + 2]
    q_s, k_s, v_s, g_s, kt_s, vt_s, prob_s, dk_s, dv_s, o_s, dq_s = refs[2 * parts + 2 :]
    rows = ins[0].shape[0]
    length = parts * rows
    places = []
    for k in range(parts):
        at = pl.ds(pl.multiple_of(xor(w[SEQ], k) * rows, rows), rows)
        places.append(at)
        q_s[at, :] = ins[k][:, 0:HD]
        k_s[at, :] = ins[k][:, HD : 2 * HD]
        v_s[at, :] = ins[k][:, 2 * HD : 3 * HD]
        g_s[at, :] = ins[k][:, 3 * HD : 4 * HD]
    for j in range(length // ksize):
        at = slice(j * ksize, (j + 1) * ksize)
        kt_s[:, at] = k_s[at, :].T
        vt_s[:, at] = v_s[at, :].T
    factor = scale * math.log2(math.e)
    for i in range(length // qsize):
        qat = slice(i * qsize, (i + 1) * qsize)
        q = q_s[qat, :]
        g = g_s[qat, :]
        chunks = []
        for first in range(0, (i + 1) * qsize, ksize):
            chunks.append((first, min(ksize, (i + 1) * qsize - first)))
        top = jnp.full((8, qsize), -1e30, F32)
        for first, size in chunks:
            s = mm(k_s[first : first + size, :], q, NT)
            if first + size > i * qsize:
                key = lax.broadcasted_iota(jnp.int32, s.shape, 0) + (first - i * qsize)
                query = lax.broadcasted_iota(jnp.int32, s.shape, 1)
                s = jnp.where(key <= query, s, -1e30)
            prob_s[first : first + size, :] = s
            top = jnp.maximum(top, jnp.max(s.reshape(size // 8, 8, qsize), 0))
        top = jnp.max(top, 0, keepdims=True)
        total = jnp.zeros((8, qsize), F32)
        acc = jnp.zeros((HD, qsize), F32)
        for first, size in chunks:
            e = jnp.exp2((prob_s[first : first + size, :] - top) * factor)
            prob_s[first : first + size, :] = e
            total = total + jnp.sum(e.reshape(size // 8, 8, qsize), 0)
            acc = acc + mm(vt_s[:, first : first + size], e.astype(BF16))
        inverse = 1.0 / jnp.sum(total, 0, keepdims=True)
        acc = acc * inverse
        delta = jnp.sum(acc * g.T.astype(F32), 0, keepdims=True)
        o_s[qat, :] = acc.T.astype(BF16)
        dqt = jnp.zeros((HD, qsize), F32)
        for first, size in chunks:
            at = slice(first, first + size)
            p = prob_s[at, :] * inverse
            ds = (p * (mm(v_s[at, :], g, NT) - delta)).astype(BF16)
            dv = mm(p.astype(BF16), g)
            dk = mm(ds, q)
            low = max(0, min(size, i * qsize - first))
            if low:
                old = slice(first, first + low)
                dv_s[old, :] += dv[:low]
                dk_s[old, :] += dk[:low]
            if low < size:
                new = slice(first + low, first + size)
                dv_s[new, :] = dv[low:]
                dk_s[new, :] = dk[low:]
            dqt = dqt + mm(kt_s[:, at], ds)
        dq_s[qat, :] = dqt.T
    for k in range(parts):
        at = places[k]
        cosine = cos_ref[at, :]
        sine = sin_ref[at, :]
        dq, dk = dq_s[at, :], dk_s[at, :]
        outs[k][:, 0:HD] = o_s[at, :]
        outs[k][:, HD : 2 * HD] = ((dq * cosine + turned(dq) * sine) * scale).astype(BF16)
        outs[k][:, 2 * HD : 3 * HD] = ((dk * cosine + turned(dk) * sine) * scale).astype(BF16)
        outs[k][:, 3 * HD : 4 * HD] = dv_s[at, :].astype(BF16)


def attention(line, w, rows, blocks, tables, qsize=512, ksize=512):
    parts = len(blocks)
    width = blocks[0][0].shape[1]
    count = 1
    length = parts * rows
    qsize, ksize = min(qsize, rows), min(ksize, rows)
    block = ((rows, width), lambda m, w: (m, 0))
    return call(
        line,
        functools.partial(attention_kernel, parts, HD ** (-0.5), qsize, ksize),
        w,
        (count,),
        [(array, (rows, width), fixed(place, 0)) for array, place in blocks] + [(table, (length, HD), fixed(0, 0)) for table in tables],
        [((count * rows, width), BF16, *block)] * parts,
        scratch=[pltpu.VMEM((length, HD), BF16)] * 4
        + [pltpu.VMEM((HD, length), BF16)] * 2
        + [pltpu.VMEM((length, qsize), F32)]
        + [pltpu.VMEM((length, HD), F32)] * 2
        + [pltpu.VMEM((length, HD), BF16)]
        + [pltpu.VMEM((length, HD), F32)],
        flops=14 * count * length * length * HD,
        nbytes=4 * count * length * width + 8 * length * HD,
        name="attention",
    )


def up_kernel(w, two, u0, u1, u2, bias, activated, slope):
    quarter = u1.shape[0]
    pre = (
        mm(two[:, : 2 * quarter], u0[...])
        + mm(two[:, 2 * quarter : 3 * quarter], u1[...])
        + mm(two[:, 3 * quarter :], u2[...])
        + bias[...]
    )
    tail = 0.5 + 0.5 * lax.erf(pre * math.sqrt(0.5))
    activated[...] = (pre * tail).astype(BF16)
    bell = jnp.exp2(pre * pre * (-0.5 * math.log2(math.e))) * (1.0 / math.sqrt(2.0 * math.pi))
    slope[...] = (tail + pre * bell).astype(BF16)


def feed_up(line, w, rows, two, up, bias):
    tokens, features = two.shape
    hidden = up[0][2]
    wide = min(1024, hidden)
    column = lambda j, m, w: (0, j)
    out = ((tokens, hidden), BF16, (rows, wide), lambda j, m, w: (m, j))
    return call(
        line,
        up_kernel,
        w,
        (hidden // wide, tokens // rows),
        [(two, (rows, features), lambda j, m, w: (m, 0))]
        + [(array, (height, wide), column) for array, height, _, _ in up]
        + [(bias, (1, wide), column)],
        [out, out],
        flops=2 * tokens * features * hidden,
        nbytes=2 * features * (hidden + 2 * tokens) + 4 * tokens * hidden,
        name="feed_up",
    )


def pre_grad_kernel(w, c0, c1, c2, c3, n0, n1, n2, slope, out, total):
    quarter = c0.shape[1]
    act_grad = (
        mm(c0[...], n0[:, :quarter], NT)
        + mm(c1[...], n0[:, quarter:], NT)
        + mm(c2[...], n1[...], NT)
        + mm(c3[...], n2[...], NT)
    )
    grad = (act_grad * slope[...].astype(F32)).astype(BF16)
    out[...] = grad

    @pl.when(pl.program_id(1) == 0)
    def _():
        total[...] = jnp.zeros_like(total)

    total[...] += groups(grad.astype(F32))


def pre_grads(line, w, rows, cot, down, slope):
    tokens, features = cot.shape
    hidden = slope.shape[1]
    wide = min(1024, hidden)
    quarter = features // 4
    inputs = []
    for b in range(4):
        inputs.append((cot, (rows, quarter), lambda j, m, w, b=b: (m, w[b])))
    inputs += [(array, (wide, width), lambda j, m, w: (j, 0)) for array, _, width, _ in down]
    tile = ((rows, wide), lambda j, m, w: (m, j))
    return call(
        line,
        pre_grad_kernel,
        w,
        (hidden // wide, tokens // rows),
        inputs + [(slope, *tile)],
        [
            ((tokens, hidden), BF16, *tile),
            ((8, hidden), F32, (8, wide), lambda j, m, w: (0, j)),
        ],
        flops=2 * tokens * features * hidden,
        nbytes=2 * features * (hidden + 2 * tokens) + 4 * tokens * hidden,
        name="pre_grads",
    )


def back_kernel(more, w, grad, w0, w1, w2, x, gain, *refs):
    if more:
        before, out, sums, e = refs
    else:
        out, sums, e = refs
    features = x.shape[1]
    quarter = features // 4
    rows = x.shape[0]

    @pl.when(pl.program_id(0) == 0)
    def _():
        sums[...] = jnp.zeros_like(sums)

    e[:, : 2 * quarter] = mm(grad[...], w0[...], NT)
    e[:, 2 * quarter : 3 * quarter] = mm(grad[...], w1[...], NT)
    e[:, 3 * quarter :] = mm(grad[...], w2[...], NT)
    values = x[...].astype(F32)
    mean = jnp.mean(values, -1, keepdims=True)
    center = values - mean
    inverse = lax.rsqrt(jnp.mean(center * center, -1, keepdims=True) + EPS)
    middle = jnp.zeros((rows, 1), F32)
    slant = jnp.zeros((rows, 1), F32)
    for b in range(4):
        at = slice(b * quarter, (b + 1) * quarter)
        unit = (x[:, columns_at(w, b, quarter)].astype(F32) - mean) * inverse
        found = e[:, at]
        sums[0:8, at] += groups(found * unit)
        sums[8:16, at] += groups(found)
        scaled = found * gain[:, at]
        middle += jnp.sum(scaled, -1, keepdims=True)
        slant += jnp.sum(scaled * unit, -1, keepdims=True)
    middle = middle * (1.0 / features)
    slant = slant * (1.0 / features)
    for b in range(4):
        at = slice(b * quarter, (b + 1) * quarter)
        place = columns_at(w, b, quarter)
        unit = (x[:, place].astype(F32) - mean) * inverse
        part = inverse * (e[:, at] * gain[:, at] - middle - unit * slant)
        if more:
            part = part + before[:, place].astype(F32)
        out[:, place] = part.astype(BF16)


def backs(line, w, rows, first, count, grad, weight, x, gain, before=None):
    features = x.shape[1]
    width = grad.shape[1]
    row = (rows, features)
    shift = lambda m, w: (m + first, 0)
    along = lambda m, w: (m, 0)
    inputs = [(grad, (rows, width), along)]
    inputs += [(array, (height, wide), fixed(0, place)) for array, height, wide, place in weight]
    inputs += [(x, row, shift), (gain, gain.shape, fixed(0, 0))]
    if before is not None:
        inputs.append((before, row, shift))
    return call(
        line,
        functools.partial(back_kernel, before is not None),
        w,
        (count,),
        inputs,
        [
            ((count * rows, features), BF16, row, along),
            ((16, features), F32, (16, features), fixed(0, 0)),
        ],
        scratch=[pltpu.VMEM(row, F32)],
        flops=2 * count * rows * features * width,
        nbytes=2 * (features * width + count * rows * (width + 3 * features)),
        name="backs",
    )


def output_kernel(heads, w, act, n0, n1, n2, d0, d1, d2, *refs):
    blocks = refs[:heads]
    part, attended, qkv_grad, total = refs[heads:]
    quarter = n1.shape[1]

    @pl.when(pl.program_id(0) == 0)
    def _():
        total[...] = jnp.zeros_like(total)

    for i in range(heads):
        head = w[ORDER + i]
        attended[:, pl.ds(pl.multiple_of(head * HD, HD), HD)] = blocks[i][:, :HD]
        at = pl.ds(pl.multiple_of(head * 3 * HD, HD), 3 * HD)
        qkv_grad[:, at] = blocks[i][:, HD:]
        total[:, at] += groups(blocks[i][:, HD:].astype(F32))
    pieces = [(n0, d0, 0), (n0, d0, 1), (n1, d1, 0), (n2, d2, 0)]
    for b, (down, dense, half) in enumerate(pieces):
        at = slice(half * quarter, (half + 1) * quarter)
        part[:, columns_at(w, b, quarter)] = (
            mm(attended[...], dense[:, at]) + mm(act[...], down[:, at])
        ).astype(BF16)


def outputs(line, w, first, rows, act, down, dense, blocks):
    hidden = act.shape[1]
    inner = dense[0][1]
    features = 2 * dense[0][2]
    heads = len(blocks)
    count = 1
    along = lambda m, w: (m, 0)
    inputs = [(act, (rows, hidden), lambda m, w: (m + first, 0))]
    for array, height, width, place in (*down, *dense):
        inputs.append((array, (height, width), fixed(0, place)))
    inputs += [(block, block.shape, fixed(0, 0)) for block in blocks]
    wide = lambda size: ((count * rows, size), BF16, (rows, size), along)
    return call(
        line,
        functools.partial(output_kernel, heads),
        w,
        (count,),
        inputs,
        [
            wide(features),
            wide(inner),
            wide(3 * inner),
            ((8, 3 * inner), F32, (8, 3 * inner), fixed(0, 0)),
        ],
        flops=2 * count * rows * features * (hidden + inner),
        nbytes=2 * features * (hidden + inner)
        + 2 * count * rows * (hidden + features + 8 * inner),
        name="outputs",
    )


def grad_kernel(pieces, count, at_left, adds, w, *refs):
    sides, swept = refs[: (1 if at_left else count)], refs[1 if at_left else count :]
    rest = swept[pieces:]
    swept = swept[:pieces]
    out = rest[-1]
    for i, side in enumerate(sides):
        value = 0.0
        start = 0
        for ref in swept:
            part = side[start : start + ref.shape[0], :]
            start += ref.shape[0]
            value = value + (mm(part, ref[...], TN) if at_left else mm(ref[...], part, TN))
        if adds:
            value = value + rest[0][i].astype(F32)
        out[i] = value.astype(BF16)


def weight_grad(line, w, at, at_left, side, swept, adds=None):
    tokens = side.shape[0]
    quarter = side.shape[1] // 4
    size = swept[0].shape[1]
    tile = min(256, quarter, size)
    heights = [piece.shape[0] for piece in swept]
    if at_left:
        split = quarter // tile
        grid = (2, split)
        inputs = [(side, (tokens, tile), lambda i, j, w: (0, w.either(at, i) * split + j))]
        inputs += [(piece, piece.shape, fixed(0, 0)) for piece in swept]
        out = ((2, quarter, size), BF16, (1, tile, size), lambda i, j, w: (i, j, 0))
    else:
        grid = (size // tile,)
        inputs = []
        for i in range(2):
            inputs.append((side, (tokens, quarter), lambda j, w, i=i: (0, w[at + i])))
        inputs += [(piece, (piece.shape[0], tile), lambda j, w: (0, j)) for piece in swept]
        out = ((2, size, quarter), BF16, (2, tile, quarter), lambda j, w: (0, j, 0))
    if adds is not None:
        inputs.append((adds, out[2], out[3]))
    return call(
        line,
        functools.partial(grad_kernel, len(swept), 2, at_left, adds is not None),
        w,
        grid,
        inputs,
        [out],
        flops=4 * tokens * quarter * size,
        nbytes=2 * tokens * (2 * quarter + size) + 8 * quarter * size,
        name="weight_grad",
    )[0]


def join(pieces):
    return [(piece, piece.shape, fixed(0, 0)) for piece in pieces]


def add_kernel(w, mine, *refs):
    *pieces, out = refs
    first = 0
    for piece in pieces:
        at = slice(first, first + piece.shape[0])
        out[at, :] = (mine[at, :].astype(F32) + piece[...].astype(F32)).astype(BF16)
        first += piece.shape[0]


def add(line, w, mine, pieces):
    shape = mine.shape[-2:]
    first = (mine, (None,) + shape, fixed(0, 0, 0)) if mine.ndim == 3 else (mine, shape, fixed(0, 0))
    return call(
        line,
        add_kernel,
        w,
        (1,),
        [first] + join(pieces),
        [(shape, BF16, shape, fixed(0, 0))],
        nbytes=6 * shape[0] * shape[1],
        name="add",
    )[0]


def first_half_kernel(w, mine, *refs):
    *pieces, wide, total = refs
    first = 0
    for piece in pieces:
        at = slice(first, first + piece.shape[0])
        value = (mine[at, :].astype(F32) + piece[...].astype(F32)).astype(BF16)
        total[at, :] = value
        wide[at, :] = value.astype(F32)
        first += piece.shape[0]


def first_half(line, w, at_left, mine, pieces):
    height, width = mine.shape
    if at_left:
        whole, place = (2 * height, width), lambda i, w: (w[KEEP], 0)
    else:
        whole, place = (height, 2 * width), lambda i, w: (0, w[KEEP])
    return call(
        line,
        first_half_kernel,
        w,
        (1,),
        [(mine, mine.shape, fixed(0, 0))] + join(pieces),
        [(whole, F32, mine.shape, place), (mine.shape, BF16, mine.shape, fixed(0, 0))],
        nbytes=10 * height * width,
        name="first_half",
    )


def second_half_kernel(w, held, other, wide):
    wide[...] = other[...].astype(F32)


def second_half(line, w, at_left, held, other):
    height, width = other.shape
    size = height // 2
    if at_left:
        whole, place = (2 * height, width), lambda i, w: (2 * w[SEND] + i, 0)
    else:
        whole, place = (height, 2 * width), lambda i, w: (i, w[SEND])
    return call(
        line,
        second_half_kernel,
        w,
        (2,),
        [(held, None, None), (other, (size, width), lambda i, w: (i, 0))],
        [(whole, F32, (size, width), place)],
        nbytes=6 * height * width,
        name="second_half",
        alias=0,
    )[0]


def gate_kernel(w, source, target):
    pass


def gate(line, w, array):
    return call(
        line,
        gate_kernel,
        w,
        (1,),
        [(array, None, None)],
        [(array.shape, array.dtype, None, None)],
        name="gate",
        alias=0,
    )[0]


def finish_kernel(more, w, kept, cols, *refs):
    refs = refs[1:] if more == "held" else refs
    *bias, out = refs
    value = kept[...].astype(F32) + cols[...].astype(F32)
    for ref in bias:
        value = value + ref[...]
    out[...] = value.astype(out.dtype)


def finish(line, w, m, held, kept, cols, bias, shape, dtype):
    count, rows, columns = shape
    block = (rows, columns)
    inputs = [
        (kept, (None,) + block, lambda i, w: (m, 0, w[TENSOR])),
        (cols, block, fixed(0, 0)),
    ]
    if held is not None:
        inputs.append((held, None, None))
    if bias is not None:
        inputs.append((bias, (1, columns), lambda i, w: (0, w[TENSOR])))
    return call(
        line,
        functools.partial(finish_kernel, None if held is None else "held"),
        w,
        (1,),
        inputs,
        [(shape, dtype, (None,) + block, fixed(m, 0, 0))],
        nbytes=8 * rows * columns,
        name="finish",
        alias=None if held is None else 2,
    )[0]


def pick_kernel(joint, w, by_rows, by_columns, *targets):
    if joint:
        width = by_columns.shape[1]
        targets[0][:, : by_rows.shape[1]] = by_rows[...]
        targets[0][: by_columns.shape[0], targets[0].shape[1] - width :] = by_columns[...]
    else:
        targets[0][...] = by_rows[...]
        targets[1][...] = by_columns[...]


def pick(line, w, by_rows, by_columns, joint):
    height, width = by_rows.shape[0] // 2, by_columns.shape[1] // 2
    first = (height, by_rows.shape[1])
    second = (by_columns.shape[0], width)
    if joint:
        shapes = [(max(first[0], second[0]), pl.cdiv(first[1], width) * width + width)]
    else:
        shapes = [first, second]
    return call(
        line,
        functools.partial(pick_kernel, joint),
        w,
        (1,),
        [
            (by_rows, first, lambda i, w: (w[KEEP], 0)),
            (by_columns, second, lambda i, w: (0, w[KEEP])),
        ],
        [(shape, BF16, shape, fixed(0, 0)) for shape in shapes],
        nbytes=4 * (first[0] * first[1] + second[0] * second[1]),
        name="pick",
    )


def on_device(
    states,
    ln1_gain,
    ln1_bias,
    ln2_gain,
    ln2_bias,
    qkv_weight,
    qkv_bias,
    dense_weight,
    dense_bias,
    up_weight,
    up_bias,
    down_weight,
    out_bias,
    out_grad,
):
    micros, rows, features = states.shape
    heads = qkv_weight.shape[1] // (3 * HD)
    tokens = micros * rows
    n = lax.axis_size("seq")
    pairs = heads * micros // n
    straight = heads == n
    s = lax.axis_index("seq")
    core = s % 2
    d = lax.axis_index("dp")
    columns = features // lax.axis_size("tensor")
    first = lax.axis_index("tensor") * columns
    w = Places(straight)

    def absolute(own, other):
        return jnp.where(d == 1, jnp.concatenate([other, own]), jnp.concatenate([own, other]))

    x = states.reshape(tokens, features)
    cot = out_grad.reshape(tokens, features)

    small = (ln1_gain, ln1_bias, ln2_gain, ln2_bias, dense_bias, out_bias, qkv_bias, up_bias)
    small_got = swap(jnp.concatenate(small, 0), "dp", 1)
    line = Line(small_got)
    joint_half = swap(pick(line, w, qkv_weight, dense_weight, True)[0], "dp", 1)
    own, other = [], []
    place = 0
    for vector in small:
        own.append(vector.astype(F32))
        other.append(small_got[place : place + vector.shape[0]].astype(F32))
        place += vector.shape[0]
    half = features // 4
    vectors = jnp.stack(
        [
            jnp.concatenate(
                [
                    own[i],
                    lax.dynamic_slice_in_dim(other[i], core * half, half),
                    lax.dynamic_slice_in_dim(other[i], (1 - core) * half, half),
                ]
            )
            for i in range(4)
        ]
    )
    tables = turn_tables(n * rows)

    one, two, cot_total = norms(line, w, x, cot, vectors)
    halves = pick(line, w, up_weight, down_weight, False)
    up_got = swap(halves[0], "dp", 1)
    down_got = swap(halves[1], "dp", 1)
    got = gate(line, w, joint_half)
    joint = (got, swap(got, "seq", 1))
    height, width = qkv_weight.shape[0], qkv_weight.shape[1]
    qkv = [(qkv_weight, height, width, 0)] + [(half, height // 2, width, 0) for half in joint]
    height, width = dense_weight.shape[0], dense_weight.shape[1]
    dense = [(dense_weight, height, width, 0)] + [
        (half, height, width // 2, half.shape[1] // (width // 2) - 1) for half in joint
    ]
    qkv_shift = absolute(own[6], other[6])[None]
    up_shift = absolute(own[7], other[7])[None]
    bias = absolute(own[4] + own[5], other[4] + other[5])[None]
    payload, arrived, results, attended, qkv_grad = {}, {}, {}, {}, {}
    branch, back_cols, held = {}, {}, {"output": None, "input_grad": None}
    out_shape = (micros, rows, columns)
    totals = {"qkv": 0.0, "one": 0.0}
    sizes = GROUPS if micros == sum(GROUPS) else (1,) * micros
    starts = [sum(sizes[:i]) for i in range(len(sizes))]

    def project(group):
        found = projections(
            line, w, starts[group], sizes[group], rows, one, qkv, qkv_shift, tables, cot, dense
        )
        for i in range(sizes[group]):
            payload[starts[group] + i] = [(array, i) for array in found]

    def bring(m, *distances):
        for k in distances if straight else ():
            array, place = payload[m][k]
            arrived[m, k] = line.ride(array, "seq", k, place * rows, rows)

    def attend(m):
        if straight:
            blocks = [payload[m][0]] + [(arrived[m, k].result, 0) for k in range(1, n)]
            results[m] = list(attention(line, w, rows, blocks, tables))

    def give(m, *distances):
        for k in distances if straight else ():
            results[m][k] = line.ride(results[m][k], "seq", k)

    def attend_pairs():
        blocks = []
        for h in range(heads):
            for m in range(micros):
                array, place = payload[m][h]
                blocks.append(array[place * rows : (place + 1) * rows])
        stacked = jnp.stack(blocks).reshape(n, pairs, rows, 4 * HD)
        found = []
        for pair in range(pairs):
            sent = [
                lax.dynamic_index_in_dim(stacked[:, pair], s ^ k, 0, False) for k in range(n)
            ]
            sent = [sent[0]] + [swap(sent[k], "seq", k) for k in range(1, n)]
            back = attention(line, w, rows, [(array, 0) for array in sent], tables)
            found.append(jnp.stack([back[0]] + [swap(back[k], "seq", k) for k in range(1, n)]))
        for m in range(micros):
            results[m] = []
            for h in range(heads):
                device, pair = divmod(h * micros + m, pairs)
                results[m].append(
                    lax.dynamic_index_in_dim(found[pair], s ^ device, 0, False)
                )

    def both_cores(shard, got, by_rows):
        got = gate(line, w, got)
        return [(shard, *shard.shape, 0)] + [
            (half, *half.shape, 0) for half in (got, swap(got, "seq", 1))
        ]

    def put_out(m):
        if not straight and not results:
            attend_pairs()
        blocks = [block.result if isinstance(block, Ride) else block for block in results[m]]
        partial, attended[m], qkv_grad[m], total = outputs(
            line, w, m, rows, activated, down, dense, blocks
        )
        totals["qkv"] = totals["qkv"] + total
        branch[m] = lax.psum_scatter(partial, "tensor", scatter_dimension=1, tiled=True)

    def go_back(m):
        part, sums = backs(line, w, rows, m, 1, qkv_grad[m], qkv, x, vectors[0:1], part_two)
        totals["one"] = totals["one"] + sums
        back_cols[m] = lax.psum_scatter(part, "tensor", scatter_dimension=1, tiled=True)

    def finish_out(m):
        held["output"] = finish(
            line, w, m, held["output"], states, branch[m], bias, out_shape, BF16
        )

    def finish_back(m):
        held["input_grad"] = finish(
            line, w, m, held["input_grad"], out_grad, back_cols[m], None, out_shape, F32
        )

    grads, terms = {}, {
        "down": (False, cot, None),
        "up": (True, two, None),
        "dense": (False, cot, None),
        "qkv": (True, one, None),
    }
    steps = {}

    found, rides = {}, {}

    def send(name, swept):
        at_left, side, _ = terms[name]
        terms[name] = (at_left, side, swept)
        at = SEND if at_left else SEND_AT
        sent = weight_grad(line, w, at, at_left, side, swept)
        found[name] = sent.reshape(-1, sent.shape[2])

    def to_sibling(name):
        rides[name] = line.ride(found[name], "seq", 1)

    def keep(name):
        at_left, side, swept = terms[name]
        at = KEEP if at_left else KEEP_AT
        added = rides[name].result
        added = added.reshape(2, added.shape[0] // 2, added.shape[1])
        found[name] = weight_grad(line, w, at, at_left, side, swept, added)
        rides[name] = []

    def parts(name, count):
        height = found[name].shape[-2]
        size = height // PIECES[name]
        first = sum(ride.rows for ride in rides[name])
        return [(first + i * size, size) for i in range(count)]

    def over_y(name, count):
        for first, size in parts(name, count):
            rides[name].append(line.ride(found[name], "dp", 1, first, size, lead=1))

    def over_x(name, count):
        for first, size in parts(name, count):
            rides[name].append(line.ride(found[name], "seq", steps[name], first, size))

    def all_over_y(name):
        rides[name] = [swap(found[name][1], "dp", 1)]

    def all_over_x(name):
        rides[name] = [swap(found[name], "seq", steps[name])]

    def landed(name):
        return [ride.result if isinstance(ride, Ride) else ride for ride in rides[name]]

    def add_up(name):
        found[name] = add(line, w, found[name], landed(name))
        rides[name] = []
        steps[name] = 2
        while 2 * steps[name] < n:
            found[name] = add(
                line, w, found[name], [swap(found[name], "seq", steps[name])]
            )
            steps[name] *= 2
            rides[name] = []

    def mine_done(name):
        held[name], found[name] = first_half(
            line, w, terms[name][0], found[name], landed(name)
        )

    def sibling_swap(name):
        rides[name] = swap(found[name], "seq", 1)

    def all_done(name):
        ride = rides[name]
        other = ride.result if isinstance(ride, Ride) else ride
        grads[name] = second_half(line, w, terms[name][0], held[name], other)

    def all_terms():
        one_sums, qkv_total = totals["one"], totals["qkv"]
        sums = jnp.concatenate([one_sums, two_sums], 0).reshape(4, 8, features).sum(1)
        norm_own, norm_oth = sums[:, : 2 * half], sums[:, 2 * half :]
        norm_oth = jnp.where(
            core == 1,
            jnp.concatenate([norm_oth[:, half:], norm_oth[:, :half]], 1),
            norm_oth,
        )
        norm_terms = jnp.where(
            d == 1,
            jnp.concatenate([norm_oth, norm_own], 1),
            jnp.concatenate([norm_own, norm_oth], 1),
        ).reshape(-1)
        rest = jnp.concatenate([qkv_total.sum(0), up_total.sum(0), cot_total.sum(0)])
        return norm_terms, rest

    def hop(vector, axis, step):
        vector = gate(line, w, vector)
        return vector + swap(vector, axis, step)

    project(0)
    bring(0, 1, 2, 3)
    project(1)
    bring(1, 1, 2)
    attend(0)
    up = both_cores(up_weight, up_got, True)
    bring(1, 3)
    give(0, 1, 2, 3)
    activated, slope = feed_up(line, w, rows, two, up, up_shift)
    down = both_cores(down_weight, down_got, False)
    put_out(0)
    bring(2, 1, 2)
    attend(1)
    send("down", [activated])
    give(1, 1, 2, 3)
    pre_grad, up_total = pre_grads(line, w, rows, cot, down, slope)
    to_sibling("down")
    put_out(1)
    bring(2, 3)
    keep("down")
    bring(3, 1, 2, 3)
    over_y("down", 3)
    part_two, two_sums = backs(line, w, rows, 0, micros, pre_grad, up, x, vectors[2:3])
    go_back(0)
    over_y("down", 1)
    attend(2)
    give(2, 1, 2)
    attend(3)
    give(2, 3)
    give(3, 1)
    send("up", [pre_grad])
    to_sibling("up")
    put_out(2)
    add_up("down")
    give(3, 2)
    keep("up")
    give(3, 3)
    over_y("up", 1)
    go_back(1)
    finish_out(0)
    over_x("down", 1)
    over_y("up", 1)
    put_out(3)
    over_x("down", 1)
    over_y("up", 1)
    go_back(2)
    heads_out = [attended[m] for m in range(micros)]
    heads_grad = [qkv_grad[m] for m in range(micros)]
    over_x("down", 1)
    over_y("up", 1)
    send("qkv", heads_grad)
    finish_out(1)
    add_up("up")
    over_x("down", 1)
    to_sibling("qkv")
    go_back(3)
    over_x("up", 1)
    keep("qkv")
    mine_done("down")
    finish_back(0)
    all_over_y("qkv")
    to_sibling("down")
    over_x("up", 1)
    send("dense", heads_out)
    to_sibling("dense")
    over_x("up", 2)
    norm_terms, rest = all_terms()
    step = 1
    while step < lax.axis_size("tensor"):
        norm_terms, step = hop(norm_terms, "tensor", step), 2 * step
    keep("dense")
    all_over_y("dense")
    mine_done("up")
    add_up("qkv")
    all_over_x("qkv")
    sibling_swap("up")
    finish_out(2)
    vector = hop(jnp.concatenate([norm_terms, rest]), "dp", 1)
    add_up("dense")
    all_over_x("dense")
    all_done("down")
    all_done("up")
    finish_back(1)
    finish_out(3)
    step = 1
    while step < n:
        vector, step = hop(vector, "seq", step), 2 * step
    mine_done("qkv")
    sibling_swap("qkv")
    mine_done("dense")
    sibling_swap("dense")
    finish_back(2)
    all_done("qkv")
    all_done("dense")
    finish_back(3)
    norm_terms = vector[: 4 * features].reshape(4, features)
    rest = vector[4 * features :]
    count = columns // 2
    norm_mine = lax.dynamic_slice_in_dim(norm_terms, first + d * count, count, 1)
    vector_grads = []
    place = 0
    for size in (3 * HD * heads, up_total.shape[1], features):
        vector_grads.append(lax.dynamic_slice_in_dim(rest, place + d * (size // 2), size // 2, 0))
        place += size

    return (
        held["output"],
        held["input_grad"],
        norm_mine[0],
        norm_mine[1],
        norm_mine[2],
        norm_mine[3],
        grads["qkv"],
        vector_grads[0],
        grads["dense"],
        vector_grads[2],
        grads["up"],
        vector_grads[1],
        grads["down"],
        vector_grads[2],
    )


def solution(mesh):
    placed = (
        P("dp", "seq", None),
        P("dp"),
        P("dp"),
        P("dp"),
        P("dp"),
        P("dp", "tensor"),
        P(("tensor", "dp")),
        P("tensor", "dp"),
        P("dp"),
        P("dp", "tensor"),
        P(("tensor", "dp")),
        P("tensor", "dp"),
        P("dp"),
        P("dp", "seq", None),
    )
    return jax.shard_map(
        on_device,
        mesh=mesh,
        in_specs=placed,
        out_specs=(
            P("dp", "seq", "tensor"),
            P("dp", "seq", "tensor"),
            P(("tensor", "dp")),
            P(("tensor", "dp")),
            P(("tensor", "dp")),
            P(("tensor", "dp")),
            P("dp", "tensor"),
            P(("tensor", "dp")),
            P("tensor", "dp"),
            P("dp"),
            P("dp", "tensor"),
            P(("tensor", "dp")),
            P("tensor", "dp"),
            P("dp"),
        ),
        check_vma=False,
    )
```

```python
import functools
import math

import jax
import jax.numpy as jnp
import numpy as np
from jax import lax
from jax.experimental import pallas as pl
from jax.experimental.pallas import tpu as pltpu
from jax.sharding import PartitionSpec as P

HD = 128
ROT = 32
HALF_ROT = ROT // 2
EPS = 1e-05
F32 = jnp.float32
BF16 = jnp.bfloat16
NN = (((1,), (0,)), ((), ()))
NT = (((1,), (1,)), ((), ()))
TN = (((0,), (0,)), ((), ()))
WEIGHT = 0.1
GROUPS = (1, 3)
PIECES = {"down": 4, "up": 4, "qkv": 2, "dense": 1}
VMEM_LIMIT = 60 * 1024 * 1024
KEEP, SEND, KEEP_AT, SEND_AT, SEQ, TENSOR, ORDER = 4, 6, 8, 10, 12, 13, 14


def bit(value, b):
    return lax.rem(lax.div(value, jnp.int32(1 << b)), jnp.int32(2))


def xor(value, other):
    value, other = jnp.int32(value), jnp.int32(other)
    return sum((1 << b) * lax.rem(bit(value, b) + bit(other, b), jnp.int32(2)) for b in range(4))


class Places:
    def __init__(self, straight):
        self.straight = straight

    def __getitem__(self, key):
        s = lax.axis_index("seq")
        if key == SEQ:
            return s
        if key == TENSOR:
            return lax.axis_index("tensor")
        if key >= ORDER:
            return self.head(key - ORDER)
        core = lax.rem(s, jnp.int32(2))
        d = lax.axis_index("dp")
        places = (2 * d, 2 * d + 1, 2 * (1 - d) + core, 2 * (1 - d) + 1 - core)
        if key < KEEP:
            return places[key]
        if key < KEEP_AT:
            return (core, 2, 1 - core, 3)[key - KEEP]
        return (2 * d + core, places[2], 2 * d + 1 - core, places[3])[key - KEEP_AT]

    def head(self, slot):
        return xor(lax.axis_index("seq"), slot) if self.straight else slot

    def either(self, key, i):
        return (1 - i) * self[key] + i * self[key + 1]


class Ride:
    def __init__(self, source, axis, distance, first=0, rows=None, lead=None):
        self.source, self.axis, self.distance = source, axis, distance
        self.first, self.lead = first, lead
        self.rows = source.shape[-2] - first if rows is None else rows
        self.result = None

    @property
    def shape(self):
        return (self.rows, self.source.shape[-1])

    def target(self):
        return {self.axis: xor(lax.axis_index(self.axis), self.distance)}

    def copy(self, source, target, sent, got):
        at = pl.ds(self.first, self.rows)
        return pltpu.make_async_remote_copy(
            src_ref=source.at[at] if self.lead is None else source.at[self.lead, at],
            dst_ref=target,
            send_sem=sent,
            recv_sem=got,
            device_id=self.target(),
            device_id_type=pl.DeviceIdType.MESH,
        )


class Line:
    def __init__(self, first):
        self.last = [first]
        self.rides = []
        self.count = 0

    def ride(self, *args, **kwargs):
        self.rides.append(Ride(*args, **kwargs))
        return self.rides[-1]


def mm(a, b, dims=NN):
    return lax.dot_general(a, b, dims, preferred_element_type=F32)


def swap(block, axis, distance):
    return lax.ppermute(block, axis, [(i, i ^ distance) for i in range(lax.axis_size(axis))])


def spec(block, index):
    if block is None:
        return pl.BlockSpec(memory_space=pl.ANY)
    return pl.BlockSpec(block, index)


def call(line, kernel, w, grid, inputs, outputs, scratch=(), flops=0, nbytes=0, name=None, alias=None):
    before = [token for token in line.last if alias is None or token is not inputs[alias][0]]
    rides, line.rides = line.rides, []
    skip = len(before) + len(rides)
    ends = len(inputs) + len(outputs)
    steps = 1
    for size in grid:
        steps *= size
    staged = [i for i in range(len(inputs)) if rides and steps == 1 and inputs[i][1] is not None]

    def stage(ref, block, index):
        cut = []
        for size, place in zip(block, index(*[0] * len(grid), w)):
            if size is None:
                cut.append(place)
            elif isinstance(place, int):
                cut.append(slice(place * size, (place + 1) * size))
            else:
                cut.append(pl.ds(pl.multiple_of(place * size, size), size))
        return ref.at[tuple(cut)]

    def at(index):
        return None if index is None else lambda *steps: index(*steps, w)

    def on_step(last, work):
        chosen = True
        for axis, size in enumerate(grid):
            if size > 1:
                step = pl.program_id(axis)
                chosen = jnp.logical_and(chosen, step == (size - 1 if last else 0))
        if chosen is True:
            work()
        else:
            pl.when(chosen)(work)

    def body(*refs):
        sources = refs[len(before) : skip]
        own = refs[skip : skip + ends]
        targets = refs[skip + ends : skip + ends + len(rides)]
        rest = refs[skip + ends + len(rides) :]
        if not rides:
            kernel(w, *own, *rest)
            return
        *rest, sent, got = rest
        own = list(own)
        loads = []
        if staged:
            *rest, loaded = rest
            buffers = rest[len(rest) - len(staged) :]
            rest = rest[: len(rest) - len(staged)]
            for k, i in enumerate(staged):
                part = stage(own[i], *inputs[i][1:])
                loads.append(pltpu.make_async_copy(part, buffers[k], loaded.at[k]))
                own[i] = buffers[k]
        copies = lambda: [
            ride.copy(source, target, sent.at[i], got.at[i])
            for i, (ride, source, target) in enumerate(zip(rides, sources, targets))
        ]

        def start():
            barrier = pltpu.get_barrier_semaphore()
            partners = {(ride.axis, ride.distance): ride for ride in rides}
            for ride in partners.values():
                pl.semaphore_signal(
                    barrier, inc=1, device_id=ride.target(), device_id_type=pl.DeviceIdType.MESH
                )
            pl.semaphore_wait(barrier, len(partners))
            for copy in copies():
                copy.start()

        def wait():
            for copy in copies():
                copy.wait()

        for load in loads:
            load.start()
        on_step(False, start)
        for load in loads:
            load.wait()
        kernel(w, *own, *rest)
        on_step(True, wait)

    params = dict(
        vmem_limit_bytes=VMEM_LIMIT, dimension_semantics=("arbitrary",) * len(grid)
    )
    sems = []
    if rides:
        params.update(collective_id=line.count, has_side_effects=True)
        line.count += 1
        for i in staged:
            array, block, _ = inputs[i]
            shape = tuple(size for size in block if size is not None)
            sems.append(pltpu.VMEM(shape, array.dtype))
        if staged:
            sems.append(pltpu.SemaphoreType.DMA((len(staged),)))
        sems += [pltpu.SemaphoreType.DMA((len(rides),))] * 2
    anywhere = pl.BlockSpec(memory_space=pl.ANY)
    results = pl.pallas_call(
        body,
        grid=grid,
        in_specs=[anywhere] * skip
        + [
            anywhere if i in staged else spec(block, at(index))
            for i, (_, block, index) in enumerate(inputs)
        ],
        out_specs=[spec(block, at(index)) for _, _, block, index in outputs]
        + [anywhere] * len(rides),
        scratch_shapes=list(scratch) + sems,
        out_shape=[jax.ShapeDtypeStruct(shape, dtype) for shape, dtype, _, _ in outputs]
        + [jax.ShapeDtypeStruct(ride.shape, ride.source.dtype) for ride in rides],
        compiler_params=pltpu.CompilerParams(**params),
        cost_estimate=pl.CostEstimate(
            flops=int(flops * WEIGHT), bytes_accessed=int(nbytes * WEIGHT), transcendentals=0
        ),
        input_output_aliases={} if alias is None else {skip + alias: 0},
        name=name,
    )(*before, *[ride.source for ride in rides], *[array for array, _, _ in inputs])
    for ride, result in zip(rides, results[len(outputs) :]):
        ride.result = result
    results = results[: len(outputs)]
    line.last = [results[-1]]
    return results


def fixed(*index):
    return lambda *_: index


def groups(values):
    return jnp.sum(values.reshape(values.shape[0] // 8, 8, values.shape[1]), 0)


def columns_at(w, b, size):
    return pl.ds(pl.multiple_of(w[b] * size, size), size)


def norm_kernel(w, x, cot, vectors, one, two, total):
    quarter = x.shape[1] // 4

    @pl.when(pl.program_id(0) == 0)
    def _():
        total[...] = jnp.zeros_like(total)

    values = x[...].astype(F32)
    mean = jnp.mean(values, -1, keepdims=True)
    center = values - mean
    inverse = lax.rsqrt(jnp.mean(center * center, -1, keepdims=True) + EPS)
    for b in range(4):
        at = slice(b * quarter, (b + 1) * quarter)
        unit = (x[:, columns_at(w, b, quarter)].astype(F32) - mean) * inverse
        one[:, at] = (unit * vectors[0:1, at] + vectors[1:2, at]).astype(BF16)
        two[:, at] = (unit * vectors[2:3, at] + vectors[3:4, at]).astype(BF16)
    total[...] += groups(cot[...].astype(F32))


def norms(line, w, x, cot, vectors):
    tokens, features = x.shape
    size = min(256, tokens)
    row = (size, features)
    along = lambda i, w: (i, 0)
    return call(
        line,
        norm_kernel,
        w,
        (tokens // size,),
        [(x, row, along), (cot, row, along), (vectors, vectors.shape, fixed(0, 0))],
        [
            ((tokens, features), BF16, row, along),
            ((tokens, features), BF16, row, along),
            ((8, features), F32, (8, features), fixed(0, 0)),
        ],
        flops=30 * tokens * features,
        nbytes=8 * tokens * features,
        name="norms",
    )


def turned(values):
    lane = lax.broadcasted_iota(jnp.int32, values.shape, 1)
    return jnp.where(
        lane < HALF_ROT, pltpu.roll(values, HD - HALF_ROT, 1), pltpu.roll(values, HALF_ROT, 1)
    )


def turn_tables(length):
    frequency = 10000.0 ** (-np.arange(HALF_ROT) * 2.0 / ROT)
    angles = np.arange(length)[:, None] * frequency[None, :]
    cosine = np.ones((length, HD), np.float32)
    sine = np.zeros((length, HD), np.float32)
    cosine[:, :ROT] = np.tile(np.cos(angles), (1, 2))
    sine[:, :HALF_ROT] = np.sin(angles)
    sine[:, HALF_ROT:ROT] = -np.sin(angles)
    return jnp.asarray(cosine), jnp.asarray(sine)


def project_kernel(
    slots, w, one, q0, q1, q2, bias, cosine, sine, c0, c1, c2, c3, d0, d1, d2, *outs
):
    step = pl.program_id(0)
    quarter = c0.shape[1]
    u = (
        mm(one[:, : 2 * quarter], q0[...])
        + mm(one[:, 2 * quarter : 3 * quarter], q1[...])
        + mm(one[:, 3 * quarter :], q2[...])
        + bias[...]
    )
    g = (
        mm(c0[...], d0[:, :quarter], NT)
        + mm(c1[...], d0[:, quarter:], NT)
        + mm(c2[...], d1[...], NT)
        + mm(c3[...], d2[...], NT)
    )
    cos, sin = cosine[...], sine[...]
    rows = u.shape[0]
    at_rows = pl.ds(pl.multiple_of(pl.program_id(1) * rows, rows), rows)
    flip = lax.rem(w.head(2 * step), jnp.int32(2))
    blocks = []
    for head in range(2):
        at = head * 3 * HD
        query, key = u[:, at : at + HD], u[:, at + HD : at + 2 * HD]
        blocks.append(
            jnp.concatenate(
                [
                    (query * cos - turned(query) * sin).astype(BF16),
                    (key * cos - turned(key) * sin).astype(BF16),
                    u[:, at + 2 * HD : at + 3 * HD].astype(BF16),
                    g[:, head * HD : (head + 1) * HD].astype(BF16),
                ],
                1,
            )
        )
    for pair in range(slots // 2):
        for turn in range(2):

            @pl.when((step == pair) & (flip == turn))
            def _():
                outs[2 * pair + turn][at_rows, :] = blocks[0]
                outs[2 * pair + 1 - turn][at_rows, :] = blocks[1]


def projections(line, w, first, count, rows, one, qkv, bias, tables, cot, dense):
    features = one.shape[1]
    quarter = features // 4
    heads = dense[0][1] // HD
    wide = 6 * HD
    pair = lambda i, m, w: (0, lax.div(w.head(2 * i), jnp.int32(2)))
    own = lambda i, m, w: (w[SEQ], 0)
    inputs = [(one, (rows, features), lambda i, m, w: (m + first, 0))]
    inputs += [(array, (height, wide), pair) for array, height, _, _ in qkv]
    inputs += [(bias, (1, wide), pair)]
    inputs += [(table, (rows, HD), own) for table in tables]
    for b in range(4):
        inputs.append((cot, (rows, quarter), lambda i, m, w, b=b: (m + first, w[b])))
    for array, _, width, place in dense:
        inputs.append(
            (array, (2 * HD, width), lambda i, m, w, b=place: (lax.div(w.head(2 * i), jnp.int32(2)), b))
        )
    return call(
        line,
        functools.partial(project_kernel, heads),
        w,
        (heads // 2, count),
        inputs,
        [((count * rows, 4 * HD), BF16, (count * rows, 4 * HD), fixed(0, 0))] * heads,
        flops=2 * count * rows * features * heads * 4 * HD,
        nbytes=2 * features * (heads * 4 * HD + 2 * count * rows) + 8 * count * rows * heads * HD,
        name="projections",
    )


def attention_kernel(parts, scale, qsize, ksize, w, *refs):
    ins = refs[:parts]
    cos_ref, sin_ref = refs[parts : parts + 2]
    outs = refs[parts + 2 : 2 * parts + 2]
    q_s, k_s, v_s, g_s, kt_s, vt_s, prob_s, dk_s, dv_s, o_s, dq_s = refs[2 * parts + 2 :]
    rows = ins[0].shape[0]
    length = parts * rows
    places = []
    for k in range(parts):
        at = pl.ds(pl.multiple_of(xor(w[SEQ], k) * rows, rows), rows)
        places.append(at)
        q_s[at, :] = ins[k][:, 0:HD]
        k_s[at, :] = ins[k][:, HD : 2 * HD]
        v_s[at, :] = ins[k][:, 2 * HD : 3 * HD]
        g_s[at, :] = ins[k][:, 3 * HD : 4 * HD]
    for j in range(length // ksize):
        at = slice(j * ksize, (j + 1) * ksize)
        kt_s[:, at] = k_s[at, :].T
        vt_s[:, at] = v_s[at, :].T
    factor = scale * math.log2(math.e)
    for i in range(length // qsize):
        qat = slice(i * qsize, (i + 1) * qsize)
        q = q_s[qat, :]
        g = g_s[qat, :]
        chunks = []
        for first in range(0, (i + 1) * qsize, ksize):
            chunks.append((first, min(ksize, (i + 1) * qsize - first)))
        top = jnp.full((8, qsize), -1e30, F32)
        for first, size in chunks:
            s = mm(k_s[first : first + size, :], q, NT)
            if first + size > i * qsize:
                key = lax.broadcasted_iota(jnp.int32, s.shape, 0) + (first - i * qsize)
                query = lax.broadcasted_iota(jnp.int32, s.shape, 1)
                s = jnp.where(key <= query, s, -1e30)
            prob_s[first : first + size, :] = s
            top = jnp.maximum(top, jnp.max(s.reshape(size // 8, 8, qsize), 0))
        top = jnp.max(top, 0, keepdims=True)
        total = jnp.zeros((8, qsize), F32)
        acc = jnp.zeros((HD, qsize), F32)
        for first, size in chunks:
            e = jnp.exp2((prob_s[first : first + size, :] - top) * factor)
            prob_s[first : first + size, :] = e
            total = total + jnp.sum(e.reshape(size // 8, 8, qsize), 0)
            acc = acc + mm(vt_s[:, first : first + size], e.astype(BF16))
        inverse = 1.0 / jnp.sum(total, 0, keepdims=True)
        acc = acc * inverse
        delta = jnp.sum(acc * g.T.astype(F32), 0, keepdims=True)
        o_s[qat, :] = acc.T.astype(BF16)
        dqt = jnp.zeros((HD, qsize), F32)
        for first, size in chunks:
            at = slice(first, first + size)
            p = prob_s[at, :] * inverse
            ds = (p * (mm(v_s[at, :], g, NT) - delta)).astype(BF16)
            dv = mm(p.astype(BF16), g)
            dk = mm(ds, q)
            low = max(0, min(size, i * qsize - first))
            if low:
                old = slice(first, first + low)
                dv_s[old, :] += dv[:low]
                dk_s[old, :] += dk[:low]
            if low < size:
                new = slice(first + low, first + size)
                dv_s[new, :] = dv[low:]
                dk_s[new, :] = dk[low:]
            dqt = dqt + mm(kt_s[:, at], ds)
        dq_s[qat, :] = dqt.T
    for k in range(parts):
        at = places[k]
        cosine = cos_ref[at, :]
        sine = sin_ref[at, :]
        dq, dk = dq_s[at, :], dk_s[at, :]
        outs[k][:, 0:HD] = o_s[at, :]
        outs[k][:, HD : 2 * HD] = ((dq * cosine + turned(dq) * sine) * scale).astype(BF16)
        outs[k][:, 2 * HD : 3 * HD] = ((dk * cosine + turned(dk) * sine) * scale).astype(BF16)
        outs[k][:, 3 * HD : 4 * HD] = dv_s[at, :].astype(BF16)


def attention(line, w, rows, blocks, tables, qsize=512, ksize=512):
    parts = len(blocks)
    width = blocks[0][0].shape[1]
    count = 1
    length = parts * rows
    qsize, ksize = min(qsize, rows), min(ksize, rows)
    block = ((rows, width), lambda m, w: (m, 0))
    return call(
        line,
        functools.partial(attention_kernel, parts, HD ** (-0.5), qsize, ksize),
        w,
        (count,),
        [(array, (rows, width), fixed(place, 0)) for array, place in blocks] + [(table, (length, HD), fixed(0, 0)) for table in tables],
        [((count * rows, width), BF16, *block)] * parts,
        scratch=[pltpu.VMEM((length, HD), BF16)] * 4
        + [pltpu.VMEM((HD, length), BF16)] * 2
        + [pltpu.VMEM((length, qsize), F32)]
        + [pltpu.VMEM((length, HD), F32)] * 2
        + [pltpu.VMEM((length, HD), BF16)]
        + [pltpu.VMEM((length, HD), F32)],
        flops=14 * count * length * length * HD,
        nbytes=4 * count * length * width + 8 * length * HD,
        name="attention",
    )


def up_kernel(w, two, u0, u1, u2, bias, activated, slope):
    quarter = u1.shape[0]
    pre = (
        mm(two[:, : 2 * quarter], u0[...])
        + mm(two[:, 2 * quarter : 3 * quarter], u1[...])
        + mm(two[:, 3 * quarter :], u2[...])
        + bias[...]
    )
    tail = 0.5 + 0.5 * lax.erf(pre * math.sqrt(0.5))
    activated[...] = (pre * tail).astype(BF16)
    bell = jnp.exp2(pre * pre * (-0.5 * math.log2(math.e))) * (1.0 / math.sqrt(2.0 * math.pi))
    slope[...] = (tail + pre * bell).astype(BF16)


def feed_up(line, w, rows, two, up, bias):
    tokens, features = two.shape
    hidden = up[0][2]
    wide = min(1024, hidden)
    column = lambda j, m, w: (0, j)
    out = ((tokens, hidden), BF16, (rows, wide), lambda j, m, w: (m, j))
    return call(
        line,
        up_kernel,
        w,
        (hidden // wide, tokens // rows),
        [(two, (rows, features), lambda j, m, w: (m, 0))]
        + [(array, (height, wide), column) for array, height, _, _ in up]
        + [(bias, (1, wide), column)],
        [out, out],
        flops=2 * tokens * features * hidden,
        nbytes=2 * features * (hidden + 2 * tokens) + 4 * tokens * hidden,
        name="feed_up",
    )


def pre_grad_kernel(w, c0, c1, c2, c3, n0, n1, n2, slope, out, total):
    quarter = c0.shape[1]
    act_grad = (
        mm(c0[...], n0[:, :quarter], NT)
        + mm(c1[...], n0[:, quarter:], NT)
        + mm(c2[...], n1[...], NT)
        + mm(c3[...], n2[...], NT)
    )
    grad = (act_grad * slope[...].astype(F32)).astype(BF16)
    out[...] = grad

    @pl.when(pl.program_id(1) == 0)
    def _():
        total[...] = jnp.zeros_like(total)

    total[...] += groups(grad.astype(F32))


def pre_grads(line, w, rows, cot, down, slope):
    tokens, features = cot.shape
    hidden = slope.shape[1]
    wide = min(1024, hidden)
    quarter = features // 4
    inputs = []
    for b in range(4):
        inputs.append((cot, (rows, quarter), lambda j, m, w, b=b: (m, w[b])))
    inputs += [(array, (wide, width), lambda j, m, w: (j, 0)) for array, _, width, _ in down]
    tile = ((rows, wide), lambda j, m, w: (m, j))
    return call(
        line,
        pre_grad_kernel,
        w,
        (hidden // wide, tokens // rows),
        inputs + [(slope, *tile)],
        [
            ((tokens, hidden), BF16, *tile),
            ((8, hidden), F32, (8, wide), lambda j, m, w: (0, j)),
        ],
        flops=2 * tokens * features * hidden,
        nbytes=2 * features * (hidden + 2 * tokens) + 4 * tokens * hidden,
        name="pre_grads",
    )


def back_kernel(more, w, grad, w0, w1, w2, x, gain, *refs):
    if more:
        before, out, sums, e = refs
    else:
        out, sums, e = refs
    features = x.shape[1]
    quarter = features // 4
    rows = x.shape[0]

    @pl.when(pl.program_id(0) == 0)
    def _():
        sums[...] = jnp.zeros_like(sums)

    e[:, : 2 * quarter] = mm(grad[...], w0[...], NT)
    e[:, 2 * quarter : 3 * quarter] = mm(grad[...], w1[...], NT)
    e[:, 3 * quarter :] = mm(grad[...], w2[...], NT)
    values = x[...].astype(F32)
    mean = jnp.mean(values, -1, keepdims=True)
    center = values - mean
    inverse = lax.rsqrt(jnp.mean(center * center, -1, keepdims=True) + EPS)
    middle = jnp.zeros((rows, 1), F32)
    slant = jnp.zeros((rows, 1), F32)
    for b in range(4):
        at = slice(b * quarter, (b + 1) * quarter)
        unit = (x[:, columns_at(w, b, quarter)].astype(F32) - mean) * inverse
        found = e[:, at]
        sums[0:8, at] += groups(found * unit)
        sums[8:16, at] += groups(found)
        scaled = found * gain[:, at]
        middle += jnp.sum(scaled, -1, keepdims=True)
        slant += jnp.sum(scaled * unit, -1, keepdims=True)
    middle = middle * (1.0 / features)
    slant = slant * (1.0 / features)
    for b in range(4):
        at = slice(b * quarter, (b + 1) * quarter)
        place = columns_at(w, b, quarter)
        unit = (x[:, place].astype(F32) - mean) * inverse
        part = inverse * (e[:, at] * gain[:, at] - middle - unit * slant)
        if more:
            part = part + before[:, place].astype(F32)
        out[:, place] = part.astype(BF16)


def backs(line, w, rows, first, count, grad, weight, x, gain, before=None):
    features = x.shape[1]
    width = grad.shape[1]
    row = (rows, features)
    shift = lambda m, w: (m + first, 0)
    along = lambda m, w: (m, 0)
    inputs = [(grad, (rows, width), along)]
    inputs += [(array, (height, wide), fixed(0, place)) for array, height, wide, place in weight]
    inputs += [(x, row, shift), (gain, gain.shape, fixed(0, 0))]
    if before is not None:
        inputs.append((before, row, shift))
    return call(
        line,
        functools.partial(back_kernel, before is not None),
        w,
        (count,),
        inputs,
        [
            ((count * rows, features), BF16, row, along),
            ((16, features), F32, (16, features), fixed(0, 0)),
        ],
        scratch=[pltpu.VMEM(row, F32)],
        flops=2 * count * rows * features * width,
        nbytes=2 * (features * width + count * rows * (width + 3 * features)),
        name="backs",
    )


def output_kernel(heads, w, act, n0, n1, n2, d0, d1, d2, *refs):
    blocks = refs[:heads]
    part, attended, qkv_grad, total = refs[heads:]
    quarter = n1.shape[1]

    @pl.when(pl.program_id(0) == 0)
    def _():
        total[...] = jnp.zeros_like(total)

    for i in range(heads):
        head = w[ORDER + i]
        attended[:, pl.ds(pl.multiple_of(head * HD, HD), HD)] = blocks[i][:, :HD]
        at = pl.ds(pl.multiple_of(head * 3 * HD, HD), 3 * HD)
        qkv_grad[:, at] = blocks[i][:, HD:]
        total[:, at] += groups(blocks[i][:, HD:].astype(F32))
    pieces = [(n0, d0, 0), (n0, d0, 1), (n1, d1, 0), (n2, d2, 0)]
    for b, (down, dense, half) in enumerate(pieces):
        at = slice(half * quarter, (half + 1) * quarter)
        part[:, columns_at(w, b, quarter)] = (
            mm(attended[...], dense[:, at]) + mm(act[...], down[:, at])
        ).astype(BF16)


def outputs(line, w, first, rows, act, down, dense, blocks):
    hidden = act.shape[1]
    inner = dense[0][1]
    features = 2 * dense[0][2]
    heads = len(blocks)
    count = 1
    along = lambda m, w: (m, 0)
    inputs = [(act, (rows, hidden), lambda m, w: (m + first, 0))]
    for array, height, width, place in (*down, *dense):
        inputs.append((array, (height, width), fixed(0, place)))
    inputs += [(block, block.shape, fixed(0, 0)) for block in blocks]
    wide = lambda size: ((count * rows, size), BF16, (rows, size), along)
    return call(
        line,
        functools.partial(output_kernel, heads),
        w,
        (count,),
        inputs,
        [
            wide(features),
            wide(inner),
            wide(3 * inner),
            ((8, 3 * inner), F32, (8, 3 * inner), fixed(0, 0)),
        ],
        flops=2 * count * rows * features * (hidden + inner),
        nbytes=2 * features * (hidden + inner)
        + 2 * count * rows * (hidden + features + 8 * inner),
        name="outputs",
    )


def grad_kernel(pieces, count, at_left, adds, w, *refs):
    sides, swept = refs[: (1 if at_left else count)], refs[1 if at_left else count :]
    rest = swept[pieces:]
    swept = swept[:pieces]
    out = rest[-1]
    for i, side in enumerate(sides):
        value = 0.0
        start = 0
        for ref in swept:
            part = side[start : start + ref.shape[0], :]
            start += ref.shape[0]
            value = value + (mm(part, ref[...], TN) if at_left else mm(ref[...], part, TN))
        if adds:
            value = value + rest[0][i].astype(F32)
        out[i] = value.astype(BF16)


def weight_grad(line, w, at, at_left, side, swept, adds=None):
    tokens = side.shape[0]
    quarter = side.shape[1] // 4
    size = swept[0].shape[1]
    tile = min(256, quarter, size)
    heights = [piece.shape[0] for piece in swept]
    if at_left:
        split = quarter // tile
        grid = (2, split)
        inputs = [(side, (tokens, tile), lambda i, j, w: (0, w.either(at, i) * split + j))]
        inputs += [(piece, piece.shape, fixed(0, 0)) for piece in swept]
        out = ((2, quarter, size), BF16, (1, tile, size), lambda i, j, w: (i, j, 0))
    else:
        grid = (size // tile,)
        inputs = []
        for i in range(2):
            inputs.append((side, (tokens, quarter), lambda j, w, i=i: (0, w[at + i])))
        inputs += [(piece, (piece.shape[0], tile), lambda j, w: (0, j)) for piece in swept]
        out = ((2, size, quarter), BF16, (2, tile, quarter), lambda j, w: (0, j, 0))
    if adds is not None:
        inputs.append((adds, out[2], out[3]))
    return call(
        line,
        functools.partial(grad_kernel, len(swept), 2, at_left, adds is not None),
        w,
        grid,
        inputs,
        [out],
        flops=4 * tokens * quarter * size,
        nbytes=2 * tokens * (2 * quarter + size) + 8 * quarter * size,
        name="weight_grad",
    )[0]


def join(pieces):
    return [(piece, piece.shape, fixed(0, 0)) for piece in pieces]


def add_kernel(w, mine, *refs):
    *pieces, out = refs
    first = 0
    for piece in pieces:
        at = slice(first, first + piece.shape[0])
        out[at, :] = (mine[at, :].astype(F32) + piece[...].astype(F32)).astype(BF16)
        first += piece.shape[0]


def add(line, w, mine, pieces):
    shape = mine.shape[-2:]
    first = (mine, (None,) + shape, fixed(0, 0, 0)) if mine.ndim == 3 else (mine, shape, fixed(0, 0))
    return call(
        line,
        add_kernel,
        w,
        (1,),
        [first] + join(pieces),
        [(shape, BF16, shape, fixed(0, 0))],
        nbytes=6 * shape[0] * shape[1],
        name="add",
    )[0]


def first_half_kernel(w, mine, *refs):
    *pieces, wide, total = refs
    first = 0
    for piece in pieces:
        at = slice(first, first + piece.shape[0])
        value = (mine[at, :].astype(F32) + piece[...].astype(F32)).astype(BF16)
        total[at, :] = value
        wide[at, :] = value.astype(F32)
        first += piece.shape[0]


def first_half(line, w, at_left, mine, pieces):
    height, width = mine.shape
    if at_left:
        whole, place = (2 * height, width), lambda i, w: (w[KEEP], 0)
    else:
        whole, place = (height, 2 * width), lambda i, w: (0, w[KEEP])
    return call(
        line,
        first_half_kernel,
        w,
        (1,),
        [(mine, mine.shape, fixed(0, 0))] + join(pieces),
        [(whole, F32, mine.shape, place), (mine.shape, BF16, mine.shape, fixed(0, 0))],
        nbytes=10 * height * width,
        name="first_half",
    )


def second_half_kernel(w, held, other, wide):
    wide[...] = other[...].astype(F32)


def second_half(line, w, at_left, held, other):
    height, width = other.shape
    size = height // 2
    if at_left:
        whole, place = (2 * height, width), lambda i, w: (2 * w[SEND] + i, 0)
    else:
        whole, place = (height, 2 * width), lambda i, w: (i, w[SEND])
    return call(
        line,
        second_half_kernel,
        w,
        (2,),
        [(held, None, None), (other, (size, width), lambda i, w: (i, 0))],
        [(whole, F32, (size, width), place)],
        nbytes=6 * height * width,
        name="second_half",
        alias=0,
    )[0]


def gate_kernel(w, source, target):
    pass


def gate(line, w, array):
    return call(
        line,
        gate_kernel,
        w,
        (1,),
        [(array, None, None)],
        [(array.shape, array.dtype, None, None)],
        name="gate",
        alias=0,
    )[0]


def finish_kernel(count, more, w, kept, *refs):
    cols, refs = refs[:count], refs[count:]
    refs = refs[1:] if more else refs
    *bias, out = refs
    for i in range(count):
        value = kept[i].astype(F32) + cols[i][...].astype(F32)
        for ref in bias:
            value = value + ref[...]
        out[i] = value.astype(out.dtype)


def finish(line, w, place, held, kept, cols, bias, shape, dtype):
    _, rows, columns = shape
    count = len(cols)
    block = (count, rows, columns)
    inputs = [(kept, block, lambda i, w: (place, 0, w[TENSOR]))]
    inputs += [(part, (rows, columns), fixed(0, 0)) for part in cols]
    if held is not None:
        inputs.append((held, None, None))
    if bias is not None:
        inputs.append((bias, (1, columns), lambda i, w: (0, w[TENSOR])))
    return call(
        line,
        functools.partial(finish_kernel, count, held is not None),
        w,
        (1,),
        inputs,
        [(shape, dtype, block, fixed(place, 0, 0))],
        nbytes=8 * count * rows * columns,
        name="finish",
        alias=None if held is None else 1 + count,
    )[0]


def pick_kernel(joint, w, by_rows, by_columns, *targets):
    if joint:
        width = by_columns.shape[1]
        targets[0][:, : by_rows.shape[1]] = by_rows[...]
        targets[0][: by_columns.shape[0], targets[0].shape[1] - width :] = by_columns[...]
    else:
        targets[0][...] = by_rows[...]
        targets[1][...] = by_columns[...]


def pick(line, w, by_rows, by_columns, joint):
    height, width = by_rows.shape[0] // 2, by_columns.shape[1] // 2
    first = (height, by_rows.shape[1])
    second = (by_columns.shape[0], width)
    if joint:
        shapes = [(max(first[0], second[0]), pl.cdiv(first[1], width) * width + width)]
    else:
        shapes = [first, second]
    return call(
        line,
        functools.partial(pick_kernel, joint),
        w,
        (1,),
        [
            (by_rows, first, lambda i, w: (w[KEEP], 0)),
            (by_columns, second, lambda i, w: (0, w[KEEP])),
        ],
        [(shape, BF16, shape, fixed(0, 0)) for shape in shapes],
        nbytes=4 * (first[0] * first[1] + second[0] * second[1]),
        name="pick",
    )


def on_device(
    states,
    ln1_gain,
    ln1_bias,
    ln2_gain,
    ln2_bias,
    qkv_weight,
    qkv_bias,
    dense_weight,
    dense_bias,
    up_weight,
    up_bias,
    down_weight,
    out_bias,
    out_grad,
):
    micros, rows, features = states.shape
    heads = qkv_weight.shape[1] // (3 * HD)
    tokens = micros * rows
    n = lax.axis_size("seq")
    pairs = heads * micros // n
    straight = heads == n
    s = lax.axis_index("seq")
    core = s % 2
    d = lax.axis_index("dp")
    columns = features // lax.axis_size("tensor")
    first = lax.axis_index("tensor") * columns
    w = Places(straight)

    def absolute(own, other):
        return jnp.where(d == 1, jnp.concatenate([other, own]), jnp.concatenate([own, other]))

    x = states.reshape(tokens, features)
    cot = out_grad.reshape(tokens, features)

    small = (ln1_gain, ln1_bias, ln2_gain, ln2_bias, dense_bias, out_bias, qkv_bias, up_bias)
    small_got = swap(jnp.concatenate(small, 0), "dp", 1)
    line = Line(small_got)
    joint_half = swap(pick(line, w, qkv_weight, dense_weight, True)[0], "dp", 1)
    own, other = [], []
    place = 0
    for vector in small:
        own.append(vector.astype(F32))
        other.append(small_got[place : place + vector.shape[0]].astype(F32))
        place += vector.shape[0]
    half = features // 4
    vectors = jnp.stack(
        [
            jnp.concatenate(
                [
                    own[i],
                    lax.dynamic_slice_in_dim(other[i], core * half, half),
                    lax.dynamic_slice_in_dim(other[i], (1 - core) * half, half),
                ]
            )
            for i in range(4)
        ]
    )
    tables = turn_tables(n * rows)

    one, two, cot_total = norms(line, w, x, cot, vectors)
    halves = pick(line, w, up_weight, down_weight, False)
    up_got = swap(halves[0], "dp", 1)
    down_got = swap(halves[1], "dp", 1)
    got = gate(line, w, joint_half)
    joint = (got, swap(got, "seq", 1))
    height, width = qkv_weight.shape[0], qkv_weight.shape[1]
    qkv = [(qkv_weight, height, width, 0)] + [(half, height // 2, width, 0) for half in joint]
    height, width = dense_weight.shape[0], dense_weight.shape[1]
    dense = [(dense_weight, height, width, 0)] + [
        (half, height, width // 2, half.shape[1] // (width // 2) - 1) for half in joint
    ]
    qkv_shift = absolute(own[6], other[6])[None]
    up_shift = absolute(own[7], other[7])[None]
    bias = absolute(own[4] + own[5], other[4] + other[5])[None]
    payload, arrived, results, attended, qkv_grad = {}, {}, {}, {}, {}
    branch, back_cols, held = {}, {}, {"output": None, "input_grad": None}
    out_shape = (micros, rows, columns)
    totals = {"qkv": 0.0, "one": 0.0}
    sizes = GROUPS if micros == sum(GROUPS) else (1,) * micros
    starts = [sum(sizes[:i]) for i in range(len(sizes))]

    def project(group):
        found = projections(
            line, w, starts[group], sizes[group], rows, one, qkv, qkv_shift, tables, cot, dense
        )
        for i in range(sizes[group]):
            payload[starts[group] + i] = [(array, i) for array in found]

    def bring(m, *distances):
        for k in distances if straight else ():
            array, place = payload[m][k]
            arrived[m, k] = line.ride(array, "seq", k, place * rows, rows)

    def attend(m):
        if straight:
            blocks = [payload[m][0]] + [(arrived[m, k].result, 0) for k in range(1, n)]
            results[m] = list(attention(line, w, rows, blocks, tables))

    def give(m, *distances):
        for k in distances if straight else ():
            results[m][k] = line.ride(results[m][k], "seq", k)

    def attend_pairs():
        blocks = []
        for h in range(heads):
            for m in range(micros):
                array, place = payload[m][h]
                blocks.append(array[place * rows : (place + 1) * rows])
        stacked = jnp.stack(blocks).reshape(n, pairs, rows, 4 * HD)
        found = []
        for pair in range(pairs):
            sent = [
                lax.dynamic_index_in_dim(stacked[:, pair], s ^ k, 0, False) for k in range(n)
            ]
            sent = [sent[0]] + [swap(sent[k], "seq", k) for k in range(1, n)]
            back = attention(line, w, rows, [(array, 0) for array in sent], tables)
            found.append(jnp.stack([back[0]] + [swap(back[k], "seq", k) for k in range(1, n)]))
        for m in range(micros):
            results[m] = []
            for h in range(heads):
                device, pair = divmod(h * micros + m, pairs)
                results[m].append(
                    lax.dynamic_index_in_dim(found[pair], s ^ device, 0, False)
                )

    def both_cores(shard, got, by_rows):
        got = gate(line, w, got)
        return [(shard, *shard.shape, 0)] + [
            (half, *half.shape, 0) for half in (got, swap(got, "seq", 1))
        ]

    def put_out(m):
        if not straight and not results:
            attend_pairs()
        blocks = [block.result if isinstance(block, Ride) else block for block in results[m]]
        partial, attended[m], qkv_grad[m], total = outputs(
            line, w, m, rows, activated, down, dense, blocks
        )
        totals["qkv"] = totals["qkv"] + total
        branch[m] = lax.psum_scatter(partial, "tensor", scatter_dimension=1, tiled=True)

    def go_back(m):
        part, sums = backs(line, w, rows, m, 1, qkv_grad[m], qkv, x, vectors[0:1], part_two)
        totals["one"] = totals["one"] + sums
        back_cols[m] = lax.psum_scatter(part, "tensor", scatter_dimension=1, tiled=True)

    def finish_out(first, count):
        held["output"] = finish(
            line,
            w,
            first // count,
            held["output"],
            states,
            [branch[m] for m in range(first, first + count)],
            bias,
            out_shape,
            BF16,
        )

    def finish_back(first, count):
        held["input_grad"] = finish(
            line,
            w,
            first // count,
            held["input_grad"],
            out_grad,
            [back_cols[m] for m in range(first, first + count)],
            None,
            out_shape,
            F32,
        )

    def spread(vector, axis):
        size = -(-vector.size // 1024) * 1024
        vector = jnp.pad(vector, (0, size - vector.size)).reshape(8, size // 8)
        return [vector] + [line.ride(vector, axis, k) for k in range(1, lax.axis_size(axis))]

    def summed(parts, size):
        parts = landed(parts)
        while len(parts) > 1:
            parts = [one + two for one, two in zip(parts[::2], parts[1::2])]
        return parts[0].reshape(-1)[:size]

    grads, terms = {}, {
        "down": (False, cot, None),
        "up": (True, two, None),
        "dense": (False, cot, None),
        "qkv": (True, one, None),
    }
    steps = {}

    found, rides = {}, {}

    def send(name, swept):
        at_left, side, _ = terms[name]
        terms[name] = (at_left, side, swept)
        at = SEND if at_left else SEND_AT
        sent = weight_grad(line, w, at, at_left, side, swept)
        found[name] = sent.reshape(-1, sent.shape[2])

    def to_sibling(name):
        rides[name] = line.ride(found[name], "seq", 1)

    def keep(name):
        at_left, side, swept = terms[name]
        at = KEEP if at_left else KEEP_AT
        added = rides[name].result
        added = added.reshape(2, added.shape[0] // 2, added.shape[1])
        found[name] = weight_grad(line, w, at, at_left, side, swept, added)
        rides[name] = []

    def parts(name, count):
        height = found[name].shape[-2]
        size = height // PIECES[name]
        first = sum(ride.rows for ride in rides[name])
        return [(first + i * size, size) for i in range(count)]

    def over_y(name, count):
        for first, size in parts(name, count):
            rides[name].append(line.ride(found[name], "dp", 1, first, size, lead=1))

    def over_x(name, count):
        for first, size in parts(name, count):
            rides[name].append(line.ride(found[name], "seq", steps[name], first, size))

    def all_over_y(name):
        rides[name] = [swap(found[name][1], "dp", 1)]

    def all_over_x(name):
        rides[name] = [swap(found[name], "seq", steps[name])]

    def rest_over_x(name):
        for first, size in parts(name, PIECES[name] - len(rides[name])):
            rides[name].append(swap(found[name][first : first + size], "seq", steps[name]))

    def landed(parts):
        return [part.result if isinstance(part, Ride) else part for part in parts]

    def add_up(name):
        found[name] = add(line, w, found[name], landed(rides[name]))
        rides[name] = []
        steps[name] = 2
        while 2 * steps[name] < n:
            found[name] = add(
                line, w, found[name], [swap(found[name], "seq", steps[name])]
            )
            steps[name] *= 2
            rides[name] = []

    def mine_done(name):
        held[name], found[name] = first_half(
            line, w, terms[name][0], found[name], landed(rides[name])
        )

    def sibling_swap(name):
        rides[name] = swap(found[name], "seq", 1)

    def all_done(name):
        ride = rides[name]
        other = ride.result if isinstance(ride, Ride) else ride
        grads[name] = second_half(line, w, terms[name][0], held[name], other)

    def all_terms():
        one_sums, qkv_total = totals["one"], totals["qkv"]
        sums = jnp.concatenate([one_sums, two_sums], 0).reshape(4, 8, features).sum(1)
        norm_own, norm_oth = sums[:, : 2 * half], sums[:, 2 * half :]
        norm_oth = jnp.where(
            core == 1,
            jnp.concatenate([norm_oth[:, half:], norm_oth[:, :half]], 1),
            norm_oth,
        )
        norm_terms = jnp.where(
            d == 1,
            jnp.concatenate([norm_oth, norm_own], 1),
            jnp.concatenate([norm_own, norm_oth], 1),
        ).reshape(-1)
        rest = jnp.concatenate([qkv_total.sum(0), up_total.sum(0), cot_total.sum(0)])
        return norm_terms, rest

    project(0)
    bring(0, 1, 2, 3)
    project(1)
    bring(1, 1, 2)
    attend(0)
    up = both_cores(up_weight, up_got, True)
    bring(1, 3)
    give(0, 1, 2, 3)
    activated, slope = feed_up(line, w, rows, two, up, up_shift)
    down = both_cores(down_weight, down_got, False)
    bring(2, 1, 2)
    put_out(0)
    bring(2, 3)
    attend(1)
    give(1, 1, 2)
    send("down", [activated])
    give(1, 3)
    bring(3, 1, 2)
    to_sibling("down")
    pre_grad, up_total = pre_grads(line, w, rows, cot, down, slope)
    bring(3, 3)
    put_out(1)
    attend(2)
    give(2, 1, 2)
    keep("down")
    give(2, 3)
    over_y("down", 1)
    attend(3)
    give(3, 1, 2)
    over_y("down", 1)
    put_out(2)
    give(3, 3)
    over_y("down", 1)
    send("up", [pre_grad])
    over_y("down", 1)
    to_sibling("up")
    put_out(3)
    add_up("down")
    over_x("down", 1)
    keep("up")
    over_x("down", 3)
    over_y("up", 3)
    part_two, two_sums = backs(line, w, rows, 0, micros, pre_grad, up, x, vectors[2:3])
    over_y("up", 1)
    go_back(0)
    add_up("up")
    heads_out = [attended[m] for m in range(micros)]
    heads_grad = [qkv_grad[m] for m in range(micros)]
    over_x("up", 1)
    send("qkv", heads_grad)
    over_x("up", 1)
    to_sibling("qkv")
    send("dense", heads_out)
    over_x("up", 1)
    to_sibling("dense")
    go_back(1)
    over_x("up", 1)
    keep("qkv")
    over_y("qkv", 1)
    go_back(2)
    over_y("qkv", 1)
    keep("dense")
    add_up("qkv")
    over_x("qkv", 1)
    over_y("dense", 1)
    go_back(3)
    norm_terms, rest = all_terms()
    size = norm_terms.size
    spreads = spread(norm_terms, "tensor")
    add_up("dense")
    norm_terms = summed(spreads, size)
    vector = jnp.concatenate([norm_terms, rest])
    size = vector.size
    spreads = spread(vector, "seq")
    one_sums = gate(line, w, totals["one"])
    vector = summed(spreads, size)
    found["qkv"] = gate(line, w, found["qkv"])
    rest_over_x("qkv")
    mine_done("down")
    sibling_swap("down")
    mine_done("up")
    sibling_swap("up")
    finish_out(0, micros)
    mine_done("qkv")
    sibling_swap("qkv")
    rest_over_x("dense")
    spreads = spread(vector, "dp")
    one_sums = gate(line, w, one_sums)
    vector = summed(spreads, size)
    all_done("down")
    all_done("up")
    mine_done("dense")
    sibling_swap("dense")
    finish_back(0, micros - 1)
    all_done("qkv")
    all_done("dense")
    finish_back(micros - 1, 1)
    norm_terms = vector[: 4 * features].reshape(4, features)
    rest = vector[4 * features :]
    count = columns // 2
    norm_mine = lax.dynamic_slice_in_dim(norm_terms, first + d * count, count, 1)
    vector_grads = []
    place = 0
    for size in (3 * HD * heads, up_total.shape[1], features):
        vector_grads.append(lax.dynamic_slice_in_dim(rest, place + d * (size // 2), size // 2, 0))
        place += size

    return (
        held["output"],
        held["input_grad"],
        norm_mine[0],
        norm_mine[1],
        norm_mine[2],
        norm_mine[3],
        grads["qkv"],
        vector_grads[0],
        grads["dense"],
        vector_grads[2],
        grads["up"],
        vector_grads[1],
        grads["down"],
        vector_grads[2],
    )


def solution(mesh):
    placed = (
        P("dp", "seq", None),
        P("dp"),
        P("dp"),
        P("dp"),
        P("dp"),
        P("dp", "tensor"),
        P(("tensor", "dp")),
        P("tensor", "dp"),
        P("dp"),
        P("dp", "tensor"),
        P(("tensor", "dp")),
        P("tensor", "dp"),
        P("dp"),
        P("dp", "seq", None),
    )
    return jax.shard_map(
        on_device,
        mesh=mesh,
        in_specs=placed,
        out_specs=(
            P("dp", "seq", "tensor"),
            P("dp", "seq", "tensor"),
            P(("tensor", "dp")),
            P(("tensor", "dp")),
            P(("tensor", "dp")),
            P(("tensor", "dp")),
            P("dp", "tensor"),
            P(("tensor", "dp")),
            P("tensor", "dp"),
            P("dp"),
            P("dp", "tensor"),
            P(("tensor", "dp")),
            P("tensor", "dp"),
            P("dp"),
        ),
        check_vma=False,
    )
```

```python
import functools
import math

import jax
import jax.numpy as jnp
import numpy as np
from jax import lax
from jax.experimental import pallas as pl
from jax.experimental.pallas import tpu as pltpu
from jax.sharding import PartitionSpec as P

HD = 128
ROT = 32
HALF_ROT = ROT // 2
EPS = 1e-05
F32 = jnp.float32
BF16 = jnp.bfloat16
NN = (((1,), (0,)), ((), ()))
NT = (((1,), (1,)), ((), ()))
TN = (((0,), (0,)), ((), ()))
WEIGHT = 0.1
GROUPS = (1, 3)
PIECES = {"down": 4, "up": 4, "qkv": 2, "dense": 1}
VMEM_LIMIT = 60 * 1024 * 1024
KEEP, SEND, KEEP_AT, SEND_AT, SEQ, TENSOR, ORDER = 4, 6, 8, 10, 12, 13, 14


def bit(value, b):
    return lax.rem(lax.div(value, jnp.int32(1 << b)), jnp.int32(2))


def xor(value, other):
    value, other = jnp.int32(value), jnp.int32(other)
    return sum((1 << b) * lax.rem(bit(value, b) + bit(other, b), jnp.int32(2)) for b in range(4))


class Places:
    def __init__(self, straight):
        self.straight = straight

    def __getitem__(self, key):
        s = lax.axis_index("seq")
        if key == SEQ:
            return s
        if key == TENSOR:
            return lax.axis_index("tensor")
        if key >= ORDER:
            return self.head(key - ORDER)
        core = lax.rem(s, jnp.int32(2))
        d = lax.axis_index("dp")
        places = (2 * d, 2 * d + 1, 2 * (1 - d) + core, 2 * (1 - d) + 1 - core)
        if key < KEEP:
            return places[key]
        if key < KEEP_AT:
            return (core, 2, 1 - core, 3)[key - KEEP]
        return (2 * d + core, places[2], 2 * d + 1 - core, places[3])[key - KEEP_AT]

    def head(self, slot):
        return xor(lax.axis_index("seq"), slot) if self.straight else slot

    def either(self, key, i):
        return (1 - i) * self[key] + i * self[key + 1]


class Ride:
    def __init__(self, source, axis, distance, first=0, rows=None, lead=None):
        self.source, self.axis, self.distance = source, axis, distance
        self.first, self.lead = first, lead
        self.rows = source.shape[-2] - first if rows is None else rows
        self.result = None

    @property
    def shape(self):
        return (self.rows, self.source.shape[-1])

    def target(self):
        return {self.axis: xor(lax.axis_index(self.axis), self.distance)}

    def copy(self, source, target, sent, got):
        at = pl.ds(self.first, self.rows)
        return pltpu.make_async_remote_copy(
            src_ref=source.at[at] if self.lead is None else source.at[self.lead, at],
            dst_ref=target,
            send_sem=sent,
            recv_sem=got,
            device_id=self.target(),
            device_id_type=pl.DeviceIdType.MESH,
        )


class Line:
    def __init__(self, first):
        self.last = [first]
        self.rides = []
        self.count = 0

    def ride(self, *args, **kwargs):
        self.rides.append(Ride(*args, **kwargs))
        return self.rides[-1]


def mm(a, b, dims=NN):
    return lax.dot_general(a, b, dims, preferred_element_type=F32)


def swap(block, axis, distance):
    return lax.ppermute(block, axis, [(i, i ^ distance) for i in range(lax.axis_size(axis))])


def spec(block, index):
    if block is None:
        return pl.BlockSpec(memory_space=pl.ANY)
    return pl.BlockSpec(block, index)


def call(line, kernel, w, grid, inputs, outputs, scratch=(), flops=0, nbytes=0, name=None, alias=None):
    before = [token for token in line.last if alias is None or token is not inputs[alias][0]]
    rides, line.rides = line.rides, []
    skip = len(before) + len(rides)
    ends = len(inputs) + len(outputs)
    steps = 1
    for size in grid:
        steps *= size
    staged = [i for i in range(len(inputs)) if rides and steps == 1 and inputs[i][1] is not None]

    def stage(ref, block, index):
        cut = []
        for size, place in zip(block, index(*[0] * len(grid), w)):
            if size is None:
                cut.append(place)
            elif isinstance(place, int):
                cut.append(slice(place * size, (place + 1) * size))
            else:
                cut.append(pl.ds(pl.multiple_of(place * size, size), size))
        return ref.at[tuple(cut)]

    def at(index):
        return None if index is None else lambda *steps: index(*steps, w)

    def on_step(last, work):
        chosen = True
        for axis, size in enumerate(grid):
            if size > 1:
                step = pl.program_id(axis)
                chosen = jnp.logical_and(chosen, step == (size - 1 if last else 0))
        if chosen is True:
            work()
        else:
            pl.when(chosen)(work)

    def body(*refs):
        sources = refs[len(before) : skip]
        own = refs[skip : skip + ends]
        targets = refs[skip + ends : skip + ends + len(rides)]
        rest = refs[skip + ends + len(rides) :]
        if not rides:
            kernel(w, *own, *rest)
            return
        *rest, sent, got = rest
        own = list(own)
        loads = []
        if staged:
            *rest, loaded = rest
            buffers = rest[len(rest) - len(staged) :]
            rest = rest[: len(rest) - len(staged)]
            for k, i in enumerate(staged):
                part = stage(own[i], *inputs[i][1:])
                loads.append(pltpu.make_async_copy(part, buffers[k], loaded.at[k]))
                own[i] = buffers[k]
        copies = lambda: [
            ride.copy(source, target, sent.at[i], got.at[i])
            for i, (ride, source, target) in enumerate(zip(rides, sources, targets))
        ]

        def start():
            barrier = pltpu.get_barrier_semaphore()
            partners = {(ride.axis, ride.distance): ride for ride in rides}
            for ride in partners.values():
                pl.semaphore_signal(
                    barrier, inc=1, device_id=ride.target(), device_id_type=pl.DeviceIdType.MESH
                )
            pl.semaphore_wait(barrier, len(partners))
            for copy in copies():
                copy.start()

        def wait():
            for copy in copies():
                copy.wait()

        for load in loads:
            load.start()
        on_step(False, start)
        for load in loads:
            load.wait()
        kernel(w, *own, *rest)
        on_step(True, wait)

    params = dict(
        vmem_limit_bytes=VMEM_LIMIT, dimension_semantics=("arbitrary",) * len(grid)
    )
    sems = []
    if rides:
        params.update(collective_id=line.count, has_side_effects=True)
        line.count += 1
        for i in staged:
            array, block, _ = inputs[i]
            shape = tuple(size for size in block if size is not None)
            sems.append(pltpu.VMEM(shape, array.dtype))
        if staged:
            sems.append(pltpu.SemaphoreType.DMA((len(staged),)))
        sems += [pltpu.SemaphoreType.DMA((len(rides),))] * 2
    anywhere = pl.BlockSpec(memory_space=pl.ANY)
    results = pl.pallas_call(
        body,
        grid=grid,
        in_specs=[anywhere] * skip
        + [
            anywhere if i in staged else spec(block, at(index))
            for i, (_, block, index) in enumerate(inputs)
        ],
        out_specs=[spec(block, at(index)) for _, _, block, index in outputs]
        + [anywhere] * len(rides),
        scratch_shapes=list(scratch) + sems,
        out_shape=[jax.ShapeDtypeStruct(shape, dtype) for shape, dtype, _, _ in outputs]
        + [jax.ShapeDtypeStruct(ride.shape, ride.source.dtype) for ride in rides],
        compiler_params=pltpu.CompilerParams(**params),
        cost_estimate=pl.CostEstimate(
            flops=int(flops * WEIGHT), bytes_accessed=int(nbytes * WEIGHT), transcendentals=0
        ),
        input_output_aliases={} if alias is None else {skip + alias: 0},
        name=name,
    )(*before, *[ride.source for ride in rides], *[array for array, _, _ in inputs])
    for ride, result in zip(rides, results[len(outputs) :]):
        ride.result = result
    results = results[: len(outputs)]
    line.last = [results[-1]]
    return results


def fixed(*index):
    return lambda *_: index


def groups(values):
    return jnp.sum(values.reshape(values.shape[0] // 8, 8, values.shape[1]), 0)


def columns_at(w, b, size):
    return pl.ds(pl.multiple_of(w[b] * size, size), size)


def norm_kernel(w, x, cot, vectors, one, two, total):
    quarter = x.shape[1] // 4

    @pl.when(pl.program_id(0) == 0)
    def _():
        total[...] = jnp.zeros_like(total)

    values = x[...].astype(F32)
    mean = jnp.mean(values, -1, keepdims=True)
    center = values - mean
    inverse = lax.rsqrt(jnp.mean(center * center, -1, keepdims=True) + EPS)
    for b in range(4):
        at = slice(b * quarter, (b + 1) * quarter)
        unit = (x[:, columns_at(w, b, quarter)].astype(F32) - mean) * inverse
        one[:, at] = (unit * vectors[0:1, at] + vectors[1:2, at]).astype(BF16)
        two[:, at] = (unit * vectors[2:3, at] + vectors[3:4, at]).astype(BF16)
    total[...] += groups(cot[...].astype(F32))


def norms(line, w, x, cot, vectors):
    tokens, features = x.shape
    size = min(256, tokens)
    row = (size, features)
    along = lambda i, w: (i, 0)
    return call(
        line,
        norm_kernel,
        w,
        (tokens // size,),
        [(x, row, along), (cot, row, along), (vectors, vectors.shape, fixed(0, 0))],
        [
            ((tokens, features), BF16, row, along),
            ((tokens, features), BF16, row, along),
            ((8, features), F32, (8, features), fixed(0, 0)),
        ],
        flops=30 * tokens * features,
        nbytes=8 * tokens * features,
        name="norms",
    )


def turned(values):
    lane = lax.broadcasted_iota(jnp.int32, values.shape, 1)
    return jnp.where(
        lane < HALF_ROT, pltpu.roll(values, HD - HALF_ROT, 1), pltpu.roll(values, HALF_ROT, 1)
    )


def turn_tables(length):
    frequency = 10000.0 ** (-np.arange(HALF_ROT) * 2.0 / ROT)
    angles = np.arange(length)[:, None] * frequency[None, :]
    cosine = np.ones((length, HD), np.float32)
    sine = np.zeros((length, HD), np.float32)
    cosine[:, :ROT] = np.tile(np.cos(angles), (1, 2))
    sine[:, :HALF_ROT] = np.sin(angles)
    sine[:, HALF_ROT:ROT] = -np.sin(angles)
    return jnp.asarray(cosine), jnp.asarray(sine)


def project_kernel(
    slots, w, one, q0, q1, q2, bias, cosine, sine, c0, c1, c2, c3, d0, d1, d2, *outs
):
    step = pl.program_id(0)
    quarter = c0.shape[1]
    u = (
        mm(one[:, : 2 * quarter], q0[...])
        + mm(one[:, 2 * quarter : 3 * quarter], q1[...])
        + mm(one[:, 3 * quarter :], q2[...])
        + bias[...]
    )
    g = (
        mm(c0[...], d0[:, :quarter], NT)
        + mm(c1[...], d0[:, quarter:], NT)
        + mm(c2[...], d1[...], NT)
        + mm(c3[...], d2[...], NT)
    )
    cos, sin = cosine[...], sine[...]
    rows = u.shape[0]
    at_rows = pl.ds(pl.multiple_of(pl.program_id(1) * rows, rows), rows)
    flip = lax.rem(w.head(2 * step), jnp.int32(2))
    blocks = []
    for head in range(2):
        at = head * 3 * HD
        query, key = u[:, at : at + HD], u[:, at + HD : at + 2 * HD]
        blocks.append(
            jnp.concatenate(
                [
                    (query * cos - turned(query) * sin).astype(BF16),
                    (key * cos - turned(key) * sin).astype(BF16),
                    u[:, at + 2 * HD : at + 3 * HD].astype(BF16),
                    g[:, head * HD : (head + 1) * HD].astype(BF16),
                ],
                1,
            )
        )
    for pair in range(slots // 2):
        for turn in range(2):

            @pl.when((step == pair) & (flip == turn))
            def _():
                outs[2 * pair + turn][at_rows, :] = blocks[0]
                outs[2 * pair + 1 - turn][at_rows, :] = blocks[1]


def projections(line, w, first, count, rows, one, qkv, bias, tables, cot, dense):
    features = one.shape[1]
    quarter = features // 4
    heads = dense[0][1] // HD
    wide = 6 * HD
    pair = lambda i, m, w: (0, lax.div(w.head(2 * i), jnp.int32(2)))
    own = lambda i, m, w: (w[SEQ], 0)
    inputs = [(one, (rows, features), lambda i, m, w: (m + first, 0))]
    inputs += [(array, (height, wide), pair) for array, height, _, _ in qkv]
    inputs += [(bias, (1, wide), pair)]
    inputs += [(table, (rows, HD), own) for table in tables]
    for b in range(4):
        inputs.append((cot, (rows, quarter), lambda i, m, w, b=b: (m + first, w[b])))
    for array, _, width, place in dense:
        inputs.append(
            (array, (2 * HD, width), lambda i, m, w, b=place: (lax.div(w.head(2 * i), jnp.int32(2)), b))
        )
    return call(
        line,
        functools.partial(project_kernel, heads),
        w,
        (heads // 2, count),
        inputs,
        [((count * rows, 4 * HD), BF16, (count * rows, 4 * HD), fixed(0, 0))] * heads,
        flops=2 * count * rows * features * heads * 4 * HD,
        nbytes=2 * features * (heads * 4 * HD + 2 * count * rows) + 8 * count * rows * heads * HD,
        name="projections",
    )


def attention_kernel(parts, scale, qsize, ksize, w, *refs):
    ins = refs[:parts]
    cos_ref, sin_ref = refs[parts : parts + 2]
    outs = refs[parts + 2 : 2 * parts + 2]
    q_s, k_s, v_s, g_s, kt_s, vt_s, prob_s, dk_s, dv_s, o_s, dq_s = refs[2 * parts + 2 :]
    rows = ins[0].shape[0]
    length = parts * rows
    places = []
    for k in range(parts):
        at = pl.ds(pl.multiple_of(xor(w[SEQ], k) * rows, rows), rows)
        places.append(at)
        q_s[at, :] = ins[k][:, 0:HD]
        k_s[at, :] = ins[k][:, HD : 2 * HD]
        v_s[at, :] = ins[k][:, 2 * HD : 3 * HD]
        g_s[at, :] = ins[k][:, 3 * HD : 4 * HD]
    for j in range(length // ksize):
        at = slice(j * ksize, (j + 1) * ksize)
        kt_s[:, at] = k_s[at, :].T
        vt_s[:, at] = v_s[at, :].T
    factor = scale * math.log2(math.e)
    for i in range(length // qsize):
        qat = slice(i * qsize, (i + 1) * qsize)
        q = q_s[qat, :]
        g = g_s[qat, :]
        chunks = []
        for first in range(0, (i + 1) * qsize, ksize):
            chunks.append((first, min(ksize, (i + 1) * qsize - first)))
        top = jnp.full((8, qsize), -1e30, F32)
        for first, size in chunks:
            s = mm(k_s[first : first + size, :], q, NT)
            if first + size > i * qsize:
                key = lax.broadcasted_iota(jnp.int32, s.shape, 0) + (first - i * qsize)
                query = lax.broadcasted_iota(jnp.int32, s.shape, 1)
                s = jnp.where(key <= query, s, -1e30)
            prob_s[first : first + size, :] = s
            top = jnp.maximum(top, jnp.max(s.reshape(size // 8, 8, qsize), 0))
        top = jnp.max(top, 0, keepdims=True)
        total = jnp.zeros((8, qsize), F32)
        acc = jnp.zeros((HD, qsize), F32)
        for first, size in chunks:
            e = jnp.exp2((prob_s[first : first + size, :] - top) * factor)
            prob_s[first : first + size, :] = e
            total = total + jnp.sum(e.reshape(size // 8, 8, qsize), 0)
            acc = acc + mm(vt_s[:, first : first + size], e.astype(BF16))
        inverse = 1.0 / jnp.sum(total, 0, keepdims=True)
        acc = acc * inverse
        delta = jnp.sum(acc * g.T.astype(F32), 0, keepdims=True)
        o_s[qat, :] = acc.T.astype(BF16)
        dqt = jnp.zeros((HD, qsize), F32)
        for first, size in chunks:
            at = slice(first, first + size)
            p = prob_s[at, :] * inverse
            ds = (p * (mm(v_s[at, :], g, NT) - delta)).astype(BF16)
            dv = mm(p.astype(BF16), g)
            dk = mm(ds, q)
            low = max(0, min(size, i * qsize - first))
            if low:
                old = slice(first, first + low)
                dv_s[old, :] += dv[:low]
                dk_s[old, :] += dk[:low]
            if low < size:
                new = slice(first + low, first + size)
                dv_s[new, :] = dv[low:]
                dk_s[new, :] = dk[low:]
            dqt = dqt + mm(kt_s[:, at], ds)
        dq_s[qat, :] = dqt.T
    for k in range(parts):
        at = places[k]
        cosine = cos_ref[at, :]
        sine = sin_ref[at, :]
        dq, dk = dq_s[at, :], dk_s[at, :]
        outs[k][:, 0:HD] = o_s[at, :]
        outs[k][:, HD : 2 * HD] = ((dq * cosine + turned(dq) * sine) * scale).astype(BF16)
        outs[k][:, 2 * HD : 3 * HD] = ((dk * cosine + turned(dk) * sine) * scale).astype(BF16)
        outs[k][:, 3 * HD : 4 * HD] = dv_s[at, :].astype(BF16)


def attention(line, w, rows, blocks, tables, qsize=512, ksize=512):
    parts = len(blocks)
    width = blocks[0][0].shape[1]
    count = 1
    length = parts * rows
    qsize, ksize = min(qsize, rows), min(ksize, rows)
    block = ((rows, width), lambda m, w: (m, 0))
    return call(
        line,
        functools.partial(attention_kernel, parts, HD ** (-0.5), qsize, ksize),
        w,
        (count,),
        [(array, (rows, width), fixed(place, 0)) for array, place in blocks] + [(table, (length, HD), fixed(0, 0)) for table in tables],
        [((count * rows, width), BF16, *block)] * parts,
        scratch=[pltpu.VMEM((length, HD), BF16)] * 4
        + [pltpu.VMEM((HD, length), BF16)] * 2
        + [pltpu.VMEM((length, qsize), F32)]
        + [pltpu.VMEM((length, HD), F32)] * 2
        + [pltpu.VMEM((length, HD), BF16)]
        + [pltpu.VMEM((length, HD), F32)],
        flops=14 * count * length * length * HD,
        nbytes=4 * count * length * width + 8 * length * HD,
        name="attention",
    )


def up_kernel(w, two, u0, u1, u2, bias, activated, slope):
    quarter = u1.shape[0]
    pre = (
        mm(two[:, : 2 * quarter], u0[...])
        + mm(two[:, 2 * quarter : 3 * quarter], u1[...])
        + mm(two[:, 3 * quarter :], u2[...])
        + bias[...]
    )
    tail = 0.5 + 0.5 * lax.erf(pre * math.sqrt(0.5))
    activated[...] = (pre * tail).astype(BF16)
    bell = jnp.exp2(pre * pre * (-0.5 * math.log2(math.e))) * (1.0 / math.sqrt(2.0 * math.pi))
    slope[...] = (tail + pre * bell).astype(BF16)


def feed_up(line, w, rows, two, up, bias):
    tokens, features = two.shape
    hidden = up[0][2]
    wide = min(1024, hidden)
    column = lambda j, m, w: (0, j)
    out = ((tokens, hidden), BF16, (rows, wide), lambda j, m, w: (m, j))
    return call(
        line,
        up_kernel,
        w,
        (hidden // wide, tokens // rows),
        [(two, (rows, features), lambda j, m, w: (m, 0))]
        + [(array, (height, wide), column) for array, height, _, _ in up]
        + [(bias, (1, wide), column)],
        [out, out],
        flops=2 * tokens * features * hidden,
        nbytes=2 * features * (hidden + 2 * tokens) + 4 * tokens * hidden,
        name="feed_up",
    )


def pre_grad_kernel(w, c0, c1, c2, c3, n0, n1, n2, slope, out, total):
    quarter = c0.shape[1]
    act_grad = (
        mm(c0[...], n0[:, :quarter], NT)
        + mm(c1[...], n0[:, quarter:], NT)
        + mm(c2[...], n1[...], NT)
        + mm(c3[...], n2[...], NT)
    )
    grad = (act_grad * slope[...].astype(F32)).astype(BF16)
    out[...] = grad

    @pl.when(pl.program_id(1) == 0)
    def _():
        total[...] = jnp.zeros_like(total)

    total[...] += groups(grad.astype(F32))


def pre_grads(line, w, rows, cot, down, slope):
    tokens, features = cot.shape
    hidden = slope.shape[1]
    wide = min(1024, hidden)
    quarter = features // 4
    inputs = []
    for b in range(4):
        inputs.append((cot, (rows, quarter), lambda j, m, w, b=b: (m, w[b])))
    inputs += [(array, (wide, width), lambda j, m, w: (j, 0)) for array, _, width, _ in down]
    tile = ((rows, wide), lambda j, m, w: (m, j))
    return call(
        line,
        pre_grad_kernel,
        w,
        (hidden // wide, tokens // rows),
        inputs + [(slope, *tile)],
        [
            ((tokens, hidden), BF16, *tile),
            ((8, hidden), F32, (8, wide), lambda j, m, w: (0, j)),
        ],
        flops=2 * tokens * features * hidden,
        nbytes=2 * features * (hidden + 2 * tokens) + 4 * tokens * hidden,
        name="pre_grads",
    )


def back_kernel(more, w, grad, w0, w1, w2, x, gain, *refs):
    if more:
        before, out, sums, e = refs
    else:
        out, sums, e = refs
    features = x.shape[1]
    quarter = features // 4
    rows = x.shape[0]

    @pl.when(pl.program_id(0) == 0)
    def _():
        sums[...] = jnp.zeros_like(sums)

    e[:, : 2 * quarter] = mm(grad[...], w0[...], NT)
    e[:, 2 * quarter : 3 * quarter] = mm(grad[...], w1[...], NT)
    e[:, 3 * quarter :] = mm(grad[...], w2[...], NT)
    values = x[...].astype(F32)
    mean = jnp.mean(values, -1, keepdims=True)
    center = values - mean
    inverse = lax.rsqrt(jnp.mean(center * center, -1, keepdims=True) + EPS)
    middle = jnp.zeros((rows, 1), F32)
    slant = jnp.zeros((rows, 1), F32)
    for b in range(4):
        at = slice(b * quarter, (b + 1) * quarter)
        unit = (x[:, columns_at(w, b, quarter)].astype(F32) - mean) * inverse
        found = e[:, at]
        sums[0:8, at] += groups(found * unit)
        sums[8:16, at] += groups(found)
        scaled = found * gain[:, at]
        middle += jnp.sum(scaled, -1, keepdims=True)
        slant += jnp.sum(scaled * unit, -1, keepdims=True)
    middle = middle * (1.0 / features)
    slant = slant * (1.0 / features)
    for b in range(4):
        at = slice(b * quarter, (b + 1) * quarter)
        place = columns_at(w, b, quarter)
        unit = (x[:, place].astype(F32) - mean) * inverse
        part = inverse * (e[:, at] * gain[:, at] - middle - unit * slant)
        if more:
            part = part + before[:, place].astype(F32)
        out[:, place] = part.astype(BF16)


def backs(line, w, rows, first, count, grad, weight, x, gain, before=None):
    features = x.shape[1]
    width = grad.shape[1]
    row = (rows, features)
    shift = lambda m, w: (m + first, 0)
    along = lambda m, w: (m, 0)
    inputs = [(grad, (rows, width), along)]
    inputs += [(array, (height, wide), fixed(0, place)) for array, height, wide, place in weight]
    inputs += [(x, row, shift), (gain, gain.shape, fixed(0, 0))]
    if before is not None:
        inputs.append((before, row, shift))
    return call(
        line,
        functools.partial(back_kernel, before is not None),
        w,
        (count,),
        inputs,
        [
            ((count * rows, features), BF16, row, along),
            ((16, features), F32, (16, features), fixed(0, 0)),
        ],
        scratch=[pltpu.VMEM(row, F32)],
        flops=2 * count * rows * features * width,
        nbytes=2 * (features * width + count * rows * (width + 3 * features)),
        name="backs",
    )


def output_kernel(heads, w, act, n0, n1, n2, d0, d1, d2, *refs):
    blocks = refs[:heads]
    part, attended, qkv_grad, total = refs[heads:]
    quarter = n1.shape[1]

    @pl.when(pl.program_id(0) == 0)
    def _():
        total[...] = jnp.zeros_like(total)

    for i in range(heads):
        head = w[ORDER + i]
        attended[:, pl.ds(pl.multiple_of(head * HD, HD), HD)] = blocks[i][:, :HD]
        at = pl.ds(pl.multiple_of(head * 3 * HD, HD), 3 * HD)
        qkv_grad[:, at] = blocks[i][:, HD:]
        total[:, at] += groups(blocks[i][:, HD:].astype(F32))
    pieces = [(n0, d0, 0), (n0, d0, 1), (n1, d1, 0), (n2, d2, 0)]
    for b, (down, dense, half) in enumerate(pieces):
        at = slice(half * quarter, (half + 1) * quarter)
        part[:, columns_at(w, b, quarter)] = (
            mm(attended[...], dense[:, at]) + mm(act[...], down[:, at])
        ).astype(BF16)


def outputs(line, w, first, rows, act, down, dense, blocks):
    hidden = act.shape[1]
    inner = dense[0][1]
    features = 2 * dense[0][2]
    heads = len(blocks)
    count = 1
    along = lambda m, w: (m, 0)
    inputs = [(act, (rows, hidden), lambda m, w: (m + first, 0))]
    for array, height, width, place in (*down, *dense):
        inputs.append((array, (height, width), fixed(0, place)))
    inputs += [(block, block.shape, fixed(0, 0)) for block in blocks]
    wide = lambda size: ((count * rows, size), BF16, (rows, size), along)
    return call(
        line,
        functools.partial(output_kernel, heads),
        w,
        (count,),
        inputs,
        [
            wide(features),
            wide(inner),
            wide(3 * inner),
            ((8, 3 * inner), F32, (8, 3 * inner), fixed(0, 0)),
        ],
        flops=2 * count * rows * features * (hidden + inner),
        nbytes=2 * features * (hidden + inner)
        + 2 * count * rows * (hidden + features + 8 * inner),
        name="outputs",
    )


def grad_kernel(pieces, count, at_left, adds, w, *refs):
    sides, swept = refs[: (1 if at_left else count)], refs[1 if at_left else count :]
    rest = swept[pieces:]
    swept = swept[:pieces]
    out = rest[-1]
    for i, side in enumerate(sides):
        value = 0.0
        start = 0
        for ref in swept:
            part = side[start : start + ref.shape[0], :]
            start += ref.shape[0]
            value = value + (mm(part, ref[...], TN) if at_left else mm(ref[...], part, TN))
        if adds:
            value = value + rest[0][i].astype(F32)
        out[i] = value.astype(BF16)


def weight_grad(line, w, at, at_left, side, swept, adds=None):
    tokens = side.shape[0]
    quarter = side.shape[1] // 4
    size = swept[0].shape[1]
    tile = min(256, quarter, size)
    heights = [piece.shape[0] for piece in swept]
    if at_left:
        split = quarter // tile
        grid = (2, split)
        inputs = [(side, (tokens, tile), lambda i, j, w: (0, w.either(at, i) * split + j))]
        inputs += [(piece, piece.shape, fixed(0, 0)) for piece in swept]
        out = ((2, quarter, size), BF16, (1, tile, size), lambda i, j, w: (i, j, 0))
    else:
        grid = (size // tile,)
        inputs = []
        for i in range(2):
            inputs.append((side, (tokens, quarter), lambda j, w, i=i: (0, w[at + i])))
        inputs += [(piece, (piece.shape[0], tile), lambda j, w: (0, j)) for piece in swept]
        out = ((2, size, quarter), BF16, (2, tile, quarter), lambda j, w: (0, j, 0))
    if adds is not None:
        inputs.append((adds, out[2], out[3]))
    return call(
        line,
        functools.partial(grad_kernel, len(swept), 2, at_left, adds is not None),
        w,
        grid,
        inputs,
        [out],
        flops=4 * tokens * quarter * size,
        nbytes=2 * tokens * (2 * quarter + size) + 8 * quarter * size,
        name="weight_grad",
    )[0]


def join(pieces):
    return [(piece, piece.shape, fixed(0, 0)) for piece in pieces]


def add_kernel(w, mine, *refs):
    *pieces, out = refs
    first = 0
    for piece in pieces:
        at = slice(first, first + piece.shape[0])
        out[at, :] = (mine[at, :].astype(F32) + piece[...].astype(F32)).astype(BF16)
        first += piece.shape[0]


def add(line, w, mine, pieces):
    shape = mine.shape[-2:]
    first = (mine, (None,) + shape, fixed(0, 0, 0)) if mine.ndim == 3 else (mine, shape, fixed(0, 0))
    return call(
        line,
        add_kernel,
        w,
        (1,),
        [first] + join(pieces),
        [(shape, BF16, shape, fixed(0, 0))],
        nbytes=6 * shape[0] * shape[1],
        name="add",
    )[0]


def first_half_kernel(w, mine, *refs):
    *pieces, wide, total = refs
    first = 0
    for piece in pieces:
        at = slice(first, first + piece.shape[0])
        value = (mine[at, :].astype(F32) + piece[...].astype(F32)).astype(BF16)
        total[at, :] = value
        wide[at, :] = value.astype(F32)
        first += piece.shape[0]


def first_half(line, w, at_left, mine, pieces):
    height, width = mine.shape
    if at_left:
        whole, place = (2 * height, width), lambda i, w: (w[KEEP], 0)
    else:
        whole, place = (height, 2 * width), lambda i, w: (0, w[KEEP])
    return call(
        line,
        first_half_kernel,
        w,
        (1,),
        [(mine, mine.shape, fixed(0, 0))] + join(pieces),
        [(whole, F32, mine.shape, place), (mine.shape, BF16, mine.shape, fixed(0, 0))],
        nbytes=10 * height * width,
        name="first_half",
    )


def second_half_kernel(w, held, other, wide):
    wide[...] = other[...].astype(F32)


def second_half(line, w, at_left, held, other):
    height, width = other.shape
    size = height // 2
    if at_left:
        whole, place = (2 * height, width), lambda i, w: (2 * w[SEND] + i, 0)
    else:
        whole, place = (height, 2 * width), lambda i, w: (i, w[SEND])
    return call(
        line,
        second_half_kernel,
        w,
        (2,),
        [(held, None, None), (other, (size, width), lambda i, w: (i, 0))],
        [(whole, F32, (size, width), place)],
        nbytes=6 * height * width,
        name="second_half",
        alias=0,
    )[0]


def gate_kernel(w, source, target):
    pass


def gate(line, w, array):
    return call(
        line,
        gate_kernel,
        w,
        (1,),
        [(array, None, None)],
        [(array.shape, array.dtype, None, None)],
        name="gate",
        alias=0,
    )[0]


def finish_kernel(count, more, w, kept, *refs):
    cols, refs = refs[:count], refs[count:]
    refs = refs[1:] if more else refs
    *bias, out = refs
    for i in range(count):
        value = kept[i].astype(F32) + cols[i][...].astype(F32)
        for ref in bias:
            value = value + ref[...]
        out[i] = value.astype(out.dtype)


def finish(line, w, place, held, kept, cols, bias, shape, dtype):
    _, rows, columns = shape
    count = len(cols)
    block = (count, rows, columns)
    inputs = [(kept, block, lambda i, w: (place, 0, w[TENSOR]))]
    inputs += [(part, (rows, columns), fixed(0, 0)) for part in cols]
    if held is not None:
        inputs.append((held, None, None))
    if bias is not None:
        inputs.append((bias, (1, columns), lambda i, w: (0, w[TENSOR])))
    return call(
        line,
        functools.partial(finish_kernel, count, held is not None),
        w,
        (1,),
        inputs,
        [(shape, dtype, block, fixed(place, 0, 0))],
        nbytes=8 * count * rows * columns,
        name="finish",
        alias=None if held is None else 1 + count,
    )[0]


def pick_kernel(joint, w, by_rows, by_columns, *targets):
    if joint:
        width = by_columns.shape[1]
        targets[0][:, : by_rows.shape[1]] = by_rows[...]
        targets[0][: by_columns.shape[0], targets[0].shape[1] - width :] = by_columns[...]
    else:
        targets[0][...] = by_rows[...]
        targets[1][...] = by_columns[...]


def pick(line, w, by_rows, by_columns, joint):
    height, width = by_rows.shape[0] // 2, by_columns.shape[1] // 2
    first = (height, by_rows.shape[1])
    second = (by_columns.shape[0], width)
    if joint:
        shapes = [(max(first[0], second[0]), pl.cdiv(first[1], width) * width + width)]
    else:
        shapes = [first, second]
    return call(
        line,
        functools.partial(pick_kernel, joint),
        w,
        (1,),
        [
            (by_rows, first, lambda i, w: (w[KEEP], 0)),
            (by_columns, second, lambda i, w: (0, w[KEEP])),
        ],
        [(shape, BF16, shape, fixed(0, 0)) for shape in shapes],
        nbytes=4 * (first[0] * first[1] + second[0] * second[1]),
        name="pick",
    )


def on_device(
    states,
    ln1_gain,
    ln1_bias,
    ln2_gain,
    ln2_bias,
    qkv_weight,
    qkv_bias,
    dense_weight,
    dense_bias,
    up_weight,
    up_bias,
    down_weight,
    out_bias,
    out_grad,
):
    micros, rows, features = states.shape
    heads = qkv_weight.shape[1] // (3 * HD)
    tokens = micros * rows
    n = lax.axis_size("seq")
    pairs = heads * micros // n
    straight = heads == n
    s = lax.axis_index("seq")
    core = s % 2
    d = lax.axis_index("dp")
    columns = features // lax.axis_size("tensor")
    first = lax.axis_index("tensor") * columns
    w = Places(straight)

    def absolute(own, other):
        return jnp.where(d == 1, jnp.concatenate([other, own]), jnp.concatenate([own, other]))

    x = states.reshape(tokens, features)
    cot = out_grad.reshape(tokens, features)

    small = (ln1_gain, ln1_bias, ln2_gain, ln2_bias, dense_bias, out_bias, qkv_bias, up_bias)
    small_got = swap(jnp.concatenate(small, 0), "dp", 1)
    line = Line(qkv_bias)
    joint_half = swap(pick(line, w, qkv_weight, dense_weight, True)[0], "dp", 1)
    own, other = [], []
    place = 0
    for vector in small:
        own.append(vector.astype(F32))
        other.append(small_got[place : place + vector.shape[0]].astype(F32))
        place += vector.shape[0]
    half = features // 4
    vectors = jnp.stack(
        [
            jnp.concatenate(
                [
                    own[i],
                    lax.dynamic_slice_in_dim(other[i], core * half, half),
                    lax.dynamic_slice_in_dim(other[i], (1 - core) * half, half),
                ]
            )
            for i in range(4)
        ]
    )
    tables = turn_tables(n * rows)

    one, two, cot_total = norms(line, w, x, cot, vectors)
    halves = pick(line, w, up_weight, down_weight, False)
    up_got = swap(halves[0], "dp", 1)
    down_got = swap(halves[1], "dp", 1)
    got = gate(line, w, joint_half)
    joint = (got, swap(got, "seq", 1))
    height, width = qkv_weight.shape[0], qkv_weight.shape[1]
    qkv = [(qkv_weight, height, width, 0)] + [(half, height // 2, width, 0) for half in joint]
    height, width = dense_weight.shape[0], dense_weight.shape[1]
    dense = [(dense_weight, height, width, 0)] + [
        (half, height, width // 2, half.shape[1] // (width // 2) - 1) for half in joint
    ]
    qkv_shift = absolute(own[6], other[6])[None]
    up_shift = absolute(own[7], other[7])[None]
    bias = absolute(own[4] + own[5], other[4] + other[5])[None]
    payload, arrived, results, attended, qkv_grad = {}, {}, {}, {}, {}
    branch, back_cols, held = {}, {}, {"output": None, "input_grad": None}
    out_shape = (micros, rows, columns)
    totals = {"qkv": 0.0, "one": 0.0}
    sizes = GROUPS if micros == sum(GROUPS) else (1,) * micros
    starts = [sum(sizes[:i]) for i in range(len(sizes))]

    def project(group):
        found = projections(
            line, w, starts[group], sizes[group], rows, one, qkv, qkv_shift, tables, cot, dense
        )
        for i in range(sizes[group]):
            payload[starts[group] + i] = [(array, i) for array in found]

    def bring(m, *distances):
        for k in distances if straight else ():
            array, place = payload[m][k]
            arrived[m, k] = line.ride(array, "seq", k, place * rows, rows)

    def attend(m):
        if straight:
            blocks = [payload[m][0]] + [(arrived[m, k].result, 0) for k in range(1, n)]
            results[m] = list(attention(line, w, rows, blocks, tables))

    def give(m, *distances):
        for k in distances if straight else ():
            results[m][k] = line.ride(results[m][k], "seq", k)

    def attend_pairs():
        blocks = []
        for h in range(heads):
            for m in range(micros):
                array, place = payload[m][h]
                blocks.append(array[place * rows : (place + 1) * rows])
        stacked = jnp.stack(blocks).reshape(n, pairs, rows, 4 * HD)
        found = []
        for pair in range(pairs):
            sent = [
                lax.dynamic_index_in_dim(stacked[:, pair], s ^ k, 0, False) for k in range(n)
            ]
            sent = [sent[0]] + [swap(sent[k], "seq", k) for k in range(1, n)]
            back = attention(line, w, rows, [(array, 0) for array in sent], tables)
            found.append(jnp.stack([back[0]] + [swap(back[k], "seq", k) for k in range(1, n)]))
        for m in range(micros):
            results[m] = []
            for h in range(heads):
                device, pair = divmod(h * micros + m, pairs)
                results[m].append(
                    lax.dynamic_index_in_dim(found[pair], s ^ device, 0, False)
                )

    def both_cores(shard, got, by_rows):
        got = gate(line, w, got)
        return [(shard, *shard.shape, 0)] + [
            (half, *half.shape, 0) for half in (got, swap(got, "seq", 1))
        ]

    def put_out(m):
        if not straight and not results:
            attend_pairs()
        blocks = [block.result if isinstance(block, Ride) else block for block in results[m]]
        partial, attended[m], qkv_grad[m], total = outputs(
            line, w, m, rows, activated, down, dense, blocks
        )
        totals["qkv"] = totals["qkv"] + total
        branch[m] = lax.psum_scatter(partial, "tensor", scatter_dimension=1, tiled=True)

    def go_back(m):
        part, sums = backs(line, w, rows, m, 1, qkv_grad[m], qkv, x, vectors[0:1], part_two)
        totals["one"] = totals["one"] + sums
        back_cols[m] = lax.psum_scatter(part, "tensor", scatter_dimension=1, tiled=True)

    def finish_out(first, count):
        held["output"] = finish(
            line,
            w,
            first // count,
            held["output"],
            states,
            [branch[m] for m in range(first, first + count)],
            bias,
            out_shape,
            BF16,
        )

    def finish_back(first, count):
        held["input_grad"] = finish(
            line,
            w,
            first // count,
            held["input_grad"],
            out_grad,
            [back_cols[m] for m in range(first, first + count)],
            None,
            out_shape,
            F32,
        )

    def spread(vector, axis):
        size = -(-vector.size // 1024) * 1024
        vector = jnp.pad(vector, (0, size - vector.size)).reshape(8, size // 8)
        return [vector] + [line.ride(vector, axis, k) for k in range(1, lax.axis_size(axis))]

    def summed(parts, size):
        parts = landed(parts)
        while len(parts) > 1:
            parts = [one + two for one, two in zip(parts[::2], parts[1::2])]
        return parts[0].reshape(-1)[:size]

    grads, terms = {}, {
        "down": (False, cot, None),
        "up": (True, two, None),
        "dense": (False, cot, None),
        "qkv": (True, one, None),
    }
    steps = {}

    found, rides = {}, {}

    def send(name, swept):
        at_left, side, _ = terms[name]
        terms[name] = (at_left, side, swept)
        at = SEND if at_left else SEND_AT
        sent = weight_grad(line, w, at, at_left, side, swept)
        found[name] = sent.reshape(-1, sent.shape[2])

    def to_sibling(name):
        rides[name] = line.ride(found[name], "seq", 1)

    def keep(name):
        at_left, side, swept = terms[name]
        at = KEEP if at_left else KEEP_AT
        added = rides[name].result
        added = added.reshape(2, added.shape[0] // 2, added.shape[1])
        found[name] = weight_grad(line, w, at, at_left, side, swept, added)
        rides[name] = []

    def parts(name, count):
        height = found[name].shape[-2]
        size = height // PIECES[name]
        first = sum(ride.rows for ride in rides[name])
        return [(first + i * size, size) for i in range(count)]

    def over_y(name, count):
        for first, size in parts(name, count):
            rides[name].append(line.ride(found[name], "dp", 1, first, size, lead=1))

    def over_x(name, count):
        for first, size in parts(name, count):
            rides[name].append(line.ride(found[name], "seq", steps[name], first, size))

    def all_over_y(name):
        rides[name] = [swap(found[name][1], "dp", 1)]

    def all_over_x(name):
        rides[name] = [swap(found[name], "seq", steps[name])]

    def rest_over_x(name):
        for first, size in parts(name, PIECES[name] - len(rides[name])):
            rides[name].append(swap(found[name][first : first + size], "seq", steps[name]))

    def landed(parts):
        return [part.result if isinstance(part, Ride) else part for part in parts]

    def add_up(name):
        found[name] = add(line, w, found[name], landed(rides[name]))
        rides[name] = []
        steps[name] = 2
        while 2 * steps[name] < n:
            found[name] = add(
                line, w, found[name], [swap(found[name], "seq", steps[name])]
            )
            steps[name] *= 2
            rides[name] = []

    def mine_done(name):
        held[name], found[name] = first_half(
            line, w, terms[name][0], found[name], landed(rides[name])
        )

    def sibling_swap(name):
        rides[name] = swap(found[name], "seq", 1)

    def all_done(name):
        ride = rides[name]
        other = ride.result if isinstance(ride, Ride) else ride
        grads[name] = second_half(line, w, terms[name][0], held[name], other)

    def all_terms():
        one_sums, qkv_total = totals["one"], totals["qkv"]
        sums = jnp.concatenate([one_sums, two_sums], 0).reshape(4, 8, features).sum(1)
        norm_own, norm_oth = sums[:, : 2 * half], sums[:, 2 * half :]
        norm_oth = jnp.where(
            core == 1,
            jnp.concatenate([norm_oth[:, half:], norm_oth[:, :half]], 1),
            norm_oth,
        )
        norm_terms = jnp.where(
            d == 1,
            jnp.concatenate([norm_oth, norm_own], 1),
            jnp.concatenate([norm_own, norm_oth], 1),
        ).reshape(-1)
        rest = jnp.concatenate([qkv_total.sum(0), up_total.sum(0), cot_total.sum(0)])
        return norm_terms, rest

    project(0)
    bring(0, 1, 2, 3)
    project(1)
    bring(1, 1, 2)
    attend(0)
    up = both_cores(up_weight, up_got, True)
    bring(1, 3)
    give(0, 1, 2, 3)
    activated, slope = feed_up(line, w, rows, two, up, up_shift)
    down = both_cores(down_weight, down_got, False)
    bring(2, 1, 2)
    put_out(0)
    bring(2, 3)
    attend(1)
    give(1, 1, 2)
    send("down", [activated])
    give(1, 3)
    bring(3, 1, 2)
    to_sibling("down")
    pre_grad, up_total = pre_grads(line, w, rows, cot, down, slope)
    bring(3, 3)
    put_out(1)
    attend(2)
    give(2, 1, 2)
    keep("down")
    give(2, 3)
    over_y("down", 1)
    attend(3)
    give(3, 1, 2)
    over_y("down", 1)
    put_out(2)
    give(3, 3)
    over_y("down", 1)
    send("up", [pre_grad])
    over_y("down", 1)
    to_sibling("up")
    put_out(3)
    add_up("down")
    over_x("down", 1)
    keep("up")
    over_x("down", 3)
    over_y("up", 3)
    part_two, two_sums = backs(line, w, rows, 0, micros, pre_grad, up, x, vectors[2:3])
    over_y("up", 1)
    go_back(0)
    add_up("up")
    heads_out = [attended[m] for m in range(micros)]
    heads_grad = [qkv_grad[m] for m in range(micros)]
    over_x("up", 1)
    send("qkv", heads_grad)
    over_x("up", 1)
    to_sibling("qkv")
    send("dense", heads_out)
    over_x("up", 1)
    to_sibling("dense")
    go_back(1)
    over_x("up", 1)
    keep("qkv")
    over_y("qkv", 1)
    go_back(2)
    over_y("qkv", 1)
    keep("dense")
    add_up("qkv")
    over_x("qkv", 1)
    over_y("dense", 1)
    go_back(3)
    norm_terms, rest = all_terms()
    size = norm_terms.size
    spreads = spread(norm_terms, "tensor")
    add_up("dense")
    norm_terms = summed(spreads, size)
    vector = jnp.concatenate([norm_terms, rest])
    size = vector.size
    spreads = spread(vector, "seq")
    one_sums = gate(line, w, totals["one"])
    vector = summed(spreads, size)
    found["qkv"] = gate(line, w, found["qkv"])
    rest_over_x("qkv")
    mine_done("down")
    sibling_swap("down")
    mine_done("up")
    sibling_swap("up")
    mine_done("qkv")
    sibling_swap("qkv")
    rest_over_x("dense")
    finish_out(0, micros)
    spreads = spread(vector, "dp")
    one_sums = gate(line, w, one_sums)
    vector = summed(spreads, size)
    all_done("down")
    mine_done("dense")
    sibling_swap("dense")
    all_done("up")
    finish_back(0, micros - 1)
    all_done("qkv")
    all_done("dense")
    finish_back(micros - 1, 1)
    norm_terms = vector[: 4 * features].reshape(4, features)
    rest = vector[4 * features :]
    count = columns // 2
    norm_mine = lax.dynamic_slice_in_dim(norm_terms, first + d * count, count, 1)
    vector_grads = []
    place = 0
    for size in (3 * HD * heads, up_total.shape[1], features):
        vector_grads.append(lax.dynamic_slice_in_dim(rest, place + d * (size // 2), size // 2, 0))
        place += size

    return (
        held["output"],
        held["input_grad"],
        norm_mine[0],
        norm_mine[1],
        norm_mine[2],
        norm_mine[3],
        grads["qkv"],
        vector_grads[0],
        grads["dense"],
        vector_grads[2],
        grads["up"],
        vector_grads[1],
        grads["down"],
        vector_grads[2],
    )


def solution(mesh):
    placed = (
        P("dp", "seq", None),
        P("dp"),
        P("dp"),
        P("dp"),
        P("dp"),
        P("dp", "tensor"),
        P(("tensor", "dp")),
        P("tensor", "dp"),
        P("dp"),
        P("dp", "tensor"),
        P(("tensor", "dp")),
        P("tensor", "dp"),
        P("dp"),
        P("dp", "seq", None),
    )
    return jax.shard_map(
        on_device,
        mesh=mesh,
        in_specs=placed,
        out_specs=(
            P("dp", "seq", "tensor"),
            P("dp", "seq", "tensor"),
            P(("tensor", "dp")),
            P(("tensor", "dp")),
            P(("tensor", "dp")),
            P(("tensor", "dp")),
            P("dp", "tensor"),
            P(("tensor", "dp")),
            P("tensor", "dp"),
            P("dp"),
            P("dp", "tensor"),
            P(("tensor", "dp")),
            P("tensor", "dp"),
            P("dp"),
        ),
        check_vma=False,
    )
```

```python
import functools
import math

import jax
import jax.numpy as jnp
import numpy as np
from jax import lax
from jax.experimental import pallas as pl
from jax.experimental.pallas import tpu as pltpu
from jax.sharding import PartitionSpec as P

HD = 128
ROT = 32
HALF_ROT = ROT // 2
EPS = 1e-05
F32 = jnp.float32
BF16 = jnp.bfloat16
NN = (((1,), (0,)), ((), ()))
NT = (((1,), (1,)), ((), ()))
TN = (((0,), (0,)), ((), ()))
WEIGHT = 0.1
GROUPS = (1, 3)
PIECES = {"down": 4, "up": 4, "qkv": 2, "dense": 1}
VMEM_LIMIT = 60 * 1024 * 1024
KEEP, SEND, KEEP_AT, SEND_AT, SEQ, TENSOR, ORDER = 4, 6, 8, 10, 12, 13, 14


def bit(value, b):
    return lax.rem(lax.div(value, jnp.int32(1 << b)), jnp.int32(2))


def xor(value, other):
    value, other = jnp.int32(value), jnp.int32(other)
    return sum((1 << b) * lax.rem(bit(value, b) + bit(other, b), jnp.int32(2)) for b in range(4))


class Places:
    def __init__(self, straight):
        self.straight = straight

    def __getitem__(self, key):
        s = lax.axis_index("seq")
        if key == SEQ:
            return s
        if key == TENSOR:
            return lax.axis_index("tensor")
        if key >= ORDER:
            return self.head(key - ORDER)
        core = lax.rem(s, jnp.int32(2))
        d = lax.axis_index("dp")
        places = (2 * d, 2 * d + 1, 2 * (1 - d) + core, 2 * (1 - d) + 1 - core)
        if key < KEEP:
            return places[key]
        if key < KEEP_AT:
            return (core, 2, 1 - core, 3)[key - KEEP]
        return (2 * d + core, places[2], 2 * d + 1 - core, places[3])[key - KEEP_AT]

    def head(self, slot):
        return xor(lax.axis_index("seq"), slot) if self.straight else slot

    def either(self, key, i):
        return (1 - i) * self[key] + i * self[key + 1]


class Ride:
    def __init__(self, source, axis, distance, first=0, rows=None, lead=None):
        self.source, self.axis, self.distance = source, axis, distance
        self.first, self.lead = first, lead
        self.rows = source.shape[-2] - first if rows is None else rows
        self.result = None

    @property
    def shape(self):
        return (self.rows, self.source.shape[-1])

    def target(self):
        return {self.axis: xor(lax.axis_index(self.axis), self.distance)}

    def copy(self, source, target, sent, got):
        at = pl.ds(self.first, self.rows)
        return pltpu.make_async_remote_copy(
            src_ref=source.at[at] if self.lead is None else source.at[self.lead, at],
            dst_ref=target,
            send_sem=sent,
            recv_sem=got,
            device_id=self.target(),
            device_id_type=pl.DeviceIdType.MESH,
        )


class Line:
    def __init__(self, first):
        self.last = [first]
        self.rides = []
        self.count = 0

    def ride(self, *args, **kwargs):
        self.rides.append(Ride(*args, **kwargs))
        return self.rides[-1]


def mm(a, b, dims=NN):
    return lax.dot_general(a, b, dims, preferred_element_type=F32)


def swap(block, axis, distance):
    return lax.ppermute(block, axis, [(i, i ^ distance) for i in range(lax.axis_size(axis))])


def spec(block, index):
    if block is None:
        return pl.BlockSpec(memory_space=pl.ANY)
    return pl.BlockSpec(block, index)


def call(line, kernel, w, grid, inputs, outputs, scratch=(), flops=0, nbytes=0, name=None, alias=None):
    before = [token for token in line.last if alias is None or token is not inputs[alias][0]]
    rides, line.rides = line.rides, []
    skip = len(before) + len(rides)
    ends = len(inputs) + len(outputs)
    steps = 1
    for size in grid:
        steps *= size
    staged = [i for i in range(len(inputs)) if rides and steps == 1 and inputs[i][1] is not None]

    def stage(ref, block, index):
        cut = []
        for size, place in zip(block, index(*[0] * len(grid), w)):
            if size is None:
                cut.append(place)
            elif isinstance(place, int):
                cut.append(slice(place * size, (place + 1) * size))
            else:
                cut.append(pl.ds(pl.multiple_of(place * size, size), size))
        return ref.at[tuple(cut)]

    def at(index):
        return None if index is None else lambda *steps: index(*steps, w)

    def on_step(last, work):
        chosen = True
        for axis, size in enumerate(grid):
            if size > 1:
                step = pl.program_id(axis)
                chosen = jnp.logical_and(chosen, step == (size - 1 if last else 0))
        if chosen is True:
            work()
        else:
            pl.when(chosen)(work)

    def body(*refs):
        sources = refs[len(before) : skip]
        own = refs[skip : skip + ends]
        targets = refs[skip + ends : skip + ends + len(rides)]
        rest = refs[skip + ends + len(rides) :]
        if not rides:
            kernel(w, *own, *rest)
            return
        *rest, sent, got = rest
        own = list(own)
        loads = []
        if staged:
            *rest, loaded = rest
            buffers = rest[len(rest) - len(staged) :]
            rest = rest[: len(rest) - len(staged)]
            for k, i in enumerate(staged):
                part = stage(own[i], *inputs[i][1:])
                loads.append(pltpu.make_async_copy(part, buffers[k], loaded.at[k]))
                own[i] = buffers[k]
        copies = lambda: [
            ride.copy(source, target, sent.at[i], got.at[i])
            for i, (ride, source, target) in enumerate(zip(rides, sources, targets))
        ]

        def start():
            barrier = pltpu.get_barrier_semaphore()
            partners = {(ride.axis, ride.distance): ride for ride in rides}
            for ride in partners.values():
                pl.semaphore_signal(
                    barrier, inc=1, device_id=ride.target(), device_id_type=pl.DeviceIdType.MESH
                )
            pl.semaphore_wait(barrier, len(partners))
            for copy in copies():
                copy.start()

        def wait():
            for copy in copies():
                copy.wait()

        for load in loads:
            load.start()
        on_step(False, start)
        for load in loads:
            load.wait()
        kernel(w, *own, *rest)
        on_step(True, wait)

    params = dict(
        vmem_limit_bytes=VMEM_LIMIT, dimension_semantics=("arbitrary",) * len(grid)
    )
    sems = []
    if rides:
        params.update(collective_id=line.count, has_side_effects=True)
        line.count += 1
        for i in staged:
            array, block, _ = inputs[i]
            shape = tuple(size for size in block if size is not None)
            sems.append(pltpu.VMEM(shape, array.dtype))
        if staged:
            sems.append(pltpu.SemaphoreType.DMA((len(staged),)))
        sems += [pltpu.SemaphoreType.DMA((len(rides),))] * 2
    anywhere = pl.BlockSpec(memory_space=pl.ANY)
    results = pl.pallas_call(
        body,
        grid=grid,
        in_specs=[anywhere] * skip
        + [
            anywhere if i in staged else spec(block, at(index))
            for i, (_, block, index) in enumerate(inputs)
        ],
        out_specs=[spec(block, at(index)) for _, _, block, index in outputs]
        + [anywhere] * len(rides),
        scratch_shapes=list(scratch) + sems,
        out_shape=[jax.ShapeDtypeStruct(shape, dtype) for shape, dtype, _, _ in outputs]
        + [jax.ShapeDtypeStruct(ride.shape, ride.source.dtype) for ride in rides],
        compiler_params=pltpu.CompilerParams(**params),
        cost_estimate=pl.CostEstimate(
            flops=int(flops * WEIGHT), bytes_accessed=int(nbytes * WEIGHT), transcendentals=0
        ),
        input_output_aliases={} if alias is None else {skip + alias: 0},
        name=name,
    )(*before, *[ride.source for ride in rides], *[array for array, _, _ in inputs])
    for ride, result in zip(rides, results[len(outputs) :]):
        ride.result = result
    results = results[: len(outputs)]
    line.last = [results[-1]]
    return results


def fixed(*index):
    return lambda *_: index


def groups(values):
    return jnp.sum(values.reshape(values.shape[0] // 8, 8, values.shape[1]), 0)


def columns_at(w, b, size):
    return pl.ds(pl.multiple_of(w[b] * size, size), size)


def norm_kernel(w, x, cot, vectors, one, two, total):
    quarter = x.shape[1] // 4

    @pl.when(pl.program_id(0) == 0)
    def _():
        total[...] = jnp.zeros_like(total)

    values = x[...].astype(F32)
    mean = jnp.mean(values, -1, keepdims=True)
    center = values - mean
    inverse = lax.rsqrt(jnp.mean(center * center, -1, keepdims=True) + EPS)
    for b in range(4):
        at = slice(b * quarter, (b + 1) * quarter)
        unit = (x[:, columns_at(w, b, quarter)].astype(F32) - mean) * inverse
        one[:, at] = (unit * vectors[0:1, at] + vectors[1:2, at]).astype(BF16)
        two[:, at] = (unit * vectors[2:3, at] + vectors[3:4, at]).astype(BF16)
    total[...] += groups(cot[...].astype(F32))


def norms(line, w, x, cot, vectors):
    tokens, features = x.shape
    size = min(256, tokens)
    row = (size, features)
    along = lambda i, w: (i, 0)
    return call(
        line,
        norm_kernel,
        w,
        (tokens // size,),
        [(x, row, along), (cot, row, along), (vectors, vectors.shape, fixed(0, 0))],
        [
            ((tokens, features), BF16, row, along),
            ((tokens, features), BF16, row, along),
            ((8, features), F32, (8, features), fixed(0, 0)),
        ],
        flops=30 * tokens * features,
        nbytes=8 * tokens * features,
        name="norms",
    )


def turned(values):
    lane = lax.broadcasted_iota(jnp.int32, values.shape, 1)
    return jnp.where(
        lane < HALF_ROT, pltpu.roll(values, HD - HALF_ROT, 1), pltpu.roll(values, HALF_ROT, 1)
    )


def turn_tables(length):
    frequency = 10000.0 ** (-np.arange(HALF_ROT) * 2.0 / ROT)
    angles = np.arange(length)[:, None] * frequency[None, :]
    cosine = np.ones((length, HD), np.float32)
    sine = np.zeros((length, HD), np.float32)
    cosine[:, :ROT] = np.tile(np.cos(angles), (1, 2))
    sine[:, :HALF_ROT] = np.sin(angles)
    sine[:, HALF_ROT:ROT] = -np.sin(angles)
    return jnp.asarray(cosine), jnp.asarray(sine)


def project_kernel(
    slots, w, one, q0, q1, q2, bias, cosine, sine, c0, c1, c2, c3, d0, d1, d2, *outs
):
    step = pl.program_id(0)
    quarter = c0.shape[1]
    u = (
        mm(one[:, : 2 * quarter], q0[...])
        + mm(one[:, 2 * quarter : 3 * quarter], q1[...])
        + mm(one[:, 3 * quarter :], q2[...])
        + bias[...]
    )
    g = (
        mm(c0[...], d0[:, :quarter], NT)
        + mm(c1[...], d0[:, quarter:], NT)
        + mm(c2[...], d1[...], NT)
        + mm(c3[...], d2[...], NT)
    )
    cos, sin = cosine[...], sine[...]
    rows = u.shape[0]
    at_rows = pl.ds(pl.multiple_of(pl.program_id(1) * rows, rows), rows)
    flip = lax.rem(w.head(2 * step), jnp.int32(2))
    blocks = []
    for head in range(2):
        at = head * 3 * HD
        query, key = u[:, at : at + HD], u[:, at + HD : at + 2 * HD]
        blocks.append(
            jnp.concatenate(
                [
                    (query * cos - turned(query) * sin).astype(BF16),
                    (key * cos - turned(key) * sin).astype(BF16),
                    u[:, at + 2 * HD : at + 3 * HD].astype(BF16),
                    g[:, head * HD : (head + 1) * HD].astype(BF16),
                ],
                1,
            )
        )
    for pair in range(slots // 2):
        for turn in range(2):

            @pl.when((step == pair) & (flip == turn))
            def _():
                outs[2 * pair + turn][at_rows, :] = blocks[0]
                outs[2 * pair + 1 - turn][at_rows, :] = blocks[1]


def projections(line, w, first, count, rows, one, qkv, bias, tables, cot, dense):
    features = one.shape[1]
    quarter = features // 4
    heads = dense[0][1] // HD
    wide = 6 * HD
    pair = lambda i, m, w: (0, lax.div(w.head(2 * i), jnp.int32(2)))
    own = lambda i, m, w: (w[SEQ], 0)
    inputs = [(one, (rows, features), lambda i, m, w: (m + first, 0))]
    inputs += [(array, (height, wide), pair) for array, height, _, _ in qkv]
    inputs += [(bias, (1, wide), pair)]
    inputs += [(table, (rows, HD), own) for table in tables]
    for b in range(4):
        inputs.append((cot, (rows, quarter), lambda i, m, w, b=b: (m + first, w[b])))
    for array, _, width, place in dense:
        inputs.append(
            (array, (2 * HD, width), lambda i, m, w, b=place: (lax.div(w.head(2 * i), jnp.int32(2)), b))
        )
    return call(
        line,
        functools.partial(project_kernel, heads),
        w,
        (heads // 2, count),
        inputs,
        [((count * rows, 4 * HD), BF16, (count * rows, 4 * HD), fixed(0, 0))] * heads,
        flops=2 * count * rows * features * heads * 4 * HD,
        nbytes=2 * features * (heads * 4 * HD + 2 * count * rows) + 8 * count * rows * heads * HD,
        name="projections",
    )


def attention_kernel(parts, scale, qsize, ksize, w, *refs):
    ins = refs[:parts]
    cos_ref, sin_ref = refs[parts : parts + 2]
    outs = refs[parts + 2 : 2 * parts + 2]
    q_s, k_s, v_s, g_s, kt_s, vt_s, prob_s, dk_s, dv_s, o_s, dq_s = refs[2 * parts + 2 :]
    rows = ins[0].shape[0]
    length = parts * rows
    places = []
    for k in range(parts):
        at = pl.ds(pl.multiple_of(xor(w[SEQ], k) * rows, rows), rows)
        places.append(at)
        q_s[at, :] = ins[k][:, 0:HD]
        k_s[at, :] = ins[k][:, HD : 2 * HD]
        v_s[at, :] = ins[k][:, 2 * HD : 3 * HD]
        g_s[at, :] = ins[k][:, 3 * HD : 4 * HD]
    for j in range(length // ksize):
        at = slice(j * ksize, (j + 1) * ksize)
        kt_s[:, at] = k_s[at, :].T
        vt_s[:, at] = v_s[at, :].T
    factor = scale * math.log2(math.e)
    for i in range(length // qsize):
        qat = slice(i * qsize, (i + 1) * qsize)
        q = q_s[qat, :]
        g = g_s[qat, :]
        chunks = []
        for first in range(0, (i + 1) * qsize, ksize):
            chunks.append((first, min(ksize, (i + 1) * qsize - first)))
        top = jnp.full((8, qsize), -1e30, F32)
        for first, size in chunks:
            s = mm(k_s[first : first + size, :], q, NT)
            if first + size > i * qsize:
                key = lax.broadcasted_iota(jnp.int32, s.shape, 0) + (first - i * qsize)
                query = lax.broadcasted_iota(jnp.int32, s.shape, 1)
                s = jnp.where(key <= query, s, -1e30)
            prob_s[first : first + size, :] = s
            top = jnp.maximum(top, jnp.max(s.reshape(size // 8, 8, qsize), 0))
        top = jnp.max(top, 0, keepdims=True)
        total = jnp.zeros((8, qsize), F32)
        acc = jnp.zeros((HD, qsize), F32)
        for first, size in chunks:
            e = jnp.exp2((prob_s[first : first + size, :] - top) * factor)
            prob_s[first : first + size, :] = e
            total = total + jnp.sum(e.reshape(size // 8, 8, qsize), 0)
            acc = acc + mm(vt_s[:, first : first + size], e.astype(BF16))
        inverse = 1.0 / jnp.sum(total, 0, keepdims=True)
        acc = acc * inverse
        delta = jnp.sum(acc * g.T.astype(F32), 0, keepdims=True)
        o_s[qat, :] = acc.T.astype(BF16)
        dqt = jnp.zeros((HD, qsize), F32)
        for first, size in chunks:
            at = slice(first, first + size)
            p = prob_s[at, :] * inverse
            ds = (p * (mm(v_s[at, :], g, NT) - delta)).astype(BF16)
            dv = mm(p.astype(BF16), g)
            dk = mm(ds, q)
            low = max(0, min(size, i * qsize - first))
            if low:
                old = slice(first, first + low)
                dv_s[old, :] += dv[:low]
                dk_s[old, :] += dk[:low]
            if low < size:
                new = slice(first + low, first + size)
                dv_s[new, :] = dv[low:]
                dk_s[new, :] = dk[low:]
            dqt = dqt + mm(kt_s[:, at], ds)
        dq_s[qat, :] = dqt.T
    for k in range(parts):
        at = places[k]
        cosine = cos_ref[at, :]
        sine = sin_ref[at, :]
        dq, dk = dq_s[at, :], dk_s[at, :]
        outs[k][:, 0:HD] = o_s[at, :]
        outs[k][:, HD : 2 * HD] = ((dq * cosine + turned(dq) * sine) * scale).astype(BF16)
        outs[k][:, 2 * HD : 3 * HD] = ((dk * cosine + turned(dk) * sine) * scale).astype(BF16)
        outs[k][:, 3 * HD : 4 * HD] = dv_s[at, :].astype(BF16)


def attention(line, w, rows, blocks, tables, qsize=512, ksize=512):
    parts = len(blocks)
    width = blocks[0][0].shape[1]
    count = 1
    length = parts * rows
    qsize, ksize = min(qsize, rows), min(ksize, rows)
    block = ((rows, width), lambda m, w: (m, 0))
    return call(
        line,
        functools.partial(attention_kernel, parts, HD ** (-0.5), qsize, ksize),
        w,
        (count,),
        [(array, (rows, width), fixed(place, 0)) for array, place in blocks] + [(table, (length, HD), fixed(0, 0)) for table in tables],
        [((count * rows, width), BF16, *block)] * parts,
        scratch=[pltpu.VMEM((length, HD), BF16)] * 4
        + [pltpu.VMEM((HD, length), BF16)] * 2
        + [pltpu.VMEM((length, qsize), F32)]
        + [pltpu.VMEM((length, HD), F32)] * 2
        + [pltpu.VMEM((length, HD), BF16)]
        + [pltpu.VMEM((length, HD), F32)],
        flops=14 * count * length * length * HD,
        nbytes=4 * count * length * width + 8 * length * HD,
        name="attention",
    )


def up_kernel(w, two, u0, u1, u2, bias, activated, slope):
    quarter = u1.shape[0]
    pre = (
        mm(two[:, : 2 * quarter], u0[...])
        + mm(two[:, 2 * quarter : 3 * quarter], u1[...])
        + mm(two[:, 3 * quarter :], u2[...])
        + bias[...]
    )
    tail = 0.5 + 0.5 * lax.erf(pre * math.sqrt(0.5))
    activated[...] = (pre * tail).astype(BF16)
    bell = jnp.exp2(pre * pre * (-0.5 * math.log2(math.e))) * (1.0 / math.sqrt(2.0 * math.pi))
    slope[...] = (tail + pre * bell).astype(BF16)


def feed_up(line, w, rows, two, up, bias):
    tokens, features = two.shape
    hidden = up[0][2]
    wide = min(1024, hidden)
    column = lambda j, m, w: (0, j)
    out = ((tokens, hidden), BF16, (rows, wide), lambda j, m, w: (m, j))
    return call(
        line,
        up_kernel,
        w,
        (hidden // wide, tokens // rows),
        [(two, (rows, features), lambda j, m, w: (m, 0))]
        + [(array, (height, wide), column) for array, height, _, _ in up]
        + [(bias, (1, wide), column)],
        [out, out],
        flops=2 * tokens * features * hidden,
        nbytes=2 * features * (hidden + 2 * tokens) + 4 * tokens * hidden,
        name="feed_up",
    )


def pre_grad_kernel(w, c0, c1, c2, c3, n0, n1, n2, slope, out, total):
    quarter = c0.shape[1]
    act_grad = (
        mm(c0[...], n0[:, :quarter], NT)
        + mm(c1[...], n0[:, quarter:], NT)
        + mm(c2[...], n1[...], NT)
        + mm(c3[...], n2[...], NT)
    )
    grad = (act_grad * slope[...].astype(F32)).astype(BF16)
    out[...] = grad

    @pl.when(pl.program_id(1) == 0)
    def _():
        total[...] = jnp.zeros_like(total)

    total[...] += groups(grad.astype(F32))


def pre_grads(line, w, rows, cot, down, slope):
    tokens, features = cot.shape
    hidden = slope.shape[1]
    wide = min(1024, hidden)
    quarter = features // 4
    inputs = []
    for b in range(4):
        inputs.append((cot, (rows, quarter), lambda j, m, w, b=b: (m, w[b])))
    inputs += [(array, (wide, width), lambda j, m, w: (j, 0)) for array, _, width, _ in down]
    tile = ((rows, wide), lambda j, m, w: (m, j))
    return call(
        line,
        pre_grad_kernel,
        w,
        (hidden // wide, tokens // rows),
        inputs + [(slope, *tile)],
        [
            ((tokens, hidden), BF16, *tile),
            ((8, hidden), F32, (8, wide), lambda j, m, w: (0, j)),
        ],
        flops=2 * tokens * features * hidden,
        nbytes=2 * features * (hidden + 2 * tokens) + 4 * tokens * hidden,
        name="pre_grads",
    )


def back_kernel(more, w, grad, w0, w1, w2, x, gain, *refs):
    if more:
        before, out, sums, e = refs
    else:
        out, sums, e = refs
    features = x.shape[1]
    quarter = features // 4
    rows = x.shape[0]

    @pl.when(pl.program_id(0) == 0)
    def _():
        sums[...] = jnp.zeros_like(sums)

    e[:, : 2 * quarter] = mm(grad[...], w0[...], NT)
    e[:, 2 * quarter : 3 * quarter] = mm(grad[...], w1[...], NT)
    e[:, 3 * quarter :] = mm(grad[...], w2[...], NT)
    values = x[...].astype(F32)
    mean = jnp.mean(values, -1, keepdims=True)
    center = values - mean
    inverse = lax.rsqrt(jnp.mean(center * center, -1, keepdims=True) + EPS)
    middle = jnp.zeros((rows, 1), F32)
    slant = jnp.zeros((rows, 1), F32)
    for b in range(4):
        at = slice(b * quarter, (b + 1) * quarter)
        unit = (x[:, columns_at(w, b, quarter)].astype(F32) - mean) * inverse
        found = e[:, at]
        sums[0:8, at] += groups(found * unit)
        sums[8:16, at] += groups(found)
        scaled = found * gain[:, at]
        middle += jnp.sum(scaled, -1, keepdims=True)
        slant += jnp.sum(scaled * unit, -1, keepdims=True)
    middle = middle * (1.0 / features)
    slant = slant * (1.0 / features)
    for b in range(4):
        at = slice(b * quarter, (b + 1) * quarter)
        place = columns_at(w, b, quarter)
        unit = (x[:, place].astype(F32) - mean) * inverse
        part = inverse * (e[:, at] * gain[:, at] - middle - unit * slant)
        if more:
            part = part + before[:, place].astype(F32)
        out[:, place] = part.astype(BF16)


def backs(line, w, rows, first, count, grad, weight, x, gain, before=None):
    features = x.shape[1]
    width = grad.shape[1]
    row = (rows, features)
    shift = lambda m, w: (m + first, 0)
    along = lambda m, w: (m, 0)
    inputs = [(grad, (rows, width), along)]
    inputs += [(array, (height, wide), fixed(0, place)) for array, height, wide, place in weight]
    inputs += [(x, row, shift), (gain, gain.shape, fixed(0, 0))]
    if before is not None:
        inputs.append((before, row, shift))
    return call(
        line,
        functools.partial(back_kernel, before is not None),
        w,
        (count,),
        inputs,
        [
            ((count * rows, features), BF16, row, along),
            ((16, features), F32, (16, features), fixed(0, 0)),
        ],
        scratch=[pltpu.VMEM(row, F32)],
        flops=2 * count * rows * features * width,
        nbytes=2 * (features * width + count * rows * (width + 3 * features)),
        name="backs",
    )


def output_kernel(heads, w, act, n0, n1, n2, d0, d1, d2, *refs):
    blocks = refs[:heads]
    part, attended, qkv_grad, total = refs[heads:]
    quarter = n1.shape[1]

    @pl.when(pl.program_id(0) == 0)
    def _():
        total[...] = jnp.zeros_like(total)

    for i in range(heads):
        head = w[ORDER + i]
        attended[:, pl.ds(pl.multiple_of(head * HD, HD), HD)] = blocks[i][:, :HD]
        at = pl.ds(pl.multiple_of(head * 3 * HD, HD), 3 * HD)
        qkv_grad[:, at] = blocks[i][:, HD:]
        total[:, at] += groups(blocks[i][:, HD:].astype(F32))
    pieces = [(n0, d0, 0), (n0, d0, 1), (n1, d1, 0), (n2, d2, 0)]
    for b, (down, dense, half) in enumerate(pieces):
        at = slice(half * quarter, (half + 1) * quarter)
        part[:, columns_at(w, b, quarter)] = (
            mm(attended[...], dense[:, at]) + mm(act[...], down[:, at])
        ).astype(BF16)


def outputs(line, w, first, rows, act, down, dense, blocks):
    hidden = act.shape[1]
    inner = dense[0][1]
    features = 2 * dense[0][2]
    heads = len(blocks)
    count = 1
    along = lambda m, w: (m, 0)
    inputs = [(act, (rows, hidden), lambda m, w: (m + first, 0))]
    for array, height, width, place in (*down, *dense):
        inputs.append((array, (height, width), fixed(0, place)))
    inputs += [(block, block.shape, fixed(0, 0)) for block in blocks]
    wide = lambda size: ((count * rows, size), BF16, (rows, size), along)
    return call(
        line,
        functools.partial(output_kernel, heads),
        w,
        (count,),
        inputs,
        [
            wide(features),
            wide(inner),
            wide(3 * inner),
            ((8, 3 * inner), F32, (8, 3 * inner), fixed(0, 0)),
        ],
        flops=2 * count * rows * features * (hidden + inner),
        nbytes=2 * features * (hidden + inner)
        + 2 * count * rows * (hidden + features + 8 * inner),
        name="outputs",
    )


def grad_kernel(pieces, count, at_left, adds, w, *refs):
    sides, swept = refs[: (1 if at_left else count)], refs[1 if at_left else count :]
    rest = swept[pieces:]
    swept = swept[:pieces]
    out = rest[-1]
    for i, side in enumerate(sides):
        value = 0.0
        start = 0
        for ref in swept:
            part = side[start : start + ref.shape[0], :]
            start += ref.shape[0]
            value = value + (mm(part, ref[...], TN) if at_left else mm(ref[...], part, TN))
        if adds:
            value = value + rest[0][i].astype(F32)
        out[i] = value.astype(BF16)


def weight_grad(line, w, at, at_left, side, swept, adds=None):
    tokens = side.shape[0]
    quarter = side.shape[1] // 4
    size = swept[0].shape[1]
    tile = min(256, quarter, size)
    heights = [piece.shape[0] for piece in swept]
    if at_left:
        split = quarter // tile
        grid = (2, split)
        inputs = [(side, (tokens, tile), lambda i, j, w: (0, w.either(at, i) * split + j))]
        inputs += [(piece, piece.shape, fixed(0, 0)) for piece in swept]
        out = ((2, quarter, size), BF16, (1, tile, size), lambda i, j, w: (i, j, 0))
    else:
        grid = (size // tile,)
        inputs = []
        for i in range(2):
            inputs.append((side, (tokens, quarter), lambda j, w, i=i: (0, w[at + i])))
        inputs += [(piece, (piece.shape[0], tile), lambda j, w: (0, j)) for piece in swept]
        out = ((2, size, quarter), BF16, (2, tile, quarter), lambda j, w: (0, j, 0))
    if adds is not None:
        inputs.append((adds, out[2], out[3]))
    return call(
        line,
        functools.partial(grad_kernel, len(swept), 2, at_left, adds is not None),
        w,
        grid,
        inputs,
        [out],
        flops=4 * tokens * quarter * size,
        nbytes=2 * tokens * (2 * quarter + size) + 8 * quarter * size,
        name="weight_grad",
    )[0]


def join(pieces):
    return [(piece, piece.shape, fixed(0, 0)) for piece in pieces]


def add_kernel(w, mine, *refs):
    *pieces, out = refs
    first = 0
    for piece in pieces:
        at = slice(first, first + piece.shape[0])
        out[at, :] = (mine[at, :].astype(F32) + piece[...].astype(F32)).astype(BF16)
        first += piece.shape[0]


def add(line, w, mine, pieces):
    shape = mine.shape[-2:]
    first = (mine, (None,) + shape, fixed(0, 0, 0)) if mine.ndim == 3 else (mine, shape, fixed(0, 0))
    return call(
        line,
        add_kernel,
        w,
        (1,),
        [first] + join(pieces),
        [(shape, BF16, shape, fixed(0, 0))],
        nbytes=6 * shape[0] * shape[1],
        name="add",
    )[0]


def first_half_kernel(w, mine, *refs):
    *pieces, wide, total = refs
    first = 0
    for piece in pieces:
        at = slice(first, first + piece.shape[0])
        value = (mine[at, :].astype(F32) + piece[...].astype(F32)).astype(BF16)
        total[at, :] = value
        wide[at, :] = value.astype(F32)
        first += piece.shape[0]


def first_half(line, w, at_left, mine, pieces):
    height, width = mine.shape
    if at_left:
        whole, place = (2 * height, width), lambda i, w: (w[KEEP], 0)
    else:
        whole, place = (height, 2 * width), lambda i, w: (0, w[KEEP])
    return call(
        line,
        first_half_kernel,
        w,
        (1,),
        [(mine, mine.shape, fixed(0, 0))] + join(pieces),
        [(whole, F32, mine.shape, place), (mine.shape, BF16, mine.shape, fixed(0, 0))],
        nbytes=10 * height * width,
        name="first_half",
    )


def second_half_kernel(w, held, other, wide):
    wide[...] = other[...].astype(F32)


def second_half(line, w, at_left, held, other):
    height, width = other.shape
    size = height // 2
    if at_left:
        whole, place = (2 * height, width), lambda i, w: (2 * w[SEND] + i, 0)
    else:
        whole, place = (height, 2 * width), lambda i, w: (i, w[SEND])
    return call(
        line,
        second_half_kernel,
        w,
        (2,),
        [(held, None, None), (other, (size, width), lambda i, w: (i, 0))],
        [(whole, F32, (size, width), place)],
        nbytes=6 * height * width,
        name="second_half",
        alias=0,
    )[0]


def gate_kernel(w, source, target):
    pass


def gate(line, w, array):
    return call(
        line,
        gate_kernel,
        w,
        (1,),
        [(array, None, None)],
        [(array.shape, array.dtype, None, None)],
        name="gate",
        alias=0,
    )[0]


def finish_kernel(count, more, w, kept, *refs):
    cols, refs = refs[:count], refs[count:]
    refs = refs[1:] if more else refs
    *bias, out = refs
    for i in range(count):
        value = kept[i].astype(F32) + cols[i][...].astype(F32)
        for ref in bias:
            value = value + ref[...]
        out[i] = value.astype(out.dtype)


def finish(line, w, place, held, kept, cols, bias, shape, dtype):
    _, rows, columns = shape
    count = len(cols)
    block = (count, rows, columns)
    inputs = [(kept, block, lambda i, w: (place, 0, w[TENSOR]))]
    inputs += [(part, (rows, columns), fixed(0, 0)) for part in cols]
    if held is not None:
        inputs.append((held, None, None))
    if bias is not None:
        inputs.append((bias, (1, columns), lambda i, w: (0, w[TENSOR])))
    return call(
        line,
        functools.partial(finish_kernel, count, held is not None),
        w,
        (1,),
        inputs,
        [(shape, dtype, block, fixed(place, 0, 0))],
        nbytes=8 * count * rows * columns,
        name="finish",
        alias=None if held is None else 1 + count,
    )[0]


def pick_kernel(joint, w, by_rows, by_columns, *targets):
    if joint:
        width = by_columns.shape[1]
        targets[0][:, : by_rows.shape[1]] = by_rows[...]
        targets[0][: by_columns.shape[0], targets[0].shape[1] - width :] = by_columns[...]
    else:
        targets[0][...] = by_rows[...]
        targets[1][...] = by_columns[...]


def pick(line, w, by_rows, by_columns, joint):
    height, width = by_rows.shape[0] // 2, by_columns.shape[1] // 2
    first = (height, by_rows.shape[1])
    second = (by_columns.shape[0], width)
    if joint:
        shapes = [(max(first[0], second[0]), pl.cdiv(first[1], width) * width + width)]
    else:
        shapes = [first, second]
    return call(
        line,
        functools.partial(pick_kernel, joint),
        w,
        (1,),
        [
            (by_rows, first, lambda i, w: (w[KEEP], 0)),
            (by_columns, second, lambda i, w: (0, w[KEEP])),
        ],
        [(shape, BF16, shape, fixed(0, 0)) for shape in shapes],
        nbytes=4 * (first[0] * first[1] + second[0] * second[1]),
        name="pick",
    )


def on_device(
    states,
    ln1_gain,
    ln1_bias,
    ln2_gain,
    ln2_bias,
    qkv_weight,
    qkv_bias,
    dense_weight,
    dense_bias,
    up_weight,
    up_bias,
    down_weight,
    out_bias,
    out_grad,
):
    micros, rows, features = states.shape
    heads = qkv_weight.shape[1] // (3 * HD)
    tokens = micros * rows
    n = lax.axis_size("seq")
    pairs = heads * micros // n
    straight = heads == n
    s = lax.axis_index("seq")
    core = s % 2
    d = lax.axis_index("dp")
    columns = features // lax.axis_size("tensor")
    first = lax.axis_index("tensor") * columns
    w = Places(straight)

    def absolute(own, other):
        return jnp.where(d == 1, jnp.concatenate([other, own]), jnp.concatenate([own, other]))

    x = states.reshape(tokens, features)
    cot = out_grad.reshape(tokens, features)

    small = (ln1_gain, ln1_bias, ln2_gain, ln2_bias, dense_bias, out_bias, qkv_bias, up_bias)
    small_got = swap(jnp.concatenate(small, 0), "dp", 1)
    line = Line(small_got)
    joint_half = swap(pick(line, w, qkv_weight, dense_weight, True)[0], "dp", 1)
    own, other = [], []
    place = 0
    for vector in small:
        own.append(vector.astype(F32))
        other.append(small_got[place : place + vector.shape[0]].astype(F32))
        place += vector.shape[0]
    half = features // 4
    vectors = jnp.stack(
        [
            jnp.concatenate(
                [
                    own[i],
                    lax.dynamic_slice_in_dim(other[i], core * half, half),
                    lax.dynamic_slice_in_dim(other[i], (1 - core) * half, half),
                ]
            )
            for i in range(4)
        ]
    )
    tables = turn_tables(n * rows)

    one, two, cot_total = norms(line, w, x, cot, vectors)
    halves = pick(line, w, up_weight, down_weight, False)
    up_got = swap(halves[0], "dp", 1)
    down_got = swap(halves[1], "dp", 1)
    got = gate(line, w, joint_half)
    joint = (got, swap(got, "seq", 1))
    height, width = qkv_weight.shape[0], qkv_weight.shape[1]
    qkv = [(qkv_weight, height, width, 0)] + [(half, height // 2, width, 0) for half in joint]
    height, width = dense_weight.shape[0], dense_weight.shape[1]
    dense = [(dense_weight, height, width, 0)] + [
        (half, height, width // 2, half.shape[1] // (width // 2) - 1) for half in joint
    ]
    qkv_shift = absolute(own[6], other[6])[None]
    up_shift = absolute(own[7], other[7])[None]
    bias = absolute(own[4] + own[5], other[4] + other[5])[None]
    payload, arrived, results, attended, qkv_grad = {}, {}, {}, {}, {}
    branch, back_cols, held = {}, {}, {"output": None, "input_grad": None}
    out_shape = (micros, rows, columns)
    totals = {"qkv": 0.0, "one": 0.0}
    sizes = GROUPS if micros == sum(GROUPS) else (1,) * micros
    starts = [sum(sizes[:i]) for i in range(len(sizes))]

    def project(group):
        found = projections(
            line, w, starts[group], sizes[group], rows, one, qkv, qkv_shift, tables, cot, dense
        )
        for i in range(sizes[group]):
            payload[starts[group] + i] = [(array, i) for array in found]

    def bring(m, *distances):
        for k in distances if straight else ():
            array, place = payload[m][k]
            arrived[m, k] = line.ride(array, "seq", k, place * rows, rows)

    def attend(m):
        if straight:
            blocks = [payload[m][0]] + [(arrived[m, k].result, 0) for k in range(1, n)]
            results[m] = list(attention(line, w, rows, blocks, tables))

    def give(m, *distances):
        for k in distances if straight else ():
            results[m][k] = line.ride(results[m][k], "seq", k)

    def attend_pairs():
        blocks = []
        for h in range(heads):
            for m in range(micros):
                array, place = payload[m][h]
                blocks.append(array[place * rows : (place + 1) * rows])
        stacked = jnp.stack(blocks).reshape(n, pairs, rows, 4 * HD)
        found = []
        for pair in range(pairs):
            sent = [
                lax.dynamic_index_in_dim(stacked[:, pair], s ^ k, 0, False) for k in range(n)
            ]
            sent = [sent[0]] + [swap(sent[k], "seq", k) for k in range(1, n)]
            back = attention(line, w, rows, [(array, 0) for array in sent], tables)
            found.append(jnp.stack([back[0]] + [swap(back[k], "seq", k) for k in range(1, n)]))
        for m in range(micros):
            results[m] = []
            for h in range(heads):
                device, pair = divmod(h * micros + m, pairs)
                results[m].append(
                    lax.dynamic_index_in_dim(found[pair], s ^ device, 0, False)
                )

    def both_cores(shard, got, by_rows):
        got = gate(line, w, got)
        return [(shard, *shard.shape, 0)] + [
            (half, *half.shape, 0) for half in (got, swap(got, "seq", 1))
        ]

    def put_out(m):
        if not straight and not results:
            attend_pairs()
        blocks = [block.result if isinstance(block, Ride) else block for block in results[m]]
        partial, attended[m], qkv_grad[m], total = outputs(
            line, w, m, rows, activated, down, dense, blocks
        )
        totals["qkv"] = totals["qkv"] + total
        branch[m] = lax.psum_scatter(partial, "tensor", scatter_dimension=1, tiled=True)

    def go_back(m):
        part, sums = backs(line, w, rows, m, 1, qkv_grad[m], qkv, x, vectors[0:1], part_two)
        totals["one"] = totals["one"] + sums
        back_cols[m] = lax.psum_scatter(part, "tensor", scatter_dimension=1, tiled=True)

    def finish_out(first, count):
        held["output"] = finish(
            line,
            w,
            first // count,
            held["output"],
            states,
            [branch[m] for m in range(first, first + count)],
            bias,
            out_shape,
            BF16,
        )

    def finish_back(first, count):
        held["input_grad"] = finish(
            line,
            w,
            first // count,
            held["input_grad"],
            out_grad,
            [back_cols[m] for m in range(first, first + count)],
            None,
            out_shape,
            F32,
        )

    def spread(vector, axis):
        size = -(-vector.size // 1024) * 1024
        vector = jnp.pad(vector, (0, size - vector.size)).reshape(8, size // 8)
        return [vector] + [line.ride(vector, axis, k) for k in range(1, lax.axis_size(axis))]

    def summed(parts, size):
        parts = landed(parts)
        while len(parts) > 1:
            parts = [one + two for one, two in zip(parts[::2], parts[1::2])]
        return parts[0].reshape(-1)[:size]

    grads, terms = {}, {
        "down": (False, cot, None),
        "up": (True, two, None),
        "dense": (False, cot, None),
        "qkv": (True, one, None),
    }
    steps = {}

    found, rides = {}, {}

    def send(name, swept):
        at_left, side, _ = terms[name]
        terms[name] = (at_left, side, swept)
        at = SEND if at_left else SEND_AT
        sent = weight_grad(line, w, at, at_left, side, swept)
        found[name] = sent.reshape(-1, sent.shape[2])

    def to_sibling(name):
        rides[name] = line.ride(found[name], "seq", 1)

    def keep(name):
        at_left, side, swept = terms[name]
        at = KEEP if at_left else KEEP_AT
        added = rides[name].result
        added = added.reshape(2, added.shape[0] // 2, added.shape[1])
        found[name] = weight_grad(line, w, at, at_left, side, swept, added)
        rides[name] = []

    def parts(name, count):
        height = found[name].shape[-2]
        size = height // PIECES[name]
        first = sum(ride.rows for ride in rides[name])
        return [(first + i * size, size) for i in range(count)]

    def over_y(name, count):
        for first, size in parts(name, count):
            rides[name].append(line.ride(found[name], "dp", 1, first, size, lead=1))

    def over_x(name, count):
        for first, size in parts(name, count):
            rides[name].append(line.ride(found[name], "seq", steps[name], first, size))

    def all_over_y(name):
        rides[name] = [swap(found[name][1], "dp", 1)]

    def all_over_x(name):
        rides[name] = [swap(found[name], "seq", steps[name])]

    def rest_over_x(name):
        for first, size in parts(name, PIECES[name] - len(rides[name])):
            rides[name].append(swap(found[name][first : first + size], "seq", steps[name]))

    def landed(parts):
        return [part.result if isinstance(part, Ride) else part for part in parts]

    def add_up(name):
        found[name] = add(line, w, found[name], landed(rides[name]))
        rides[name] = []
        steps[name] = 2
        while 2 * steps[name] < n:
            found[name] = add(
                line, w, found[name], [swap(found[name], "seq", steps[name])]
            )
            steps[name] *= 2
            rides[name] = []

    def mine_done(name):
        held[name], found[name] = first_half(
            line, w, terms[name][0], found[name], landed(rides[name])
        )

    def sibling_swap(name):
        rides[name] = swap(found[name], "seq", 1)

    def all_done(name):
        ride = rides[name]
        other = ride.result if isinstance(ride, Ride) else ride
        grads[name] = second_half(line, w, terms[name][0], held[name], other)

    def all_terms():
        one_sums, qkv_total = totals["one"], totals["qkv"]
        sums = jnp.concatenate([one_sums, two_sums], 0).reshape(4, 8, features).sum(1)
        norm_own, norm_oth = sums[:, : 2 * half], sums[:, 2 * half :]
        norm_oth = jnp.where(
            core == 1,
            jnp.concatenate([norm_oth[:, half:], norm_oth[:, :half]], 1),
            norm_oth,
        )
        norm_terms = jnp.where(
            d == 1,
            jnp.concatenate([norm_oth, norm_own], 1),
            jnp.concatenate([norm_own, norm_oth], 1),
        ).reshape(-1)
        rest = jnp.concatenate([qkv_total.sum(0), up_total.sum(0), cot_total.sum(0)])
        return norm_terms, rest

    project(0)
    bring(0, 1, 2, 3)
    project(1)
    bring(1, 1, 2)
    attend(0)
    up = both_cores(up_weight, up_got, True)
    bring(1, 3)
    give(0, 1, 2, 3)
    activated, slope = feed_up(line, w, rows, two, up, up_shift)
    down = both_cores(down_weight, down_got, False)
    bring(2, 1, 2)
    put_out(0)
    bring(2, 3)
    attend(1)
    give(1, 1, 2)
    send("down", [activated])
    give(1, 3)
    bring(3, 1, 2)
    to_sibling("down")
    pre_grad, up_total = pre_grads(line, w, rows, cot, down, slope)
    bring(3, 3)
    put_out(1)
    attend(2)
    give(2, 1, 2)
    keep("down")
    give(2, 3)
    over_y("down", 1)
    attend(3)
    give(3, 1, 2)
    over_y("down", 1)
    put_out(2)
    give(3, 3)
    over_y("down", 1)
    send("up", [pre_grad])
    over_y("down", 1)
    to_sibling("up")
    put_out(3)
    add_up("down")
    over_x("down", 1)
    keep("up")
    over_x("down", 3)
    over_y("up", 3)
    part_two, two_sums = backs(line, w, rows, 0, micros, pre_grad, up, x, vectors[2:3])
    over_y("up", 1)
    go_back(0)
    add_up("up")
    heads_out = [attended[m] for m in range(micros)]
    heads_grad = [qkv_grad[m] for m in range(micros)]
    over_x("up", 1)
    send("qkv", heads_grad)
    over_x("up", 1)
    to_sibling("qkv")
    send("dense", heads_out)
    over_x("up", 1)
    to_sibling("dense")
    go_back(1)
    over_x("up", 1)
    keep("qkv")
    over_y("qkv", 1)
    go_back(2)
    mine_done("down")
    sibling_swap("down")
    finish_out(0, micros)
    over_y("qkv", 1)
    keep("dense")
    add_up("qkv")
    over_x("qkv", 1)
    over_y("dense", 1)
    go_back(3)
    norm_terms, rest = all_terms()
    size = norm_terms.size
    spreads = spread(norm_terms, "tensor")
    add_up("dense")
    norm_terms = summed(spreads, size)
    vector = jnp.concatenate([norm_terms, rest])
    size = vector.size
    spreads = spread(vector, "seq")
    one_sums = gate(line, w, totals["one"])
    vector = summed(spreads, size)
    found["qkv"] = gate(line, w, found["qkv"])
    rest_over_x("qkv")
    mine_done("up")
    sibling_swap("up")
    all_done("down")
    mine_done("qkv")
    sibling_swap("qkv")
    rest_over_x("dense")
    spreads = spread(vector, "dp")
    one_sums = gate(line, w, one_sums)
    vector = summed(spreads, size)
    all_done("up")
    mine_done("dense")
    sibling_swap("dense")
    finish_back(0, micros - 1)
    all_done("qkv")
    all_done("dense")
    finish_back(micros - 1, 1)
    norm_terms = vector[: 4 * features].reshape(4, features)
    rest = vector[4 * features :]
    count = columns // 2
    norm_mine = lax.dynamic_slice_in_dim(norm_terms, first + d * count, count, 1)
    vector_grads = []
    place = 0
    for size in (3 * HD * heads, up_total.shape[1], features):
        vector_grads.append(lax.dynamic_slice_in_dim(rest, place + d * (size // 2), size // 2, 0))
        place += size

    return (
        held["output"],
        held["input_grad"],
        norm_mine[0],
        norm_mine[1],
        norm_mine[2],
        norm_mine[3],
        grads["qkv"],
        vector_grads[0],
        grads["dense"],
        vector_grads[2],
        grads["up"],
        vector_grads[1],
        grads["down"],
        vector_grads[2],
    )


def solution(mesh):
    placed = (
        P("dp", "seq", None),
        P("dp"),
        P("dp"),
        P("dp"),
        P("dp"),
        P("dp", "tensor"),
        P(("tensor", "dp")),
        P("tensor", "dp"),
        P("dp"),
        P("dp", "tensor"),
        P(("tensor", "dp")),
        P("tensor", "dp"),
        P("dp"),
        P("dp", "seq", None),
    )
    return jax.shard_map(
        on_device,
        mesh=mesh,
        in_specs=placed,
        out_specs=(
            P("dp", "seq", "tensor"),
            P("dp", "seq", "tensor"),
            P(("tensor", "dp")),
            P(("tensor", "dp")),
            P(("tensor", "dp")),
            P(("tensor", "dp")),
            P("dp", "tensor"),
            P(("tensor", "dp")),
            P("tensor", "dp"),
            P("dp"),
            P("dp", "tensor"),
            P(("tensor", "dp")),
            P("tensor", "dp"),
            P("dp"),
        ),
        check_vma=False,
    )
```
